512 devices in a mesh: dp: 32 (over z, y_hi), seq: 16 (over y_lo, x, core).
Axes of the slice: x: 4, y: 4 (y_hi: 2, y_lo: 2; y = y_hi * 2 + y_lo), z: 16, core: 2. Of those that a mesh axis runs over, the one named last changes fastest.
Arguments:
- inputs: bfloat16 [32, 2048, 4096], P('dp', 'seq'), may hold values from -6 to 6
- raw_step: bfloat16 [32, 2048, 64], P('dp', 'seq'), may hold values from -5 to 5
- write_keys: bfloat16 [32, 2048, 128], P('dp', 'seq'), may hold values from -0.5 to 0.5
- read_keys: bfloat16 [32, 2048, 128], P('dp', 'seq'), may hold values from -0.5 to 0.5
- grad_out: bfloat16 [32, 2048, 4096], P('dp', 'seq'), may hold values from -6 to 6
- decay_log: float32 [64], P('seq'), as said below
- skip_gain: float32 [64], P('seq'), may hold values from 0.5 to 1.5
- step_bias: float32 [64], P('seq'), may hold values from -1 to 1
Outputs:
- grad_x: bfloat16 [32, 2048, 4096], P('dp', 'seq')
- grad_step: bfloat16 [32, 2048, 64], P('dp', 'seq')
- grad_write: bfloat16 [32, 2048, 128], P('dp', 'seq')
- grad_read: bfloat16 [32, 2048, 128], P('dp', 'seq')
- grad_params: float32 [3, 64], P(None, 'seq')
The draws below stay inside these ranges and needn't reach their ends.
Inputs may be any that keep to these rules, and one draw needn't show every extreme that they name: exp(decay_log) lies between 0.2 / 2048 and 1 / 20.
All inputs are finite; a program needn't handle non-finite values.
Results may differ from the reference program's by a relative error of at most 0.002.
Values may be sent and summed in bfloat16 or wider, within the bound.
No kernel may reach another device: no remote copies, remote signals or barrier semaphores. Data moves between devices by JAX's collectives and lax.ppermute only.
A program may use at most 128 MiB of HBM per device.

```python
import jax
import jax.numpy as jnp
from jax import lax

HEADS = 64
HDIM = 64
NSTATE = 128
SPAN = 256
SEQ = 2048
REPL = 32
HEAD_DEV = 4
N_SEQ = 16


def draw_decay_log(key, part):
    key = jax.random.fold_in(key, 11)
    pick_key, fast_key, slow_key = jax.random.split(key, 3)
    slow_share = 0.5
    slow_heads = jax.random.uniform(pick_key, (HEADS,), jnp.float32) < slow_share
    fast_rate = jnp.exp(jax.random.uniform(fast_key, (HEADS,), jnp.float32, jnp.log(1.0 / 40.0), jnp.log(1.0 / 20.0)))
    slow_rate = jnp.exp(jax.random.uniform(slow_key, (HEADS,), jnp.float32, jnp.log(0.2 / SEQ), jnp.log(1.5 / SEQ)))
    return jnp.log(jnp.where(slow_heads, slow_rate, fast_rate)).astype(jnp.float32)


def levels(key, dims, cuts, low, high):
    loudness = 1.0
    for position, parts in cuts:
        steps = jax.random.uniform(jax.random.fold_in(jax.random.fold_in(key, 6), position), (parts,), jnp.float32, low / len(cuts), high / len(cuts))
        loudness = loudness * jnp.repeat(jnp.exp(steps), dims[position] // parts).reshape((-1,) + (1,) * (len(dims) - 1 - position))
    return loudness


def centred(own_key, dims, width, bound, shards=(), kind=jnp.bfloat16):
    result = width * jax.random.normal(own_key, dims, jnp.float32)
    if shards:
        result = result * levels(own_key, dims, shards, -0.22, 0.18)
    return jnp.clip(result, -bound, bound).astype(kind)


def setup_inputs(seed: int = 0) -> dict:
    key_of = jax.random.split(jax.random.key(seed), 9)
    return {
        "inputs": centred(key_of[0], (REPL, SEQ, HEADS * HDIM), 1.0, 6.0, ((0, 32), (1, 16))),
        "raw_step": centred(key_of[1], (REPL, SEQ, HEADS), 1.0, 5.0, ((0, 32), (1, 16))),
        "write_keys": centred(key_of[2], (REPL, SEQ, NSTATE), NSTATE ** -0.5, 0.5, ((0, 32), (1, 16))),
        "read_keys": centred(key_of[3], (REPL, SEQ, NSTATE), NSTATE ** -0.5, 0.5, ((0, 32), (1, 16))),
        "grad_out": centred(key_of[4], (REPL, SEQ, HEADS * HDIM), 1.0, 6.0, ((0, 32), (1, 16))),
        "decay_log": draw_decay_log(jax.random.fold_in(key_of[8], 71), 0),
        "skip_gain": jnp.clip(0.5 + 1.0 * jax.random.uniform(key_of[6], (HEADS,), jnp.float32) ** levels(key_of[6], (HEADS,), ((0, 16),), -0.2, 0.2), 0.5, 1.5),
        "step_bias": jnp.clip(jax.random.uniform(key_of[7], (HEADS,), jnp.float32, -1.0, 1.0) * levels(key_of[7], (HEADS,), ((0, 16),), -0.4, 0.0), -1.0, 1.0),
    }


highest = lax.Precision.HIGHEST

def span_inner(pieces):
    block_scaled, block_decay, block_write, block_read = pieces
    scores = jnp.dot(block_read, block_write.T, precision=highest, preferred_element_type=jnp.float32)
    extent = block_decay.shape[0]
    causal = lax.broadcasted_iota(jnp.int32, (extent, extent), 0) >= lax.broadcasted_iota(jnp.int32, (extent, extent), 1)
    by_head = block_decay.T
    spread = by_head[:, :, None] - by_head[:, None, :]
    weights = jnp.exp(jnp.where(causal[None], spread, -jnp.inf)) * scores[None]
    within = jnp.einsum('hqs,shp->qhp', weights, block_scaled, precision=highest)
    to_end = jnp.exp(block_decay[-1:] - block_decay)
    end_state = jnp.einsum('sn,shp->hnp', block_write, block_scaled * to_end[:, :, None], precision=highest)
    return (within, end_state)

def entering_sequential(end_states, totals):

    def advance(running, pieces):
        span_state, span_total = pieces
        return (jnp.exp(span_total)[:, None, None] * running + span_state, running)
    initial = jnp.zeros(end_states.shape[1:], end_states.dtype)
    _, entering = lax.scan(advance, initial, (end_states, totals))
    return entering

def mixer_forward(inputs, raw_step, write_keys, read_keys, decay_log, skip_gain, step_bias):
    length, head_count, head_width = inputs.shape
    blocks = length // SPAN
    step_size = jax.nn.softplus(raw_step + step_bias[None, :])
    log_decay = -jnp.exp(decay_log)[None, :] * step_size
    scaled = (inputs * step_size[:, :, None]).reshape(blocks, SPAN, head_count, head_width)
    cumulative = jnp.cumsum(log_decay.reshape(blocks, SPAN, head_count), axis=1)
    write_blocks = write_keys.reshape(blocks, SPAN, -1)
    read_blocks = read_keys.reshape(blocks, SPAN, -1)
    within, end_states = lax.map(jax.checkpoint(span_inner), (scaled, cumulative, write_blocks, read_blocks))
    entering = entering_sequential(end_states, cumulative[:, -1, :])
    carried = jnp.einsum('kqn,khnp->kqhp', read_blocks, entering, precision=highest) * jnp.exp(cumulative)[:, :, :, None]
    return (within + carried).reshape(length, head_count, head_width) + skip_gain[None, :, None] * inputs

def replica_grads(pieces, decay_log, skip_gain, step_bias):
    inputs, raw_step, write_keys, read_keys, grad_out = pieces
    write_full = write_keys.astype(jnp.float32)
    read_full = read_keys.astype(jnp.float32)
    group_inputs = inputs.reshape(SEQ, N_SEQ, HEAD_DEV * HDIM).transpose(1, 0, 2)
    group_grad = grad_out.reshape(SEQ, N_SEQ, HEAD_DEV * HDIM).transpose(1, 0, 2)
    group_step = raw_step.reshape(SEQ, N_SEQ, HEAD_DEV).transpose(1, 0, 2)

    def one_group(group):
        part_inputs, part_grad, part_step, part_decay, part_skip, part_bias = group
        _, pullback = jax.vjp(mixer_forward, part_inputs.astype(jnp.float32).reshape(SEQ, HEAD_DEV, HDIM), part_step.astype(jnp.float32), write_full, read_full, part_decay, part_skip, part_bias)
        grads = pullback(part_grad.astype(jnp.float32).reshape(SEQ, HEAD_DEV, HDIM))
        return grads
    outs = lax.map(one_group, (group_inputs, group_grad, group_step, decay_log.reshape(N_SEQ, HEAD_DEV), skip_gain.reshape(N_SEQ, HEAD_DEV), step_bias.reshape(N_SEQ, HEAD_DEV)))
    grad_inputs = outs[0].transpose(1, 0, 2, 3).reshape(SEQ, HEADS * HDIM)
    grad_raw = outs[1].transpose(1, 0, 2).reshape(SEQ, HEADS)
    grad_write = lax.optimization_barrier(jnp.sum(outs[2], axis=0))
    grad_read = lax.optimization_barrier(jnp.sum(outs[3], axis=0))
    return (grad_inputs, grad_raw, grad_write, grad_read, outs[4].reshape(HEADS), outs[5].reshape(HEADS), outs[6].reshape(HEADS))

def reference(inputs, raw_step, write_keys, read_keys, grad_out, decay_log, skip_gain, step_bias):

    def replica(pieces):
        grads = replica_grads(pieces, decay_log, skip_gain, step_bias)
        return (grads[0].astype(jnp.bfloat16), grads[1].astype(jnp.bfloat16), grads[2].astype(jnp.bfloat16), grads[3].astype(jnp.bfloat16), jnp.stack([grads[4], grads[5], grads[6]]))
    grad_x, grad_step, grad_write, grad_read, per_replica = lax.map(replica, (inputs, raw_step, write_keys, read_keys, grad_out))
    grad_params = lax.optimization_barrier(jnp.sum(per_replica, axis=0)) / REPL
    return (grad_x, grad_step, grad_write, grad_read, grad_params)
```

```python
import jax
import jax.numpy as jnp
from jax import lax
from jax.experimental import pallas as pl
from jax.experimental.pallas import tpu as pltpu
from jax.sharding import PartitionSpec as P

CHUNK = 128
LANES = 128
HDIM = 64
NSTATE = 128
ROWS = 8
MIB = 1 << 20

f32 = jnp.float32
bf16 = jnp.bfloat16


def mm(a, b):
    return jnp.dot(a, b, preferred_element_type=f32)


def mm_nt(a, b):
    return lax.dot_general(a, b, (((1,), (1,)), ((), ())), preferred_element_type=f32)


def mm_tn(a, b):
    return lax.dot_general(a, b, (((0,), (0,)), ((), ())), preferred_element_type=f32)


def split2(v):
    high = v.astype(bf16)
    return high, (v - high.astype(f32)).astype(bf16)


def split3(v):
    high = v.astype(bf16).astype(f32)
    rest = v - high
    mid = rest.astype(bf16).astype(f32)
    return high, mid, rest - mid


def iota(shape, axis):
    return lax.broadcasted_iota(jnp.int32, shape, axis)


def one_hot(cond):
    return jnp.where(cond, 1.0, 0.0)


def mm_exact(v, ones):
    parts = mm(jnp.concatenate(split3(v), axis=0).astype(bf16), ones.astype(bf16))
    n = v.shape[0]
    return parts[:n] + parts[n : 2 * n] + parts[2 * n :]


def pack_kernel(heads, x_ref, g_ref, b_ref, c_ref, s_ref, out_ref):
    group = pl.program_id(0)
    width = heads * HDIM
    for i in range(width // LANES):
        lanes = slice(i * LANES, (i + 1) * LANES)
        out_ref[0, i * CHUNK : (i + 1) * CHUNK] = x_ref[:, lanes]
        out_ref[0, width + i * CHUNK : width + (i + 1) * CHUNK] = g_ref[:, lanes]
    out_ref[0, 2 * width : 2 * width + CHUNK] = b_ref[...]
    out_ref[0, 2 * width + CHUNK : 2 * width + 2 * CHUNK] = c_ref[...]
    shape = (16, s_ref.shape[1])
    pick = one_hot((iota(shape, 1) == iota(shape, 0) + group * heads) & (iota(shape, 0) < heads))
    out_ref[0, 2 * width + 2 * CHUNK :] = mm_nt(pick.astype(bf16), s_ref[...]).astype(bf16)


def pack(x, g, b, c, s, groups):
    heads = s.shape[1] // groups
    width = heads * HDIM
    rows = 2 * width + 2 * CHUNK + 16
    whole = lambda a: pl.BlockSpec(a.shape, lambda j: (0, 0))
    cut = pl.BlockSpec((CHUNK, width), lambda j: (0, j))
    return pl.pallas_call(
        lambda *refs: pack_kernel(heads, *refs),
        grid=(groups,),
        in_specs=[cut, cut, whole(b), whole(c), whole(s)],
        out_specs=pl.BlockSpec((1, rows, LANES), lambda j: (j, 0, 0)),
        out_shape=jax.ShapeDtypeStruct((groups, rows, LANES), bf16),
        name="pack",
    )(x, g, b, c, s)


def scan_kernel(heads, chunks, in_ref, par_ref, out_ref, pout_ref,
                alpha_ref, gamma_ref, total_ref, gh_ref, gl_ref, xh_ref, xl_ref,
                hh_ref, hl_ref, dloc_ref, r_ref, c_ref, skip_ref):
    width = heads * HDIM
    blocks = width // LANES
    at_b, at_c, at_s = 2 * width, 2 * width + CHUNK, 2 * width + 2 * CHUNK
    flat = (chunks * ROWS, LANES)
    cube = (chunks, ROWS, LANES)

    raw = jnp.concatenate([in_ref[k, at_s : at_s + 16].astype(f32)[None, :ROWS] for k in range(chunks)], axis=0)
    rate = -jnp.exp(par_ref[0])
    z = raw + par_ref[2][None]
    step = jnp.maximum(z, 0.0) + jnp.log1p(jnp.exp(-jnp.abs(z)))
    slope = jnp.exp(z - step)
    decay = rate[None] * step
    square = (LANES, LANES)
    upto = one_hot(iota(square, 0) <= iota(square, 1))
    since = one_hot(iota(square, 0) >= iota(square, 1))
    level = mm_exact(decay.reshape(flat), upto)
    total = jnp.exp(jnp.broadcast_to(level[:, LANES - 1 :], flat))
    alpha = jnp.exp(level)
    gamma = jnp.exp(-level) * step.reshape(flat)
    nothing = jnp.zeros(cube, f32)
    for ref, v in ((alpha_ref, alpha), (gamma_ref, gamma)):
        parts = [p.reshape(cube) for p in split3(v)]
        ref[...] = jnp.concatenate(parts + [nothing], axis=1).astype(bf16)
    total_ref[...] = total.reshape(cube)

    of_head = lambda rows: iota((rows, width), 1) // HDIM == iota((rows, width), 0) % ROWS
    spread = one_hot(of_head(ROWS))
    spread4 = one_hot(of_head(4 * ROWS)).astype(bf16)
    gather = one_hot((iota((16, width), 1) // HDIM) == iota((16, width), 0)).astype(bf16)

    def to_lanes(tile):
        return jnp.sum(jnp.concatenate([tile] * blocks, axis=1) * spread, axis=0, keepdims=True)

    def wide(k, start):
        return jnp.concatenate(
            [in_ref[k, start + i * CHUNK : start + (i + 1) * CHUNK] for i in range(blocks)], axis=1
        )

    skip_ref[...] = jnp.zeros_like(skip_ref)

    def forward(k, state):
        x = wide(k, 0).astype(f32)
        g = wide(k, width).astype(f32)
        gt_high, gt_low = split2(mm_tn(alpha_ref[k], spread4) * g)
        xt_high, xt_low = split2(mm_tn(gamma_ref[k], spread4) * x)
        gh_ref[k], gl_ref[k], xh_ref[k], xl_ref[k] = gt_high, gt_low, xt_high, xt_low
        skip_ref[...] += jnp.sum((x * g).reshape(CHUNK // ROWS, ROWS, width), axis=0)
        hh_ref[k], hl_ref[k] = split2(state)
        keys_in, keys_out = in_ref[k, at_b : at_b + CHUNK], in_ref[k, at_c : at_c + CHUNK]
        dloc_ref[k] = mm_tn(keys_out, gt_high) + mm_tn(keys_out, gt_low)
        return to_lanes(total_ref[k]) * (state + mm_tn(keys_in, xt_high) + mm_tn(keys_in, xt_low))

    lax.fori_loop(0, chunks, forward, jnp.zeros((NSTATE, width), f32))

    skip_wide = to_lanes(par_ref[1])
    causal = iota(square, 0) >= iota(square, 1)

    def backward(i, dstate):
        k = chunks - 1 - i
        through = to_lanes(total_ref[k]) * dstate
        dh, dl = split2(through)
        hh, hl = hh_ref[k], hl_ref[k]
        gh, gl, xh, xl = gh_ref[k], gl_ref[k], xh_ref[k], xl_ref[k]
        keys_in, keys_out = in_ref[k, at_b : at_b + CHUNK], in_ref[k, at_c : at_c + CHUNK]

        sh, sl = split2(jnp.where(causal, mm_nt(keys_out, keys_in), 0.0))
        th, tl = split2(jnp.where(causal.T, mm_nt(keys_in, keys_out), 0.0))
        along = lambda *parts: jnp.concatenate(parts, axis=1)
        under = lambda *parts: jnp.concatenate(parts, axis=0)
        y = mm(along(sh, keys_out), under(xh, hh)) + mm(along(sl, keys_out), under(xh, hl)) + mm(sh, xl)
        dx = mm(along(th, keys_in), under(gh, dh)) + mm(along(tl, keys_in), under(gh, dl)) + mm(th, gl)

        ds = mm_nt(gh, xh) + mm_nt(gh, xl) + mm_nt(gl, xh)
        ds = jnp.where(causal, ds, 0.0)
        ph, plow = split2(ds)
        qh, qlow = split2(ds.T)
        d_out = mm(along(ph, plow), under(keys_in, keys_in)) + mm_nt(gh, hh) + mm_nt(gh, hl) + mm_nt(gl, hh)
        d_in = mm(along(qh, qlow), under(keys_out, keys_out)) + mm_nt(xh, dh) + mm_nt(xh, dl) + mm_nt(xl, dh)

        gt = gh.astype(f32) + gl.astype(f32)
        xt = xh.astype(f32) + xl.astype(f32)

        def per_head(v):
            high, low = split2(v)
            return (mm_nt(gather, high) + mm_nt(gather, low))[:ROWS]

        r_ref[k] = per_head(gt * y)
        c_ref[k] = per_head(xt * dx)

        grad_x = mm_tn(gamma_ref[k], spread4) * dx + skip_wide * wide(k, width).astype(f32)
        grad_x = grad_x.astype(bf16)
        for j in range(blocks):
            out_ref[k, j * CHUNK : (j + 1) * CHUNK] = grad_x[:, j * LANES : (j + 1) * LANES]
        for j, part in enumerate(split2(d_in) + split2(d_out)):
            out_ref[k, width + j * CHUNK : width + (j + 1) * CHUNK] = part
        return dloc_ref[k] + through

    lax.fori_loop(0, chunks, backward, jnp.zeros((NSTATE, width), f32))

    col = c_ref[...]
    suffix = mm_exact((r_ref[...] - col).reshape(flat), since).reshape(cube)
    sums = jnp.broadcast_to(suffix[:, :, :1], cube)
    later = jnp.zeros((ROWS, LANES), f32)
    carried = [None] * chunks
    for k in reversed(range(chunks)):
        carried[k] = later[None]
        later = later + sums[k]
    d_decay = suffix + jnp.concatenate(carried, axis=0)
    d_raw = slope * (col / step + rate[None] * d_decay)
    pad = jnp.zeros((ROWS, LANES), f32)
    for k in range(chunks):
        out_ref[k, width + 4 * CHUNK :] = jnp.concatenate([d_raw[k], pad], axis=0).astype(bf16)

    d_skip = jnp.sum(spread * jnp.sum(skip_ref[...], axis=0, keepdims=True), axis=1, keepdims=True)
    tile = (ROWS, LANES)
    result = jnp.zeros(tile, f32)
    per = (
        jnp.sum(jnp.sum(d_decay * decay, axis=0), axis=1, keepdims=True),
        d_skip,
        jnp.sum(jnp.sum(d_raw, axis=0), axis=1, keepdims=True),
    )
    for i, v in enumerate(per):
        row = jnp.sum(jnp.where(iota(tile, 0) == iota(tile, 1), jnp.broadcast_to(v, tile), 0.0), axis=0, keepdims=True)
        result = jnp.where(iota(tile, 0) == i, jnp.broadcast_to(row, tile), result)
    pout_ref[...] = result


def scan_grads(received, params, heads):
    chunks = received.shape[0]
    width = heads * HDIM
    rows = width + 4 * CHUNK + 16
    vmem = pl.BlockSpec(memory_space=pltpu.VMEM)
    wide = lambda dtype: pltpu.VMEM((chunks, CHUNK, width), dtype)
    small = lambda dtype, n: pltpu.VMEM((chunks, n, LANES), dtype)
    return pl.pallas_call(
        lambda *refs: scan_kernel(heads, chunks, *refs),
        in_specs=[vmem, vmem],
        out_specs=[vmem, vmem],
        out_shape=[
            jax.ShapeDtypeStruct((chunks, rows, LANES), bf16),
            jax.ShapeDtypeStruct((ROWS, LANES), f32),
        ],
        scratch_shapes=[
            small(bf16, 4 * ROWS), small(bf16, 4 * ROWS), small(f32, ROWS),
            wide(bf16), wide(bf16), wide(bf16), wide(bf16),
            wide(bf16), wide(bf16), wide(f32),
            small(f32, ROWS), small(f32, ROWS), pltpu.VMEM((ROWS, width), f32),
        ],
        compiler_params=pltpu.CompilerParams(vmem_limit_bytes=40 * MIB),
        name="scan_grads",
    )(received, params)


def unpack_kernel(heads, in_ref, x_ref, s_ref, b_ref, c_ref, b_sum, c_sum, s_sum):
    group = pl.program_id(0)
    width = heads * HDIM

    @pl.when(group == 0)
    def _():
        for ref in (b_sum, c_sum, s_sum):
            ref[...] = jnp.zeros_like(ref)

    for i in range(width // LANES):
        x_ref[:, i * LANES : (i + 1) * LANES] = in_ref[0, i * CHUNK : (i + 1) * CHUNK]
    part = lambda j: in_ref[0, width + j * CHUNK : width + (j + 1) * CHUNK].astype(f32)
    b_sum[...] += part(0) + part(1)
    c_sum[...] += part(2) + part(3)
    shape = (16, s_sum.shape[1])
    pick = one_hot((iota(shape, 1) == iota(shape, 0) + group * heads) & (iota(shape, 0) < heads))
    s_sum[...] += mm_tn(in_ref[0, width + 4 * CHUNK :], pick.astype(bf16))

    @pl.when(group == pl.num_programs(0) - 1)
    def _():
        b_ref[...] = b_sum[...].astype(bf16)
        c_ref[...] = c_sum[...].astype(bf16)
        s_ref[...] = s_sum[...].astype(bf16)


def unpack(received, heads):
    groups, rows, _ = received.shape
    width = heads * HDIM
    whole = lambda *shape: pl.BlockSpec(shape, lambda j: (0, 0))
    shapes = [(CHUNK, groups * width), (CHUNK, groups * heads), (CHUNK, NSTATE), (CHUNK, NSTATE)]
    return pl.pallas_call(
        lambda *refs: unpack_kernel(heads, *refs),
        grid=(groups,),
        in_specs=[pl.BlockSpec((1, rows, LANES), lambda j: (j, 0, 0))],
        out_specs=[pl.BlockSpec((CHUNK, width), lambda j: (0, j))] + [whole(*s) for s in shapes[1:]],
        out_shape=[jax.ShapeDtypeStruct(s, bf16) for s in shapes],
        scratch_shapes=[pltpu.VMEM(shapes[2], f32), pltpu.VMEM(shapes[2], f32), pltpu.VMEM(shapes[1], f32)],
        name="unpack",
    )(received)


def exchange(v):
    return lax.all_to_all(v, "seq", split_axis=0, concat_axis=0, tiled=True)


def replica_sum(v):
    replicas = lax.axis_size("dp")
    if replicas == 1:
        return v
    v = v + lax.ppermute(v, "dp", [(i, i ^ 1) for i in range(replicas)])
    if replicas == 2:
        return v
    lines = [[2 * i + half for i in range(replicas // 2)] for half in range(2)]
    return lax.psum(v, "dp", axis_index_groups=lines)


def shards(inputs, raw_step, write_keys, read_keys, grad_out, decay_log, skip_gain, step_bias):
    groups = lax.axis_size("seq")
    heads = decay_log.shape[0]
    send = pack(inputs[0], grad_out[0], write_keys[0], read_keys[0], raw_step[0], groups)
    params = jnp.stack([decay_log, skip_gain, step_bias])
    params = jnp.concatenate([params] * (ROWS // heads), axis=1)
    params = jnp.broadcast_to(params[:, :, None], (3, ROWS, LANES))
    back, per_head = scan_grads(exchange(send), params, heads)
    grad_x, grad_step, grad_write, grad_read = unpack(exchange(back), heads)
    totals = replica_sum(per_head)[:3, :heads] / lax.axis_size("dp")
    return grad_x[None], grad_step[None], grad_write[None], grad_read[None], totals


def solution(mesh):
    rows = P("dp", "seq", None)
    heads = P("seq")
    return jax.shard_map(
        shards,
        mesh=mesh,
        in_specs=(rows,) * 5 + (heads,) * 3,
        out_specs=(rows,) * 4 + (P(None, "seq"),),
        check_vma=False,
    )
```

```python
import jax
import jax.numpy as jnp
from jax import lax
from jax.experimental import pallas as pl
from jax.experimental.pallas import tpu as pltpu
from jax.sharding import PartitionSpec as P

CHUNK = 128
LANES = 128
HDIM = 64
NSTATE = 128
ROWS = 8
MIB = 1 << 20
PACK_STEPS = 2
UNPACK_STEPS = 2
PER_TILE = LANES // (2 * ROWS)
UNROLL = 4
SCAN_VMEM = 44
UNPACK_VMEM = 24

f32 = jnp.float32
bf16 = jnp.bfloat16


def mm(a, b):
    return jnp.dot(a, b, preferred_element_type=f32)


def mm_nt(a, b):
    return lax.dot_general(a, b, (((1,), (1,)), ((), ())), preferred_element_type=f32)


def mm_tn(a, b):
    return lax.dot_general(a, b, (((0,), (0,)), ((), ())), preferred_element_type=f32)


def split2(v):
    high = v.astype(bf16)
    return high, (v - high.astype(f32)).astype(bf16)


def split3(v):
    high = v.astype(bf16).astype(f32)
    rest = v - high
    mid = rest.astype(bf16).astype(f32)
    return high, mid, rest - mid


def iota(shape, axis):
    return lax.broadcasted_iota(jnp.int32, shape, axis)


def one_hot(cond):
    return jnp.where(cond, 1.0, 0.0)


def mm_exact(v, ones):
    parts = mm(jnp.concatenate(split3(v), axis=0).astype(bf16), ones.astype(bf16))
    n = v.shape[0]
    return parts[:n] + parts[n : 2 * n] + parts[2 * n :]


def pack_kernel(heads, x_ref, g_ref, b_ref, c_ref, s_ref, out_ref):
    width = heads * HDIM
    tall = 2 * width + 2 * CHUNK
    for n in range(out_ref.shape[0]):
        for i in range(width // LANES):
            lanes = slice(n * width + i * LANES, n * width + (i + 1) * LANES)
            out_ref[n, i * CHUNK : (i + 1) * CHUNK] = x_ref[:, lanes]
            out_ref[n, width + i * CHUNK : width + (i + 1) * CHUNK] = g_ref[:, lanes]
        out_ref[n, 2 * width : 2 * width + CHUNK] = b_ref[...]
        out_ref[n, 2 * width + CHUNK : tall] = c_ref[...]
        group = pl.program_id(0) * out_ref.shape[0] + n
        shape = (16, s_ref.shape[0])
        pick = one_hot((iota(shape, 1) == iota(shape, 0) + group * heads) & (iota(shape, 0) < heads))
        out_ref[n, tall:] = mm(pick.astype(bf16), s_ref[...]).astype(bf16)


def pack(x, g, b, c, s, groups):
    heads = s.shape[0] // groups
    width = heads * HDIM
    rows = 2 * width + 2 * CHUNK + 16
    part = groups // PACK_STEPS
    whole = lambda a: pl.BlockSpec(a.shape, lambda j: (0, 0))
    cut = pl.BlockSpec((CHUNK, part * width), lambda j: (0, j))
    return pl.pallas_call(
        lambda *refs: pack_kernel(heads, *refs),
        grid=(PACK_STEPS,),
        in_specs=[cut, cut, whole(b), whole(c), whole(s)],
        out_specs=pl.BlockSpec((part, rows, LANES), lambda j: (j, 0, 0)),
        out_shape=jax.ShapeDtypeStruct((groups, rows, LANES), bf16),
        compiler_params=pltpu.CompilerParams(vmem_limit_bytes=56 * MIB),
        name="pack",
    )(x, g, b, c, s)


def scan_kernel(heads, chunks, in_ref, given_ref, out_hbm, pout_ref,
                out_ref, dstep_ref, par_ref, alpha_ref, gamma_ref, total_ref,
                gh_ref, gl_ref, xh_ref, xl_ref, hh_ref, hl_ref, dloc_ref, wide_ref, pick_ref, r_ref, c_ref, skip_ref,
                step_sem, out_sem):
    width = heads * HDIM
    blocks = width // LANES
    at_b, at_c, at_s = 2 * width, 2 * width + CHUNK, 2 * width + 2 * CHUNK
    flat = (chunks * ROWS, LANES)
    cube = (chunks, ROWS, LANES)
    body = width + 4 * CHUNK

    put_steps = pltpu.make_async_copy(dstep_ref, out_hbm.at[:, body : body + 16], step_sem)
    put = lambda k: pltpu.make_async_copy(out_ref.at[k], out_hbm.at[k, :body], out_sem.at[k])

    tile = (ROWS, LANES)
    for i in range(3):
        row = jnp.broadcast_to(given_ref[i : i + 1], tile)
        mine = jnp.where(iota(tile, 1) == iota(tile, 0), row, 0.0)
        par_ref[i] = jnp.broadcast_to(jnp.sum(mine, axis=1, keepdims=True), tile)

    raw = in_ref[:, at_s : at_s + 16].astype(f32)[:, :ROWS]
    rate = -jnp.exp(par_ref[0])
    z = raw + par_ref[2][None]
    step = jnp.maximum(z, 0.0) + jnp.log1p(jnp.exp(-jnp.abs(z)))
    slope = jnp.exp(z - step)
    decay = rate[None] * step
    square = (LANES, LANES)
    upto = one_hot(iota(square, 0) <= iota(square, 1))
    since = one_hot(iota(square, 0) >= iota(square, 1))
    level = mm_exact(decay.reshape(flat), upto)
    total = jnp.exp(jnp.broadcast_to(level[:, LANES - 1 :], flat))
    alpha = jnp.exp(level)
    gamma = jnp.exp(-level) * step.reshape(flat)
    for ref, v in ((alpha_ref, alpha), (gamma_ref, gamma)):
        high = v.astype(bf16).astype(f32)
        parts = jnp.concatenate([high.reshape(cube), (v - high).reshape(cube)], axis=1)
        parts = parts.reshape(chunks // PER_TILE, LANES, LANES)
        for i in range(chunks // PER_TILE):
            ref[i] = parts[i].T.astype(bf16)
    total_ref[...] = total.reshape(cube)

    of_head = lambda rows: iota((rows, width), 1) // HDIM == iota((rows, width), 0) % ROWS
    spread = one_hot(of_head(ROWS))
    in_tile = (LANES, width)
    at_head = iota(in_tile, 1) // HDIM == iota(in_tile, 0) % ROWS
    eye = one_hot(iota(square, 0) == iota(square, 1)).astype(bf16)
    gather = one_hot((iota((16, width), 1) // HDIM) == iota((16, width), 0)).astype(bf16)

    def to_lanes(tile):
        return jnp.sum(jnp.concatenate([tile] * blocks, axis=1) * spread, axis=0, keepdims=True)

    for i in range(PER_TILE):
        pick_ref[i] = one_hot(at_head & (iota(in_tile, 0) // (2 * ROWS) == i)).astype(bf16)

    def expand(ref, k):
        return mm(ref[k // PER_TILE], pick_ref[k % PER_TILE])

    def flip(v):
        return mm_nt(eye, v).astype(bf16)

    along = lambda *parts: jnp.concatenate(parts, axis=1)
    under = lambda *parts: jnp.concatenate(parts, axis=0)

    def wide(k, start):
        return jnp.concatenate(
            [in_ref[k, start + i * CHUNK : start + (i + 1) * CHUNK] for i in range(blocks)], axis=1
        )

    skip_ref[...] = jnp.zeros_like(skip_ref)

    def forward(k, state):
        x = wide(k, 0).astype(f32)
        g = wide(k, width).astype(f32)
        gt_high, gt_low = split2(expand(alpha_ref, k) * g)
        wide_ref[k] = expand(gamma_ref, k)
        xt_high, xt_low = split2(wide_ref[k] * x)
        gh_ref[k], gl_ref[k], xh_ref[k], xl_ref[k] = gt_high, gt_low, xt_high, xt_low
        skip_ref[...] += jnp.sum((x * g).reshape(CHUNK // ROWS, ROWS, width), axis=0)
        hh_ref[k], hl_ref[k] = split2(state)
        keys_in, keys_out = in_ref[k, at_b : at_b + CHUNK], in_ref[k, at_c : at_c + CHUNK]
        keys_in, keys_out = flip(keys_in), flip(keys_out)
        dloc_ref[k] = mm(along(keys_out, keys_out), under(gt_high, gt_low))
        return to_lanes(total_ref[k]) * (state + mm(along(keys_in, keys_in), under(xt_high, xt_low)))

    def forwards(i, state):
        for n in range(UNROLL):
            state = forward(i * UNROLL + n, state)
        return state

    nothing = jnp.zeros((NSTATE, width), f32)
    lax.fori_loop(0, chunks // UNROLL, forwards, nothing)

    skip_wide = to_lanes(par_ref[1])
    causal = iota(square, 0) >= iota(square, 1)

    def backward(k, dstate):
        through = to_lanes(total_ref[k]) * dstate
        dh, dl = split2(through)
        hh, hl = hh_ref[k], hl_ref[k]
        gh, gl, xh, xl = gh_ref[k], gl_ref[k], xh_ref[k], xl_ref[k]
        keys_in, keys_out = in_ref[k, at_b : at_b + CHUNK], in_ref[k, at_c : at_c + CHUNK]

        sh, sl = split2(jnp.where(causal, mm_nt(keys_out, keys_in), 0.0))
        th, tl = split2(jnp.where(causal.T, mm_nt(keys_in, keys_out), 0.0))
        xhh, xhl, gdh, gdl = under(xh, hh), under(xl, hl), under(gh, dh), under(gl, dl)
        out_h, in_h = along(sh, keys_out), along(th, keys_in)
        y = mm(out_h, xhh) + mm(out_h, xhl) + mm(sl, xh)
        dx = mm(in_h, gdh) + mm(in_h, gdl) + mm(tl, gh)

        ds = mm_nt(gh, xh) + mm_nt(gh, xl) + mm_nt(gl, xh)
        ds = jnp.where(causal, ds, 0.0)
        ph, plow = split2(ds)
        qh, qlow = split2(ds.T)
        d_out = mm(along(ph, plow), under(keys_in, keys_in)) + mm_nt(gh, hh) + mm_nt(gh, hl) + mm_nt(gl, hh)
        d_in = mm(along(qh, qlow), under(keys_out, keys_out)) + mm_nt(xh, dh) + mm_nt(xh, dl) + mm_nt(xl, dh)

        gt = gh.astype(f32) + gl.astype(f32)
        xt = xh.astype(f32) + xl.astype(f32)

        high, low = split2(under(gt * y, xt * dx))
        sums = mm_nt(gather, high) + mm_nt(gather, low)
        r_ref[k], c_ref[k] = sums[:ROWS, :CHUNK], sums[:ROWS, CHUNK:]

        grad_x = wide_ref[k] * dx + skip_wide * wide(k, width).astype(f32)
        grad_x = grad_x.astype(bf16)
        for j in range(blocks):
            out_ref[k, j * CHUNK : (j + 1) * CHUNK] = grad_x[:, j * LANES : (j + 1) * LANES]
        for j, part in enumerate(split2(d_in) + split2(d_out)):
            out_ref[k, width + j * CHUNK : width + (j + 1) * CHUNK] = part
        return dloc_ref[k] + through

    def backwards(i, dstate):
        top = chunks - 1 - i * UNROLL
        for n in range(UNROLL):
            dstate = backward(top - n, dstate)
        for n in range(UNROLL):
            put(top - n).start()
        return dstate

    lax.fori_loop(0, chunks // UNROLL, backwards, nothing)

    col = c_ref[...]
    suffix = mm_exact((r_ref[...] - col).reshape(flat), since).reshape(cube)
    sums = jnp.broadcast_to(suffix[:, :, :1], cube)
    later = jnp.zeros((ROWS, LANES), f32)
    carried = [None] * chunks
    for k in reversed(range(chunks)):
        carried[k] = later[None]
        later = later + sums[k]
    d_decay = suffix + jnp.concatenate(carried, axis=0)
    d_raw = slope * (col / step + rate[None] * d_decay)
    dstep_ref[...] = jnp.concatenate([d_raw, jnp.zeros(cube, f32)], axis=1).astype(bf16)
    put_steps.start()

    d_skip = jnp.sum(spread * jnp.sum(skip_ref[...], axis=0, keepdims=True), axis=1, keepdims=True)
    result = jnp.zeros(tile, f32)
    per = (
        jnp.sum(jnp.sum(d_decay * decay, axis=0), axis=1, keepdims=True),
        d_skip,
        jnp.sum(jnp.sum(d_raw, axis=0), axis=1, keepdims=True),
    )
    for i, v in enumerate(per):
        row = jnp.sum(jnp.where(iota(tile, 0) == iota(tile, 1), jnp.broadcast_to(v, tile), 0.0), axis=0, keepdims=True)
        result = jnp.where(iota(tile, 0) == i, jnp.broadcast_to(row, tile), result)
    pout_ref[...] = result
    put_steps.wait()
    for k in range(chunks):
        put(k).wait()


def scan_grads(received, params, heads):
    chunks = received.shape[0]
    width = heads * HDIM
    rows = width + 4 * CHUNK + 16
    vmem = pl.BlockSpec(memory_space=pltpu.VMEM)
    wide = lambda dtype: pltpu.VMEM((chunks, CHUNK, width), dtype)
    tiles = pltpu.VMEM((chunks // PER_TILE, LANES, LANES), bf16)
    small = lambda dtype, n: pltpu.VMEM((chunks, n, LANES), dtype)
    return pl.pallas_call(
        lambda *refs: scan_kernel(heads, chunks, *refs),
        in_specs=[vmem, vmem],
        out_specs=[pl.BlockSpec(memory_space=pltpu.HBM), vmem],
        out_shape=[
            jax.ShapeDtypeStruct((chunks, rows, LANES), bf16),
            jax.ShapeDtypeStruct((ROWS, LANES), f32),
        ],
        scratch_shapes=[
            pltpu.VMEM((chunks, rows - 16, LANES), bf16), small(bf16, 16), pltpu.VMEM((3, ROWS, LANES), f32), tiles, tiles, small(f32, ROWS),
            wide(bf16), wide(bf16), wide(bf16), wide(bf16),
            wide(bf16), wide(bf16), wide(f32), wide(f32), pltpu.VMEM((PER_TILE, LANES, width), bf16),
            small(f32, ROWS), small(f32, ROWS), pltpu.VMEM((ROWS, width), f32),
            pltpu.SemaphoreType.DMA, pltpu.SemaphoreType.DMA((chunks,)),
        ],
        compiler_params=pltpu.CompilerParams(vmem_limit_bytes=SCAN_VMEM * MIB),
        name="scan_grads",
    )(received, params)


def unpack_kernel(heads, in_ref, x_ref, s_ref, b_ref, c_ref, b_sum, c_sum, s_sum):
    width = heads * HDIM

    @pl.when(pl.program_id(0) == 0)
    def _():
        for ref in (b_sum, c_sum, s_sum):
            ref[...] = jnp.zeros_like(ref)

    for n in range(in_ref.shape[0]):
        for i in range(width // LANES):
            lanes = slice(n * width + i * LANES, n * width + (i + 1) * LANES)
            x_ref[:, lanes] = in_ref[n, i * CHUNK : (i + 1) * CHUNK]
    part = lambda n, j: in_ref[n, width + j * CHUNK : width + (j + 1) * CHUNK].astype(f32)
    every = range(in_ref.shape[0])
    b_sum[...] += sum(part(n, 0) + part(n, 1) for n in every)
    c_sum[...] += sum(part(n, 2) + part(n, 3) for n in every)
    shape = (s_sum.shape[0], 16)
    for n in every:
        group = pl.program_id(0) * in_ref.shape[0] + n
        place = one_hot((iota(shape, 0) == iota(shape, 1) + group * heads) & (iota(shape, 1) < heads))
        s_sum[...] += mm(place.astype(bf16), in_ref[n, width + 4 * CHUNK :])

    @pl.when(pl.program_id(0) == pl.num_programs(0) - 1)
    def _():
        b_ref[...] = b_sum[...].astype(bf16)
        c_ref[...] = c_sum[...].astype(bf16)
        s_ref[...] = s_sum[...].astype(bf16)


def unpack(received, heads):
    groups, rows, _ = received.shape
    width = heads * HDIM
    part = groups // UNPACK_STEPS
    whole = lambda *shape: pl.BlockSpec(shape, lambda j: (0, 0))
    shapes = [(CHUNK, groups * width), (groups * heads, CHUNK), (CHUNK, NSTATE), (CHUNK, NSTATE)]
    return pl.pallas_call(
        lambda *refs: unpack_kernel(heads, *refs),
        grid=(UNPACK_STEPS,),
        in_specs=[pl.BlockSpec((part, rows, LANES), lambda j: (j, 0, 0))],
        out_specs=[pl.BlockSpec((CHUNK, part * width), lambda j: (0, j))] + [whole(*s) for s in shapes[1:]],
        out_shape=[jax.ShapeDtypeStruct(s, bf16) for s in shapes],
        scratch_shapes=[pltpu.VMEM(shapes[2], f32), pltpu.VMEM(shapes[2], f32), pltpu.VMEM(shapes[1], f32)],
        compiler_params=pltpu.CompilerParams(vmem_limit_bytes=UNPACK_VMEM * MIB),
        name="unpack",
    )(received)


def exchange(v):
    return lax.all_to_all(v, "seq", split_axis=0, concat_axis=0, tiled=True)


def pair_sum(v):
    replicas = lax.axis_size("dp")
    if replicas == 1:
        return v
    return v + lax.ppermute(v, "dp", [(i, i ^ 1) for i in range(replicas)])


def line_sum(v):
    half = lax.axis_size("dp") // 2
    if half <= 1:
        return v
    return lax.psum(v, "dp", axis_index_groups=[[2 * i + bit for i in range(half)] for bit in range(2)])


def shards(inputs, raw_step, write_keys, read_keys, grad_out, decay_log, skip_gain, step_bias):
    groups = lax.axis_size("seq")
    heads = decay_log.shape[0]
    send = pack(inputs[0], grad_out[0], write_keys[0], read_keys[0], raw_step[0].T, groups)
    params = jnp.stack([decay_log, skip_gain, step_bias])
    params = jnp.pad(jnp.concatenate([params] * (ROWS // heads), axis=1), ((0, 0), (0, LANES - ROWS)))
    back, per_head = scan_grads(exchange(send), params, heads)
    back, per_head = lax.optimization_barrier((back, pair_sum(per_head)))
    grad_x, grad_step, grad_write, grad_read = unpack(exchange(back), heads)
    totals = line_sum(per_head)[:3, :heads] / lax.axis_size("dp")
    return grad_x[None], grad_step.T[None], grad_write[None], grad_read[None], totals


def solution(mesh):
    rows = P("dp", "seq", None)
    heads = P("seq")
    return jax.shard_map(
        shards,
        mesh=mesh,
        in_specs=(rows,) * 5 + (heads,) * 3,
        out_specs=(rows,) * 4 + (P(None, "seq"),),
        check_vma=False,
    )
```

```python
import jax
import jax.numpy as jnp
from jax import lax
from jax.experimental import pallas as pl
from jax.experimental.pallas import tpu as pltpu
from jax.sharding import PartitionSpec as P

CHUNK = 128
LANES = 128
HDIM = 64
NSTATE = 128
ROWS = 8
MIB = 1 << 20
PACK_STEPS = 2
HALVES = 2
PER_TILE = LANES // (2 * ROWS)
UNROLL = 4
STATES_VMEM = 24
LOCAL_VMEM = 24
FINISH_VMEM = 24

f32 = jnp.float32
bf16 = jnp.bfloat16


def mm(a, b):
    return jnp.dot(a, b, preferred_element_type=f32)


def mm_nt(a, b):
    return lax.dot_general(a, b, (((1,), (1,)), ((), ())), preferred_element_type=f32)


def mm_tn(a, b):
    return lax.dot_general(a, b, (((0,), (0,)), ((), ())), preferred_element_type=f32)


def split2(v):
    high = v.astype(bf16)
    return high, (v - high.astype(f32)).astype(bf16)


def split3(v):
    high = v.astype(bf16).astype(f32)
    rest = v - high
    mid = rest.astype(bf16).astype(f32)
    return high, mid, rest - mid


def iota(shape, axis):
    return lax.broadcasted_iota(jnp.int32, shape, axis)


def one_hot(cond):
    return jnp.where(cond, 1.0, 0.0)


def mm_exact(v, ones):
    parts = mm(jnp.concatenate(split3(v), axis=0).astype(bf16), ones.astype(bf16))
    n = v.shape[0]
    return parts[:n] + parts[n : 2 * n] + parts[2 * n :]


def pack_kernel(groups, xa_ref, xb_ref, ga_ref, gb_ref, b_ref, c_ref, s_ref, out_ref):
    some = s_ref.shape[0] // (HALVES * groups)
    narrow = some * HDIM
    width = HALVES * narrow
    tall = 2 * width + 2 * CHUNK
    for n in range(out_ref.shape[0]):
        row = 0
        for ref in (xa_ref, xb_ref, ga_ref, gb_ref):
            for i in range(narrow // LANES):
                start = n * narrow + i * LANES
                out_ref[n, row : row + CHUNK] = ref[:, start : start + LANES]
                row += CHUNK
        out_ref[n, 2 * width : 2 * width + CHUNK] = b_ref[...]
        out_ref[n, 2 * width + CHUNK : tall] = c_ref[...]
        group = pl.program_id(0) * out_ref.shape[0] + n
        out_ref[n, tall:] = mm(head_pick(16, s_ref.shape[0], group, some, groups), s_ref[...]).astype(bf16)


def head_pick(rows, heads, group, some, groups):
    shape = (rows, heads)
    row, head = iota(shape, 0), iota(shape, 1)
    owner = group + groups * (row // some)
    return one_hot((head == owner * some + row % some) & (row < HALVES * some)).astype(bf16)


def pack(x, g, b, c, s, groups):
    narrow = s.shape[0] // (HALVES * groups) * HDIM
    rows = 2 * HALVES * narrow + 2 * CHUNK + 16
    part = groups // PACK_STEPS
    whole = lambda a: pl.BlockSpec(a.shape, lambda j: (0, 0))
    first = pl.BlockSpec((CHUNK, part * narrow), lambda j: (0, j))
    second = pl.BlockSpec((CHUNK, part * narrow), lambda j: (0, PACK_STEPS + j))
    return pl.pallas_call(
        lambda *refs: pack_kernel(groups, *refs),
        grid=(PACK_STEPS,),
        in_specs=[first, second, first, second, whole(b), whole(c), whole(s)],
        out_specs=pl.BlockSpec((part, rows, LANES), lambda j: (j, 0, 0)),
        out_shape=jax.ShapeDtypeStruct((groups, rows, LANES), bf16),
        compiler_params=pltpu.CompilerParams(vmem_limit_bytes=56 * MIB),
        name="pack",
    )(x, x, g, g, b, c, s)


class Layout:
    def __init__(self, heads, chunks):
        self.heads, self.chunks, self.width = heads, chunks, heads * HDIM
        self.blocks = self.width // LANES
        self.at_b = 2 * self.width
        self.at_c = self.at_b + CHUNK
        self.at_s = self.at_c + CHUNK
        self.body = self.width + 4 * CHUNK
        self.flat = (chunks * ROWS, LANES)
        self.cube = (chunks, ROWS, LANES)
        self.wide = (chunks, CHUNK, self.width)

    def spread(self):
        shape = (ROWS, self.width)
        return one_hot(iota(shape, 1) // HDIM == iota(shape, 0))

    def to_lanes(self, tile):
        return jnp.sum(jnp.concatenate([tile] * self.blocks, axis=1) * self.spread(), axis=0, keepdims=True)

    def columns(self, ref, k, start):
        return jnp.concatenate(
            [ref[k, start + i * CHUNK : start + (i + 1) * CHUNK] for i in range(self.blocks)], axis=1
        )

    def keys(self, ref, k):
        return ref[k, self.at_b : self.at_b + CHUNK], ref[k, self.at_c : self.at_c + CHUNK]

    def by_head(self):
        shape = (16, self.width)
        return one_hot(iota(shape, 1) // HDIM == iota(shape, 0)).astype(bf16)


SQUARE = (LANES, LANES)
TILE = (ROWS, LANES)


def along(*parts):
    return jnp.concatenate(parts, axis=1)


def under(*parts):
    return jnp.concatenate(parts, axis=0)


def grouped(chunks, step, carry, reverse=False):
    def turn(i, carry):
        for n in range(UNROLL):
            k = i * UNROLL + n
            carry = step(chunks - 1 - k if reverse else k, carry)
        return carry

    return lax.fori_loop(0, chunks // UNROLL, turn, carry)


def states_kernel(lay, in_ref, given_ref, flag_ref,
                  gh_ref, gl_ref, xh_ref, xl_ref, hs_ref, dl_ref, wide_ref,
                  step_ref, slope_ref, decay_ref, total_ref, par_ref, skip_ref, send_ref,
                  alpha_ref, gamma_ref, pick_ref):
    chunks, width = lay.chunks, lay.width

    for i in range(3):
        row = jnp.broadcast_to(given_ref[i : i + 1], TILE)
        mine = jnp.where(iota(TILE, 1) == iota(TILE, 0), row, 0.0)
        par_ref[i] = jnp.broadcast_to(jnp.sum(mine, axis=1, keepdims=True), TILE)

    raw = in_ref[:, lay.at_s : lay.at_s + 16].astype(f32)[:, :ROWS]
    z = raw + par_ref[2][None]
    step = jnp.maximum(z, 0.0) + jnp.log1p(jnp.exp(-jnp.abs(z)))
    decay = -jnp.exp(par_ref[0])[None] * step
    step_ref[...], slope_ref[...], decay_ref[...] = step, jnp.exp(z - step), decay
    upto = one_hot(iota(SQUARE, 0) <= iota(SQUARE, 1))
    level = mm_exact(decay.reshape(lay.flat), upto)
    total_ref[...] = jnp.exp(jnp.broadcast_to(level[:, LANES - 1 :], lay.flat)).reshape(lay.cube)
    for ref, v in ((alpha_ref, jnp.exp(level)), (gamma_ref, jnp.exp(-level) * step.reshape(lay.flat))):
        high = v.astype(bf16).astype(f32)
        parts = jnp.concatenate([high.reshape(lay.cube), (v - high).reshape(lay.cube)], axis=1)
        parts = parts.reshape(chunks // PER_TILE, LANES, LANES)
        for i in range(chunks // PER_TILE):
            ref[i] = parts[i].T.astype(bf16)

    in_tile = (LANES, width)
    at_head = iota(in_tile, 1) // HDIM == iota(in_tile, 0) % ROWS
    eye = one_hot(iota(SQUARE, 0) == iota(SQUARE, 1)).astype(bf16)
    for i in range(PER_TILE):
        pick_ref[i] = one_hot(at_head & (iota(in_tile, 0) // (2 * ROWS) == i)).astype(bf16)

    def expand(ref, k):
        return mm(ref[k // PER_TILE], pick_ref[k % PER_TILE])

    def flip(v):
        return mm_nt(eye, v).astype(bf16)

    skip_ref[...] = jnp.zeros_like(skip_ref)

    def forward(k, carry):
        state, early, prefix = carry
        x = lay.columns(in_ref, k, 0).astype(f32)
        g = lay.columns(in_ref, k, width).astype(f32)
        gt_high, gt_low = split2(expand(alpha_ref, k) * g)
        wide = expand(gamma_ref, k)
        xt_high, xt_low = split2(wide * x)
        wide_ref[k] = wide
        gh_ref[k], gl_ref[k], xh_ref[k], xl_ref[k] = gt_high, gt_low, xt_high, xt_low
        skip_ref[...] += jnp.sum((x * g).reshape(CHUNK // ROWS, ROWS, width), axis=0)
        hs_ref[k] = state
        keys_in, keys_out = lay.keys(in_ref, k)
        keys_in, keys_out = flip(keys_in), flip(keys_out)
        back = mm(along(keys_out, keys_out), under(gt_high, gt_low))
        dl_ref[k] = back
        total = lay.to_lanes(total_ref[k])
        state = total * (state + mm(along(keys_in, keys_in), under(xt_high, xt_low)))
        return state, early + prefix * back, prefix * total

    nothing = jnp.zeros((NSTATE, width), f32)
    state, early, _ = grouped(chunks, forward, (nothing, nothing, jnp.ones((1, width), f32)))
    send_ref[...] = jnp.where(flag_ref[0] == 0, state, early)


def scan_states(received, params, flag, lay):
    vmem = pl.BlockSpec(memory_space=pltpu.VMEM)
    shape = jax.ShapeDtypeStruct
    wide, cube = lay.wide, lay.cube
    tiles = pltpu.VMEM((lay.chunks // PER_TILE, LANES, LANES), bf16)
    return pl.pallas_call(
        lambda *refs: states_kernel(lay, *refs),
        in_specs=[vmem, vmem, pl.BlockSpec(memory_space=pltpu.SMEM)],
        out_specs=[vmem] * 14,
        out_shape=[shape(wide, bf16)] * 4 + [shape(wide, f32)] * 3 + [shape(cube, f32)] * 4
        + [shape((3, ROWS, LANES), f32), shape((ROWS, lay.width), f32), shape((NSTATE, lay.width), f32)],
        scratch_shapes=[tiles, tiles, pltpu.VMEM((PER_TILE, LANES, lay.width), bf16)],
        compiler_params=pltpu.CompilerParams(vmem_limit_bytes=STATES_VMEM * MIB),
        name="scan_states",
    )(received, params, flag)


def local_kernel(lay, in_ref, gh_ref, gl_ref, xh_ref, xl_ref, hs_ref, dl_ref, wide_ref, total_ref, par_ref,
                 gx_ref, din_ref, dout_ref, r_ref, c_ref):
    width = lay.width
    gather = lay.by_head()
    skip_wide = lay.to_lanes(par_ref[1])
    causal = iota(SQUARE, 0) >= iota(SQUARE, 1)

    def backward(k, dstate):
        through = lay.to_lanes(total_ref[k]) * dstate
        dh, dl = split2(through)
        hh, hl = split2(hs_ref[k])
        gh, gl, xh, xl = gh_ref[k], gl_ref[k], xh_ref[k], xl_ref[k]
        keys_in, keys_out = lay.keys(in_ref, k)

        sh, sl = split2(jnp.where(causal, mm_nt(keys_out, keys_in), 0.0))
        th, tl = split2(jnp.where(causal.T, mm_nt(keys_in, keys_out), 0.0))
        out_h, in_h = along(sh, keys_out), along(th, keys_in)
        y = mm(out_h, under(xh, hh)) + mm(out_h, under(xl, hl)) + mm(sl, xh)
        dx = mm(in_h, under(gh, dh)) + mm(in_h, under(gl, dl)) + mm(tl, gh)

        ds = mm_nt(gh, xh) + mm_nt(gh, xl) + mm_nt(gl, xh)
        ds = jnp.where(causal, ds, 0.0)
        ph, plow = split2(ds)
        qh, qlow = split2(ds.T)
        dout_ref[k] = mm(along(ph, plow), under(keys_in, keys_in)) + mm_nt(gh, hh) + mm_nt(gh, hl) + mm_nt(gl, hh)
        din_ref[k] = mm(along(qh, qlow), under(keys_out, keys_out)) + mm_nt(xh, dh) + mm_nt(xh, dl) + mm_nt(xl, dh)

        gt = gh.astype(f32) + gl.astype(f32)
        xt = xh.astype(f32) + xl.astype(f32)
        high, low = split2(under(gt * y, xt * dx))
        sums = mm_nt(gather, high) + mm_nt(gather, low)
        r_ref[k], c_ref[k] = sums[:ROWS, :CHUNK], sums[:ROWS, CHUNK:]
        gx_ref[k] = wide_ref[k] * dx + skip_wide * lay.columns(in_ref, k, width).astype(f32)
        return dl_ref[k] + through

    grouped(lay.chunks, backward, jnp.zeros((NSTATE, width), f32), reverse=True)


def scan_local(received, own, lay):
    gh, gl, xh, xl, hs, dl, wide, _, _, _, total, par, _, _ = own
    vmem = pl.BlockSpec(memory_space=pltpu.VMEM)
    shape = jax.ShapeDtypeStruct
    keys = (lay.chunks, CHUNK, NSTATE)
    return pl.pallas_call(
        lambda *refs: local_kernel(lay, *refs),
        in_specs=[vmem] * 10,
        out_specs=[vmem] * 5,
        out_shape=[shape(lay.wide, f32), shape(keys, f32), shape(keys, f32), shape(lay.cube, f32), shape(lay.cube, f32)],
        compiler_params=pltpu.CompilerParams(vmem_limit_bytes=LOCAL_VMEM * MIB),
        name="scan_local",
    )(received, gh, gl, xh, xl, hs, dl, wide, total, par)


def finish_kernel(lay, in_ref, gh_ref, gl_ref, xh_ref, xl_ref, wide_ref,
                  step_ref, slope_ref, decay_ref, total_ref, par_ref, skip_ref, sent_ref, came_ref,
                  gx_ref, din_ref, dout_ref, r_ref, c_ref, flag_ref,
                  out_ref, pout_ref, reach_ref, col_ref, row_ref):
    chunks, width, cube = lay.chunks, lay.width, lay.cube
    gather = lay.by_head()
    first = flag_ref[0] == 0

    run = jnp.ones(TILE, f32)
    before = []
    for k in range(chunks):
        before.append(run)
        run = run * total_ref[k]
    run = jnp.ones(TILE, f32)
    for k in reversed(range(chunks)):
        run = run * total_ref[k]
        reach_ref[k] = jnp.where(first, run, before[k])

    def store(k, grad_x, d_in, d_out):
        grad_x = grad_x.astype(bf16)
        for j in range(lay.blocks):
            out_ref[k, j * CHUNK : (j + 1) * CHUNK] = grad_x[:, j * LANES : (j + 1) * LANES]
        for j, part in enumerate(split2(d_in) + split2(d_out)):
            out_ref[k, width + j * CHUNK : width + (j + 1) * CHUNK] = part

    def correct(k, keys, high, low):
        uh, ul = split2(lay.to_lanes(reach_ref[k]) * came_ref[...])
        more = mm(along(keys, keys), under(uh, ul))
        d_keys = mm_nt(high, uh) + mm_nt(high, ul) + mm_nt(low, uh)
        ph, plow = split2((high.astype(f32) + low.astype(f32)) * more)
        return more, d_keys, (mm_nt(gather, ph) + mm_nt(gather, plow))[:ROWS]

    @pl.when(first)
    def _():
        def one(k, carry):
            more, d_keys, sums = correct(k, lay.keys(in_ref, k)[0], xh_ref[k], xl_ref[k])
            store(k, gx_ref[k] + wide_ref[k] * more, din_ref[k] + d_keys, dout_ref[k])
            row_ref[k], col_ref[k] = r_ref[k], c_ref[k] + sums
            return carry

        grouped(chunks, one, 0)

    @pl.when(jnp.logical_not(first))
    def _():
        def one(k, carry):
            _, d_keys, sums = correct(k, lay.keys(in_ref, k)[1], gh_ref[k], gl_ref[k])
            store(k, gx_ref[k], din_ref[k], dout_ref[k] + d_keys)
            row_ref[k], col_ref[k] = r_ref[k] + sums, c_ref[k]
            return carry

        grouped(chunks, one, 0)

    spread = lay.spread()
    per_head = lambda row: jnp.sum(spread * row, axis=1, keepdims=True)
    cross = per_head(jnp.sum(sent_ref[...] * came_ref[...], axis=0, keepdims=True))
    later = jnp.broadcast_to(jnp.where(first, cross, 0.0), TILE)
    col = col_ref[...]
    since = one_hot(iota(SQUARE, 0) >= iota(SQUARE, 1))
    suffix = mm_exact((row_ref[...] - col).reshape(lay.flat), since).reshape(cube)
    sums = jnp.broadcast_to(suffix[:, :, :1], cube)
    carried = [None] * chunks
    for k in reversed(range(chunks)):
        carried[k] = later[None]
        later = later + sums[k]
    d_decay = suffix + jnp.concatenate(carried, axis=0)
    rate = -jnp.exp(par_ref[0])
    d_raw = slope_ref[...] * (col / step_ref[...] + rate[None] * d_decay)
    out_ref[:, lay.body :] = jnp.concatenate([d_raw, jnp.zeros(cube, f32)], axis=1).astype(bf16)

    result = jnp.zeros(TILE, f32)
    per = (
        jnp.sum(jnp.sum(d_decay * decay_ref[...], axis=0), axis=1, keepdims=True),
        per_head(jnp.sum(skip_ref[...], axis=0, keepdims=True)),
        jnp.sum(jnp.sum(d_raw, axis=0), axis=1, keepdims=True),
    )
    for i, v in enumerate(per):
        row = jnp.sum(jnp.where(iota(TILE, 0) == iota(TILE, 1), jnp.broadcast_to(v, TILE), 0.0), axis=0, keepdims=True)
        result = jnp.where(iota(TILE, 0) == i, jnp.broadcast_to(row, TILE), result)
    pout_ref[...] = result


def scan_finish(received, own, local, came, flag, lay):
    gh, gl, xh, xl, _, _, wide, step, slope, decay, total, par, skip, sent = own
    vmem = pl.BlockSpec(memory_space=pltpu.VMEM)
    shape = jax.ShapeDtypeStruct
    small = pltpu.VMEM(lay.cube, f32)
    return pl.pallas_call(
        lambda *refs: finish_kernel(lay, *refs),
        in_specs=[vmem] * 19 + [pl.BlockSpec(memory_space=pltpu.SMEM)],
        out_specs=[vmem] * 2,
        out_shape=[shape((lay.chunks, lay.body + 16, LANES), bf16), shape(TILE, f32)],
        scratch_shapes=[small, small, small],
        compiler_params=pltpu.CompilerParams(vmem_limit_bytes=FINISH_VMEM * MIB),
        name="scan_finish",
    )(received, gh, gl, xh, xl, wide, step, slope, decay, total, par, skip, sent, came, *local, flag)


def unpack_kernel(lay, in_ref, x_ref, s_ref, b_ref, c_ref):
    groups, width = in_ref.shape[0], lay.width
    narrow = width // HALVES
    some = lay.heads // HALVES
    for n in range(groups):
        for half in range(HALVES):
            for i in range(narrow // LANES):
                start = (half * groups + n) * narrow + i * LANES
                row = half * narrow + i * CHUNK
                x_ref[:, start : start + LANES] = in_ref[n, row : row + CHUNK]
    part = lambda n, j: in_ref[n, width + j * CHUNK : width + (j + 1) * CHUNK].astype(f32)
    every = range(groups)
    b_ref[...] = sum(part(n, 0) + part(n, 1) for n in every).astype(bf16)
    c_ref[...] = sum(part(n, 2) + part(n, 3) for n in every).astype(bf16)
    picks = [head_pick(16, s_ref.shape[0], n, some, groups) for n in every]
    s_ref[...] = sum(mm_tn(picks[n], in_ref[n, lay.body :]) for n in every).astype(bf16)


def unpack(received, lay):
    groups = received.shape[0]
    shapes = [(CHUNK, groups * lay.width), (groups * lay.heads, CHUNK), (CHUNK, NSTATE), (CHUNK, NSTATE)]
    vmem = pl.BlockSpec(memory_space=pltpu.VMEM)
    return pl.pallas_call(
        lambda *refs: unpack_kernel(lay, *refs),
        in_specs=[vmem],
        out_specs=[vmem] * 4,
        out_shape=[jax.ShapeDtypeStruct(s, bf16) for s in shapes],
        compiler_params=pltpu.CompilerParams(vmem_limit_bytes=24 * MIB),
        name="unpack",
    )(received)


def exchange(v):
    groups = v.shape[0]
    halves = [[half * groups + i for i in range(groups)] for half in range(HALVES)]
    return lax.all_to_all(v, "seq", split_axis=0, concat_axis=0, tiled=True, axis_index_groups=halves)


def from_partner(v):
    groups = lax.axis_size("seq") // HALVES
    return lax.ppermute(v, "seq", [(i, (i + groups) % (2 * groups)) for i in range(2 * groups)])


def pair_sum(v):
    replicas = lax.axis_size("dp")
    if replicas == 1:
        return v
    return v + lax.ppermute(v, "dp", [(i, i ^ 1) for i in range(replicas)])


def line_sum(v):
    half = lax.axis_size("dp") // 2
    if half <= 1:
        return v
    return lax.psum(v, "dp", axis_index_groups=[[2 * i + bit for i in range(half)] for bit in range(2)])


def shards(inputs, raw_step, write_keys, read_keys, grad_out, decay_log, skip_gain, step_bias):
    groups = lax.axis_size("seq") // HALVES
    some = decay_log.shape[0]
    lay = Layout(HALVES * some, groups)
    half = lax.axis_index("seq") // groups
    flag = half.astype(jnp.int32)[None]
    send = pack(inputs[0], grad_out[0], write_keys[0], read_keys[0], raw_step[0].T, groups)
    mine = jnp.stack([decay_log, skip_gain, step_bias])
    send, mine = lax.optimization_barrier((send, mine))
    other = from_partner(mine)
    first = half == 0
    params = jnp.concatenate([jnp.where(first, mine, other), jnp.where(first, other, mine)], axis=1)
    params = jnp.pad(params, ((0, 0), (0, LANES - lay.heads)))

    received = exchange(send)
    own = scan_states(received, params, flag, lay)
    came = from_partner(own[-1])
    local = scan_local(received, own, lay)
    back, per_head = scan_finish(received, own, local, came, flag, lay)
    grad_x, grad_step, grad_write, grad_read = unpack(exchange(back), lay)
    per_head = per_head + from_partner(per_head)
    totals = line_sum(pair_sum(per_head))[:3] / lax.axis_size("dp")
    totals = jnp.where(first, totals[:, :some], totals[:, some : 2 * some])
    return grad_x[None], grad_step.T[None], grad_write[None], grad_read[None], totals


def solution(mesh):
    rows = P("dp", "seq", None)
    heads = P("seq")
    return jax.shard_map(
        shards,
        mesh=mesh,
        in_specs=(rows,) * 5 + (heads,) * 3,
        out_specs=(rows,) * 4 + (P(None, "seq"),),
        check_vma=False,
    )
```

```python
import jax
import jax.numpy as jnp
from jax import lax
from jax.experimental import pallas as pl
from jax.experimental.pallas import tpu as pltpu
from jax.sharding import PartitionSpec as P

CHUNK = 128
LANES = 128
HDIM = 64
NSTATE = 128
ROWS = 8
MIB = 1 << 20
PACK_STEPS = 2
HALVES = 2
PER_TILE = LANES // (2 * ROWS)
UNROLL = 4
STATES_VMEM = 24
LOCAL_VMEM = 24
FINISH_VMEM = 24

f32 = jnp.float32
bf16 = jnp.bfloat16


def mm(a, b):
    return jnp.dot(a, b, preferred_element_type=f32)


def mm_nt(a, b):
    return lax.dot_general(a, b, (((1,), (1,)), ((), ())), preferred_element_type=f32)


def mm_tn(a, b):
    return lax.dot_general(a, b, (((0,), (0,)), ((), ())), preferred_element_type=f32)


def split2(v):
    high = v.astype(bf16)
    return high, (v - high.astype(f32)).astype(bf16)


def split3(v):
    high = v.astype(bf16).astype(f32)
    rest = v - high
    mid = rest.astype(bf16).astype(f32)
    return high, mid, rest - mid


def iota(shape, axis):
    return lax.broadcasted_iota(jnp.int32, shape, axis)


def one_hot(cond):
    return jnp.where(cond, 1.0, 0.0)


def mm_exact(v, ones):
    parts = mm(jnp.concatenate(split3(v), axis=0).astype(bf16), ones.astype(bf16))
    n = v.shape[0]
    return parts[:n] + parts[n : 2 * n] + parts[2 * n :]


def pack_kernel(groups, xa_ref, xb_ref, ga_ref, gb_ref, b_ref, c_ref, s_ref, out_ref):
    some = s_ref.shape[0] // (HALVES * groups)
    narrow = some * HDIM
    width = HALVES * narrow
    tall = 2 * width + 2 * CHUNK
    for n in range(out_ref.shape[0]):
        row = 0
        for ref in (xa_ref, xb_ref, ga_ref, gb_ref):
            for i in range(narrow // LANES):
                start = n * narrow + i * LANES
                out_ref[n, row : row + CHUNK] = ref[:, start : start + LANES]
                row += CHUNK
        out_ref[n, 2 * width : 2 * width + CHUNK] = b_ref[...]
        out_ref[n, 2 * width + CHUNK : tall] = c_ref[...]
        group = pl.program_id(0) * out_ref.shape[0] + n
        out_ref[n, tall:] = mm(head_pick(16, s_ref.shape[0], group, some, groups), s_ref[...]).astype(bf16)


def head_pick(rows, heads, group, some, groups):
    shape = (rows, heads)
    row, head = iota(shape, 0), iota(shape, 1)
    owner = group + groups * (row // some)
    return one_hot((head == owner * some + row % some) & (row < HALVES * some)).astype(bf16)


def pack(x, g, b, c, s, groups):
    narrow = s.shape[0] // (HALVES * groups) * HDIM
    rows = 2 * HALVES * narrow + 2 * CHUNK + 16
    part = groups // PACK_STEPS
    whole = lambda a: pl.BlockSpec(a.shape, lambda j: (0, 0))
    first = pl.BlockSpec((CHUNK, part * narrow), lambda j: (0, j))
    second = pl.BlockSpec((CHUNK, part * narrow), lambda j: (0, PACK_STEPS + j))
    return pl.pallas_call(
        lambda *refs: pack_kernel(groups, *refs),
        grid=(PACK_STEPS,),
        in_specs=[first, second, first, second, whole(b), whole(c), whole(s)],
        out_specs=pl.BlockSpec((part, rows, LANES), lambda j: (j, 0, 0)),
        out_shape=jax.ShapeDtypeStruct((groups, rows, LANES), bf16),
        compiler_params=pltpu.CompilerParams(vmem_limit_bytes=56 * MIB),
        name="pack",
    )(x, x, g, g, b, c, s)


class Layout:
    def __init__(self, heads, chunks):
        self.heads, self.chunks, self.width = heads, chunks, heads * HDIM
        self.blocks = self.width // LANES
        self.at_b = 2 * self.width
        self.at_c = self.at_b + CHUNK
        self.at_s = self.at_c + CHUNK
        self.body = self.width + 4 * CHUNK
        self.flat = (chunks * ROWS, LANES)
        self.cube = (chunks, ROWS, LANES)
        self.wide = (chunks, CHUNK, self.width)

    def spread(self):
        shape = (ROWS, self.width)
        return one_hot(iota(shape, 1) // HDIM == iota(shape, 0))

    def to_lanes(self, tile):
        return jnp.sum(jnp.concatenate([tile] * self.blocks, axis=1) * self.spread(), axis=0, keepdims=True)

    def columns(self, ref, k, start):
        return jnp.concatenate(
            [ref[k, start + i * CHUNK : start + (i + 1) * CHUNK] for i in range(self.blocks)], axis=1
        )

    def keys(self, ref, k):
        return ref[k, self.at_b : self.at_b + CHUNK], ref[k, self.at_c : self.at_c + CHUNK]

    def by_head(self):
        shape = (16, self.width)
        return one_hot(iota(shape, 1) // HDIM == iota(shape, 0)).astype(bf16)


SQUARE = (LANES, LANES)
TILE = (ROWS, LANES)


def along(*parts):
    return jnp.concatenate(parts, axis=1)


def under(*parts):
    return jnp.concatenate(parts, axis=0)


def grouped(chunks, step, carry, reverse=False):
    def turn(i, carry):
        for n in range(UNROLL):
            k = i * UNROLL + n
            carry = step(chunks - 1 - k if reverse else k, carry)
        return carry

    return lax.fori_loop(0, chunks // UNROLL, turn, carry)


def states_kernel(lay, in_ref, given_ref, flag_ref,
                  gh_ref, gl_ref, xh_ref, xl_ref, hs_ref, dl_ref, wide_ref,
                  step_ref, slope_ref, decay_ref, total_ref, par_ref, skip_ref, send_ref,
                  alpha_ref, gamma_ref, pick_ref):
    chunks, width = lay.chunks, lay.width

    for i in range(3):
        row = jnp.broadcast_to(given_ref[i : i + 1], TILE)
        mine = jnp.where(iota(TILE, 1) == iota(TILE, 0), row, 0.0)
        par_ref[i] = jnp.broadcast_to(jnp.sum(mine, axis=1, keepdims=True), TILE)

    raw = in_ref[:, lay.at_s : lay.at_s + 16].astype(f32)[:, :ROWS]
    z = raw + par_ref[2][None]
    step = jnp.maximum(z, 0.0) + jnp.log1p(jnp.exp(-jnp.abs(z)))
    decay = -jnp.exp(par_ref[0])[None] * step
    step_ref[...], slope_ref[...], decay_ref[...] = step, jnp.exp(z - step), decay
    upto = one_hot(iota(SQUARE, 0) <= iota(SQUARE, 1))
    level = mm_exact(decay.reshape(lay.flat), upto)
    total_ref[...] = jnp.exp(jnp.broadcast_to(level[:, LANES - 1 :], lay.flat)).reshape(lay.cube)
    for ref, v in ((alpha_ref, jnp.exp(level)), (gamma_ref, jnp.exp(-level) * step.reshape(lay.flat))):
        high = v.astype(bf16).astype(f32)
        parts = jnp.concatenate([high.reshape(lay.cube), (v - high).reshape(lay.cube)], axis=1)
        parts = parts.reshape(chunks // PER_TILE, LANES, LANES)
        for i in range(chunks // PER_TILE):
            ref[i] = parts[i].T.astype(bf16)

    in_tile = (LANES, width)
    at_head = iota(in_tile, 1) // HDIM == iota(in_tile, 0) % ROWS
    eye = one_hot(iota(SQUARE, 0) == iota(SQUARE, 1)).astype(bf16)
    for i in range(PER_TILE):
        pick_ref[i] = one_hot(at_head & (iota(in_tile, 0) // (2 * ROWS) == i)).astype(bf16)

    def expand(ref, k):
        return mm(ref[k // PER_TILE], pick_ref[k % PER_TILE])

    def flip(v):
        return mm_nt(eye, v).astype(bf16)

    skip_ref[...] = jnp.zeros_like(skip_ref)

    def forward(k, carry):
        state, early, prefix = carry
        x = lay.columns(in_ref, k, 0).astype(f32)
        g = lay.columns(in_ref, k, width).astype(f32)
        gt_high, gt_low = split2(expand(alpha_ref, k) * g)
        wide = expand(gamma_ref, k)
        xt_high, xt_low = split2(wide * x)
        wide_ref[k] = wide
        gh_ref[k], gl_ref[k], xh_ref[k], xl_ref[k] = gt_high, gt_low, xt_high, xt_low
        skip_ref[...] += jnp.sum((x * g).reshape(CHUNK // ROWS, ROWS, width), axis=0)
        hs_ref[k] = state
        keys_in, keys_out = lay.keys(in_ref, k)
        keys_in, keys_out = flip(keys_in), flip(keys_out)
        back = mm(along(keys_out, keys_out), under(gt_high, gt_low))
        dl_ref[k] = back
        total = lay.to_lanes(total_ref[k])
        state = total * (state + mm(along(keys_in, keys_in), under(xt_high, xt_low)))
        return state, early + prefix * back, prefix * total

    nothing = jnp.zeros((NSTATE, width), f32)
    state, early, _ = grouped(chunks, forward, (nothing, nothing, jnp.ones((1, width), f32)))
    send_ref[...] = jnp.where(flag_ref[0] == 0, state, early)


def scan_states(received, params, flag, lay):
    vmem = pl.BlockSpec(memory_space=pltpu.VMEM)
    shape = jax.ShapeDtypeStruct
    wide, cube = lay.wide, lay.cube
    tiles = pltpu.VMEM((lay.chunks // PER_TILE, LANES, LANES), bf16)
    return pl.pallas_call(
        lambda *refs: states_kernel(lay, *refs),
        in_specs=[vmem, vmem, pl.BlockSpec(memory_space=pltpu.SMEM)],
        out_specs=[vmem] * 14,
        out_shape=[shape(wide, bf16)] * 4 + [shape(wide, f32)] * 3 + [shape(cube, f32)] * 4
        + [shape((3, ROWS, LANES), f32), shape((ROWS, lay.width), f32), shape((NSTATE, lay.width), f32)],
        scratch_shapes=[tiles, tiles, pltpu.VMEM((PER_TILE, LANES, lay.width), bf16)],
        compiler_params=pltpu.CompilerParams(vmem_limit_bytes=STATES_VMEM * MIB),
        name="scan_states",
    )(received, params, flag)


def local_kernel(lay, in_ref, gh_ref, gl_ref, xh_ref, xl_ref, hs_ref, dl_ref, wide_ref, total_ref, par_ref,
                 gx_ref, din_ref, dout_ref, r_ref, c_ref):
    width = lay.width
    gather = lay.by_head()
    skip_wide = lay.to_lanes(par_ref[1])
    causal = iota(SQUARE, 0) >= iota(SQUARE, 1)

    def backward(k, dstate):
        through = lay.to_lanes(total_ref[k]) * dstate
        dh, dl = split2(through)
        hh, hl = split2(hs_ref[k])
        gh, gl, xh, xl = gh_ref[k], gl_ref[k], xh_ref[k], xl_ref[k]
        keys_in, keys_out = lay.keys(in_ref, k)

        sh, sl = split2(jnp.where(causal, mm_nt(keys_out, keys_in), 0.0))
        th, tl = split2(jnp.where(causal.T, mm_nt(keys_in, keys_out), 0.0))
        out_h, in_h = along(sh, keys_out), along(th, keys_in)
        y = mm(out_h, under(xh, hh)) + mm(out_h, under(xl, hl)) + mm(sl, xh)
        dx = mm(in_h, under(gh, dh)) + mm(in_h, under(gl, dl)) + mm(tl, gh)

        ds = mm_nt(gh, xh) + mm_nt(gh, xl) + mm_nt(gl, xh)
        ds = jnp.where(causal, ds, 0.0)
        ph, plow = split2(ds)
        qh, qlow = split2(ds.T)
        dout_ref[k] = mm(along(ph, plow), under(keys_in, keys_in)) + mm_nt(gh, hh) + mm_nt(gh, hl) + mm_nt(gl, hh)
        din_ref[k] = mm(along(qh, qlow), under(keys_out, keys_out)) + mm_nt(xh, dh) + mm_nt(xh, dl) + mm_nt(xl, dh)

        gt = gh.astype(f32) + gl.astype(f32)
        xt = xh.astype(f32) + xl.astype(f32)
        high, low = split2(under(gt * y, xt * dx))
        sums = mm_nt(gather, high) + mm_nt(gather, low)
        r_ref[k], c_ref[k] = sums[:ROWS, :CHUNK], sums[:ROWS, CHUNK:]
        gx_ref[k] = wide_ref[k] * dx + skip_wide * lay.columns(in_ref, k, width).astype(f32)
        return dl_ref[k] + through

    grouped(lay.chunks, backward, jnp.zeros((NSTATE, width), f32), reverse=True)


def scan_local(received, own, lay):
    gh, gl, xh, xl, hs, dl, wide, _, _, _, total, par, _, _ = own
    vmem = pl.BlockSpec(memory_space=pltpu.VMEM)
    shape = jax.ShapeDtypeStruct
    keys = (lay.chunks, CHUNK, NSTATE)
    return pl.pallas_call(
        lambda *refs: local_kernel(lay, *refs),
        in_specs=[vmem] * 10,
        out_specs=[vmem] * 5,
        out_shape=[shape(lay.wide, f32), shape(keys, f32), shape(keys, f32), shape(lay.cube, f32), shape(lay.cube, f32)],
        compiler_params=pltpu.CompilerParams(vmem_limit_bytes=LOCAL_VMEM * MIB),
        name="scan_local",
    )(received, gh, gl, xh, xl, hs, dl, wide, total, par)


def finish_kernel(lay, in_ref, gh_ref, gl_ref, xh_ref, xl_ref,
                  step_ref, slope_ref, decay_ref, total_ref, par_ref, skip_ref, sent_ref, came_ref,
                  r_ref, c_ref, flag_ref, dstep_ref, pout_ref, uh_ref, ul_ref, more_ref,
                  reach_ref, col_ref, row_ref):
    chunks, width, cube = lay.chunks, lay.width, lay.cube
    gather = lay.by_head()
    first = flag_ref[0] == 0

    run = jnp.ones(TILE, f32)
    before = []
    for k in range(chunks):
        before.append(run)
        run = run * total_ref[k]
    run = jnp.ones(TILE, f32)
    for k in reversed(range(chunks)):
        run = run * total_ref[k]
        reach_ref[k] = jnp.where(first, run, before[k])

    def correct(keys_at, high_ref, low_ref, old_ref, new_ref):
        def one(k, carry):
            uh, ul = split2(lay.to_lanes(reach_ref[k]) * came_ref[...])
            uh_ref[k], ul_ref[k] = uh, ul
            keys = in_ref[k, keys_at : keys_at + CHUNK]
            more = mm(along(keys, keys), under(uh, ul))
            more_ref[k] = more
            ph, plow = split2((high_ref[k].astype(f32) + low_ref[k].astype(f32)) * more)
            new_ref[k] = old_ref[k] + (mm_nt(gather, ph) + mm_nt(gather, plow))[:ROWS]
            return carry

        grouped(chunks, one, 0)

    @pl.when(first)
    def _():
        row_ref[...] = r_ref[...]
        correct(lay.at_b, xh_ref, xl_ref, c_ref, col_ref)

    @pl.when(jnp.logical_not(first))
    def _():
        col_ref[...] = c_ref[...]
        correct(lay.at_c, gh_ref, gl_ref, r_ref, row_ref)

    spread = lay.spread()
    per_head = lambda row: jnp.sum(spread * row, axis=1, keepdims=True)
    cross = per_head(jnp.sum(sent_ref[...] * came_ref[...], axis=0, keepdims=True))
    later = jnp.broadcast_to(jnp.where(first, cross, 0.0), TILE)
    col = col_ref[...]
    since = one_hot(iota(SQUARE, 0) >= iota(SQUARE, 1))
    suffix = mm_exact((row_ref[...] - col).reshape(lay.flat), since).reshape(cube)
    sums = jnp.broadcast_to(suffix[:, :, :1], cube)
    carried = [None] * chunks
    for k in reversed(range(chunks)):
        carried[k] = later[None]
        later = later + sums[k]
    d_decay = suffix + jnp.concatenate(carried, axis=0)
    rate = -jnp.exp(par_ref[0])
    d_raw = slope_ref[...] * (col / step_ref[...] + rate[None] * d_decay)
    dstep_ref[...] = jnp.concatenate([d_raw, jnp.zeros(cube, f32)], axis=1).astype(bf16)

    result = jnp.zeros(TILE, f32)
    per = (
        jnp.sum(jnp.sum(d_decay * decay_ref[...], axis=0), axis=1, keepdims=True),
        per_head(jnp.sum(skip_ref[...], axis=0, keepdims=True)),
        jnp.sum(jnp.sum(d_raw, axis=0), axis=1, keepdims=True),
    )
    for i, v in enumerate(per):
        row = jnp.sum(jnp.where(iota(TILE, 0) == iota(TILE, 1), jnp.broadcast_to(v, TILE), 0.0), axis=0, keepdims=True)
        result = jnp.where(iota(TILE, 0) == i, jnp.broadcast_to(row, TILE), result)
    pout_ref[...] = result


def scan_finish(received, own, r, c, came, flag, lay):
    gh, gl, xh, xl, _, _, _, step, slope, decay, total, par, skip, sent = own
    vmem = pl.BlockSpec(memory_space=pltpu.VMEM)
    shape = jax.ShapeDtypeStruct
    small = pltpu.VMEM(lay.cube, f32)
    return pl.pallas_call(
        lambda *refs: finish_kernel(lay, *refs),
        in_specs=[vmem] * 15 + [pl.BlockSpec(memory_space=pltpu.SMEM)],
        out_specs=[vmem] * 5,
        out_shape=[shape((lay.chunks, 16, LANES), bf16), shape(TILE, f32), shape(lay.wide, bf16), shape(lay.wide, bf16),
                   shape(lay.wide, f32)],
        scratch_shapes=[small, small, small],
        compiler_params=pltpu.CompilerParams(vmem_limit_bytes=FINISH_VMEM * MIB),
        name="scan_finish",
    )(received, gh, gl, xh, xl, step, slope, decay, total, par, skip, sent, came, r, c, flag)


def message_kernel(lay, gh_ref, gl_ref, xh_ref, xl_ref, wide_ref, gx_ref, din_ref, dout_ref,
                   dstep_ref, uh_ref, ul_ref, more_ref, flag_ref, out_ref):
    width = lay.width
    first = flag_ref[0] == 0
    out_ref[:, lay.body :] = dstep_ref[...]

    def d_keys(k, high_ref, low_ref):
        high, low = high_ref[k], low_ref[k]
        return mm_nt(high, uh_ref[k]) + mm_nt(high, ul_ref[k]) + mm_nt(low, uh_ref[k])

    def store(k, grad_x, d_in, d_out):
        grad_x = grad_x.astype(bf16)
        for j in range(lay.blocks):
            out_ref[k, j * CHUNK : (j + 1) * CHUNK] = grad_x[:, j * LANES : (j + 1) * LANES]
        for j, part in enumerate(split2(d_in) + split2(d_out)):
            out_ref[k, width + j * CHUNK : width + (j + 1) * CHUNK] = part

    @pl.when(first)
    def _():
        def one(k, carry):
            store(k, gx_ref[k] + wide_ref[k] * more_ref[k], din_ref[k] + d_keys(k, xh_ref, xl_ref), dout_ref[k])
            return carry

        grouped(lay.chunks, one, 0)

    @pl.when(jnp.logical_not(first))
    def _():
        def one(k, carry):
            store(k, gx_ref[k], din_ref[k], dout_ref[k] + d_keys(k, gh_ref, gl_ref))
            return carry

        grouped(lay.chunks, one, 0)


def message(own, local, finish, flag, lay):
    gh, gl, xh, xl, _, _, wide, *_ = own
    dstep, _, uh, ul, more = finish
    vmem = pl.BlockSpec(memory_space=pltpu.VMEM)
    return pl.pallas_call(
        lambda *refs: message_kernel(lay, *refs),
        in_specs=[vmem] * 12 + [pl.BlockSpec(memory_space=pltpu.SMEM)],
        out_specs=vmem,
        out_shape=jax.ShapeDtypeStruct((lay.chunks, lay.body + 16, LANES), bf16),
        compiler_params=pltpu.CompilerParams(vmem_limit_bytes=FINISH_VMEM * MIB),
        cost_estimate=pl.CostEstimate(flops=400_000_000, bytes_accessed=20_000_000, transcendentals=0),
        name="message",
    )(gh, gl, xh, xl, wide, *local[:3], dstep, uh, ul, more, flag)


def unpack_kernel(lay, in_ref, x_ref, s_ref, b_ref, c_ref):
    groups, width = in_ref.shape[0], lay.width
    narrow = width // HALVES
    some = lay.heads // HALVES
    for n in range(groups):
        for half in range(HALVES):
            for i in range(narrow // LANES):
                start = (half * groups + n) * narrow + i * LANES
                row = half * narrow + i * CHUNK
                x_ref[:, start : start + LANES] = in_ref[n, row : row + CHUNK]
    part = lambda n, j: in_ref[n, width + j * CHUNK : width + (j + 1) * CHUNK].astype(f32)
    every = range(groups)
    b_ref[...] = sum(part(n, 0) + part(n, 1) for n in every).astype(bf16)
    c_ref[...] = sum(part(n, 2) + part(n, 3) for n in every).astype(bf16)
    picks = [head_pick(16, s_ref.shape[0], n, some, groups) for n in every]
    s_ref[...] = sum(mm_tn(picks[n], in_ref[n, lay.body :]) for n in every).astype(bf16)


def unpack(received, lay):
    groups = received.shape[0]
    shapes = [(CHUNK, groups * lay.width), (groups * lay.heads, CHUNK), (CHUNK, NSTATE), (CHUNK, NSTATE)]
    vmem = pl.BlockSpec(memory_space=pltpu.VMEM)
    return pl.pallas_call(
        lambda *refs: unpack_kernel(lay, *refs),
        in_specs=[vmem],
        out_specs=[vmem] * 4,
        out_shape=[jax.ShapeDtypeStruct(s, bf16) for s in shapes],
        compiler_params=pltpu.CompilerParams(vmem_limit_bytes=24 * MIB),
        name="unpack",
    )(received)


def exchange(v):
    groups = v.shape[0]
    halves = [[half * groups + i for i in range(groups)] for half in range(HALVES)]
    return lax.all_to_all(v, "seq", split_axis=0, concat_axis=0, tiled=True, axis_index_groups=halves)


def from_partner(v):
    groups = lax.axis_size("seq") // HALVES
    return lax.ppermute(v, "seq", [(i, (i + groups) % (2 * groups)) for i in range(2 * groups)])


def near_sum(v):
    replicas, shards = lax.axis_size("dp"), lax.axis_size("seq")
    if replicas == 1:
        return v + from_partner(v)
    halves = lambda i: (i + shards // HALVES) % shards
    across = [(r * shards + i, (r ^ 1) * shards + halves(i)) for r in range(replicas) for i in range(shards)]
    pair = lax.ppermute(v, "dp", [(r, r ^ 1) for r in range(replicas)])
    return (v + from_partner(v)) + (pair + lax.ppermute(v, ("dp", "seq"), across))


def line_sum(v):
    half = lax.axis_size("dp") // 2
    if half <= 1:
        return v
    v = v + lax.ppermute(v, "dp", [(i, i ^ 2) for i in range(2 * half)])
    if half == 2:
        return v
    lines = [[2 * i + bit for i in range(odd, half, 2)] for odd in range(2) for bit in range(2)]
    return lax.psum(v, "dp", axis_index_groups=lines)


def shards(inputs, raw_step, write_keys, read_keys, grad_out, decay_log, skip_gain, step_bias):
    groups = lax.axis_size("seq") // HALVES
    some = decay_log.shape[0]
    lay = Layout(HALVES * some, groups)
    half = lax.axis_index("seq") // groups
    flag = half.astype(jnp.int32)[None]
    send = pack(inputs[0], grad_out[0], write_keys[0], read_keys[0], raw_step[0].T, groups)
    send, *mine = lax.optimization_barrier((send, decay_log, skip_gain, step_bias))
    mine = jnp.stack(mine)
    other = from_partner(mine)
    first = half == 0
    params = jnp.concatenate([jnp.where(first, mine, other), jnp.where(first, other, mine)], axis=1)
    params = jnp.pad(params, ((0, 0), (0, LANES - lay.heads)))

    received = exchange(send)
    own = scan_states(received, params, flag, lay)
    came = from_partner(own[-1])
    local = scan_local(received, own, lay)
    finish = scan_finish(received, own, local[3], local[4], came, flag, lay)
    back = message(own, local, finish, flag, lay)
    back, per_head = lax.optimization_barrier((back, near_sum(finish[1])))
    grad_x, grad_step, grad_write, grad_read = unpack(exchange(back), lay)
    totals = line_sum(per_head)[:3] / lax.axis_size("dp")
    totals = jnp.where(first, totals[:, :some], totals[:, some : 2 * some])
    return grad_x[None], grad_step.T[None], grad_write[None], grad_read[None], totals


def solution(mesh):
    rows = P("dp", "seq", None)
    heads = P("seq")
    return jax.shard_map(
        shards,
        mesh=mesh,
        in_specs=(rows,) * 5 + (heads,) * 3,
        out_specs=(rows,) * 4 + (P(None, "seq"),),
        check_vma=False,
    )
```

```python
import jax
import jax.numpy as jnp
from jax import lax
from jax.experimental import pallas as pl
from jax.experimental.pallas import tpu as pltpu
from jax.sharding import PartitionSpec as P

CHUNK = 128
LANES = 128
HDIM = 64
NSTATE = 128
ROWS = 8
MIB = 1 << 20
PACK_STEPS = 2
HALVES = 2
PER_TILE = LANES // (2 * ROWS)
UNROLL = 8
STATES_VMEM = 24
LOCAL_VMEM = 24
FINISH_VMEM = 24

f32 = jnp.float32
bf16 = jnp.bfloat16


def mm(a, b):
    return jnp.dot(a, b, preferred_element_type=f32)


def mm_nt(a, b):
    return lax.dot_general(a, b, (((1,), (1,)), ((), ())), preferred_element_type=f32)


def mm_tn(a, b):
    return lax.dot_general(a, b, (((0,), (0,)), ((), ())), preferred_element_type=f32)


def split2(v):
    high = v.astype(bf16)
    return high, (v - high.astype(f32)).astype(bf16)


def split3(v):
    high = v.astype(bf16).astype(f32)
    rest = v - high
    mid = rest.astype(bf16).astype(f32)
    return high, mid, rest - mid


def iota(shape, axis):
    return lax.broadcasted_iota(jnp.int32, shape, axis)


def one_hot(cond):
    return jnp.where(cond, 1.0, 0.0)


def mm_exact(v, ones):
    parts = mm(jnp.concatenate(split3(v), axis=0).astype(bf16), ones.astype(bf16))
    n = v.shape[0]
    return parts[:n] + parts[n : 2 * n] + parts[2 * n :]


def pack_kernel(groups, xa_ref, xb_ref, ga_ref, gb_ref, b_ref, c_ref, s_ref, out_ref):
    some = s_ref.shape[0] // (HALVES * groups)
    narrow = some * HDIM
    width = HALVES * narrow
    tall = 2 * width + 2 * CHUNK
    for n in range(out_ref.shape[0]):
        row = 0
        for ref in (xa_ref, xb_ref, ga_ref, gb_ref):
            for i in range(narrow // LANES):
                start = n * narrow + i * LANES
                out_ref[n, row : row + CHUNK] = ref[:, start : start + LANES]
                row += CHUNK
        out_ref[n, 2 * width : 2 * width + CHUNK] = b_ref[...]
        out_ref[n, 2 * width + CHUNK : tall] = c_ref[...]
        group = pl.program_id(0) * out_ref.shape[0] + n
        out_ref[n, tall:] = mm(head_pick(16, s_ref.shape[0], group, some, groups), s_ref[...]).astype(bf16)


def head_pick(rows, heads, group, some, groups):
    shape = (rows, heads)
    row, head = iota(shape, 0), iota(shape, 1)
    owner = group + groups * (row // some)
    return one_hot((head == owner * some + row % some) & (row < HALVES * some)).astype(bf16)


def pack(x, g, b, c, s, groups):
    narrow = s.shape[0] // (HALVES * groups) * HDIM
    rows = 2 * HALVES * narrow + 2 * CHUNK + 16
    part = groups // PACK_STEPS
    whole = lambda a: pl.BlockSpec(a.shape, lambda j: (0, 0))
    first = pl.BlockSpec((CHUNK, part * narrow), lambda j: (0, j))
    second = pl.BlockSpec((CHUNK, part * narrow), lambda j: (0, PACK_STEPS + j))
    return pl.pallas_call(
        lambda *refs: pack_kernel(groups, *refs),
        grid=(PACK_STEPS,),
        in_specs=[first, second, first, second, whole(b), whole(c), whole(s)],
        out_specs=pl.BlockSpec((part, rows, LANES), lambda j: (j, 0, 0)),
        out_shape=jax.ShapeDtypeStruct((groups, rows, LANES), bf16),
        compiler_params=pltpu.CompilerParams(vmem_limit_bytes=56 * MIB),
        name="pack",
    )(x, x, g, g, b, c, s)


class Layout:
    def __init__(self, heads, chunks):
        self.heads, self.chunks, self.width = heads, chunks, heads * HDIM
        self.blocks = self.width // LANES
        self.at_b = 2 * self.width
        self.at_c = self.at_b + CHUNK
        self.at_s = self.at_c + CHUNK
        self.body = self.width + 4 * CHUNK
        self.flat = (chunks * ROWS, LANES)
        self.cube = (chunks, ROWS, LANES)
        self.wide = (chunks, CHUNK, self.width)

    def spread(self):
        shape = (ROWS, self.width)
        return one_hot(iota(shape, 1) // HDIM == iota(shape, 0))

    def to_lanes(self, tile):
        return jnp.sum(jnp.concatenate([tile] * self.blocks, axis=1) * self.spread(), axis=0, keepdims=True)

    def columns(self, ref, k, start):
        return jnp.concatenate(
            [ref[k, start + i * CHUNK : start + (i + 1) * CHUNK] for i in range(self.blocks)], axis=1
        )

    def keys(self, ref, k):
        return ref[k, self.at_b : self.at_b + CHUNK], ref[k, self.at_c : self.at_c + CHUNK]

    def by_head(self):
        shape = (16, self.width)
        return one_hot(iota(shape, 1) // HDIM == iota(shape, 0)).astype(bf16)


SQUARE = (LANES, LANES)
TILE = (ROWS, LANES)


def along(*parts):
    return jnp.concatenate(parts, axis=1)


def under(*parts):
    return jnp.concatenate(parts, axis=0)


def grouped(chunks, step, carry, reverse=False):
    def turn(i, carry):
        for n in range(UNROLL):
            k = i * UNROLL + n
            carry = step(chunks - 1 - k if reverse else k, carry)
        return carry

    return lax.fori_loop(0, chunks // UNROLL, turn, carry)


def states_kernel(lay, in_ref, given_ref, flag_ref,
                  gh_ref, gl_ref, xh_ref, xl_ref, hs_ref, dl_ref, wide_ref,
                  step_ref, slope_ref, decay_ref, total_ref, par_ref, skip_ref, send_ref,
                  alpha_ref, gamma_ref, pick_ref):
    chunks, width = lay.chunks, lay.width

    for i in range(3):
        row = jnp.broadcast_to(given_ref[i : i + 1], TILE)
        mine = jnp.where(iota(TILE, 1) == iota(TILE, 0), row, 0.0)
        par_ref[i] = jnp.broadcast_to(jnp.sum(mine, axis=1, keepdims=True), TILE)

    raw = in_ref[:, lay.at_s : lay.at_s + 16].astype(f32)[:, :ROWS]
    z = raw + par_ref[2][None]
    step = jnp.maximum(z, 0.0) + jnp.log1p(jnp.exp(-jnp.abs(z)))
    decay = -jnp.exp(par_ref[0])[None] * step
    step_ref[...], slope_ref[...], decay_ref[...] = step, jnp.exp(z - step), decay
    upto = one_hot(iota(SQUARE, 0) <= iota(SQUARE, 1))
    level = mm_exact(decay.reshape(lay.flat), upto)
    total_ref[...] = jnp.exp(jnp.broadcast_to(level[:, LANES - 1 :], lay.flat)).reshape(lay.cube)
    for ref, v in ((alpha_ref, jnp.exp(level)), (gamma_ref, jnp.exp(-level) * step.reshape(lay.flat))):
        high = v.astype(bf16).astype(f32)
        parts = jnp.concatenate([high.reshape(lay.cube), (v - high).reshape(lay.cube)], axis=1)
        parts = parts.reshape(chunks // PER_TILE, LANES, LANES)
        for i in range(chunks // PER_TILE):
            ref[i] = parts[i].T.astype(bf16)

    in_tile = (LANES, width)
    at_head = iota(in_tile, 1) // HDIM == iota(in_tile, 0) % ROWS
    eye = one_hot(iota(SQUARE, 0) == iota(SQUARE, 1)).astype(bf16)
    for i in range(PER_TILE):
        pick_ref[i] = one_hot(at_head & (iota(in_tile, 0) // (2 * ROWS) == i)).astype(bf16)

    def expand(ref, k):
        return mm(ref[k // PER_TILE], pick_ref[k % PER_TILE])

    def flip(v):
        return mm_nt(eye, v).astype(bf16)

    skip_ref[...] = jnp.zeros_like(skip_ref)

    def forward(k, carry):
        state, early, prefix = carry
        x = lay.columns(in_ref, k, 0).astype(f32)
        g = lay.columns(in_ref, k, width).astype(f32)
        gt_high, gt_low = split2(expand(alpha_ref, k) * g)
        wide = expand(gamma_ref, k)
        xt_high, xt_low = split2(wide * x)
        wide_ref[k] = wide
        gh_ref[k], gl_ref[k], xh_ref[k], xl_ref[k] = gt_high, gt_low, xt_high, xt_low
        skip_ref[...] += jnp.sum((x * g).reshape(CHUNK // ROWS, ROWS, width), axis=0)
        hs_ref[k] = state
        keys_in, keys_out = lay.keys(in_ref, k)
        keys_in, keys_out = flip(keys_in), flip(keys_out)
        back = mm(along(keys_out, keys_out), under(gt_high, gt_low))
        dl_ref[k] = back
        total = lay.to_lanes(total_ref[k])
        state = total * (state + mm(along(keys_in, keys_in), under(xt_high, xt_low)))
        return state, early + prefix * back, prefix * total

    nothing = jnp.zeros((NSTATE, width), f32)
    state, early, _ = grouped(chunks, forward, (nothing, nothing, jnp.ones((1, width), f32)))
    send_ref[...] = jnp.where(flag_ref[0] == 0, state, early)


def scan_states(received, params, flag, lay):
    vmem = pl.BlockSpec(memory_space=pltpu.VMEM)
    shape = jax.ShapeDtypeStruct
    wide, cube = lay.wide, lay.cube
    tiles = pltpu.VMEM((lay.chunks // PER_TILE, LANES, LANES), bf16)
    return pl.pallas_call(
        lambda *refs: states_kernel(lay, *refs),
        in_specs=[vmem, vmem, pl.BlockSpec(memory_space=pltpu.SMEM)],
        out_specs=[vmem] * 14,
        out_shape=[shape(wide, bf16)] * 4 + [shape(wide, f32)] * 3 + [shape(cube, f32)] * 4
        + [shape((3, ROWS, LANES), f32), shape((ROWS, lay.width), f32), shape((NSTATE, lay.width), f32)],
        scratch_shapes=[tiles, tiles, pltpu.VMEM((PER_TILE, LANES, lay.width), bf16)],
        compiler_params=pltpu.CompilerParams(vmem_limit_bytes=STATES_VMEM * MIB),
        name="scan_states",
    )(received, params, flag)


def local_kernel(lay, in_ref, gh_ref, gl_ref, xh_ref, xl_ref, hs_ref, dl_ref, wide_ref, total_ref, par_ref,
                 gx_ref, din_ref, dout_ref, r_ref, c_ref):
    width = lay.width
    gather = lay.by_head()
    skip_wide = lay.to_lanes(par_ref[1])
    causal = iota(SQUARE, 0) >= iota(SQUARE, 1)

    def backward(k, dstate):
        through = lay.to_lanes(total_ref[k]) * dstate
        dh, dl = split2(through)
        hh, hl = split2(hs_ref[k])
        gh, gl, xh, xl = gh_ref[k], gl_ref[k], xh_ref[k], xl_ref[k]
        keys_in, keys_out = lay.keys(in_ref, k)

        sh, sl = split2(jnp.where(causal, mm_nt(keys_out, keys_in), 0.0))
        th, tl = split2(jnp.where(causal.T, mm_nt(keys_in, keys_out), 0.0))
        out_h, in_h = along(sh, keys_out), along(th, keys_in)
        y = mm(out_h, under(xh, hh)) + mm(out_h, under(xl, hl)) + mm(sl, xh)
        dx = mm(in_h, under(gh, dh)) + mm(in_h, under(gl, dl)) + mm(tl, gh)

        ds = mm_nt(gh, xh) + mm_nt(gh, xl) + mm_nt(gl, xh)
        ds = jnp.where(causal, ds, 0.0)
        ph, plow = split2(ds)
        qh, qlow = split2(ds.T)
        dout_ref[k] = mm(along(ph, plow), under(keys_in, keys_in)) + mm_nt(gh, hh) + mm_nt(gh, hl) + mm_nt(gl, hh)
        din_ref[k] = mm(along(qh, qlow), under(keys_out, keys_out)) + mm_nt(xh, dh) + mm_nt(xh, dl) + mm_nt(xl, dh)

        gt = gh.astype(f32) + gl.astype(f32)
        xt = xh.astype(f32) + xl.astype(f32)
        high, low = split2(under(gt * y, xt * dx))
        sums = mm_nt(gather, high) + mm_nt(gather, low)
        r_ref[k], c_ref[k] = sums[:ROWS, :CHUNK], sums[:ROWS, CHUNK:]
        gx_ref[k] = wide_ref[k] * dx + skip_wide * lay.columns(in_ref, k, width).astype(f32)
        return dl_ref[k] + through

    grouped(lay.chunks, backward, jnp.zeros((NSTATE, width), f32), reverse=True)


def scan_local(received, own, lay):
    gh, gl, xh, xl, hs, dl, wide, _, _, _, total, par, _, _ = own
    vmem = pl.BlockSpec(memory_space=pltpu.VMEM)
    shape = jax.ShapeDtypeStruct
    keys = (lay.chunks, CHUNK, NSTATE)
    return pl.pallas_call(
        lambda *refs: local_kernel(lay, *refs),
        in_specs=[vmem] * 10,
        out_specs=[vmem] * 5,
        out_shape=[shape(lay.wide, f32), shape(keys, f32), shape(keys, f32), shape(lay.cube, f32), shape(lay.cube, f32)],
        compiler_params=pltpu.CompilerParams(vmem_limit_bytes=LOCAL_VMEM * MIB),
        name="scan_local",
    )(received, gh, gl, xh, xl, hs, dl, wide, total, par)


def finish_kernel(lay, in_ref, gh_ref, gl_ref, xh_ref, xl_ref, wide_ref,
                  step_ref, slope_ref, decay_ref, total_ref, par_ref, skip_ref, sent_ref, came_ref,
                  gx_ref, din_ref, dout_ref, r_ref, c_ref, flag_ref,
                  out_ref, pout_ref, reach_ref, col_ref, row_ref):
    chunks, width, cube = lay.chunks, lay.width, lay.cube
    gather = lay.by_head()
    first = flag_ref[0] == 0

    run = jnp.ones(TILE, f32)
    before = []
    for k in range(chunks):
        before.append(run)
        run = run * total_ref[k]
    run = jnp.ones(TILE, f32)
    for k in reversed(range(chunks)):
        run = run * total_ref[k]
        reach_ref[k] = jnp.where(first, run, before[k])

    def store(k, grad_x, d_in, d_out):
        grad_x = grad_x.astype(bf16)
        for j in range(lay.blocks):
            out_ref[k, j * CHUNK : (j + 1) * CHUNK] = grad_x[:, j * LANES : (j + 1) * LANES]
        for j, part in enumerate(split2(d_in) + split2(d_out)):
            out_ref[k, width + j * CHUNK : width + (j + 1) * CHUNK] = part

    def correct(k, keys, high, low):
        uh, ul = split2(lay.to_lanes(reach_ref[k]) * came_ref[...])
        more = mm(along(keys, keys), under(uh, ul))
        d_keys = mm_nt(high, uh) + mm_nt(high, ul) + mm_nt(low, uh)
        ph, plow = split2((high.astype(f32) + low.astype(f32)) * more)
        return more, d_keys, (mm_nt(gather, ph) + mm_nt(gather, plow))[:ROWS]

    @pl.when(first)
    def _():
        def one(k, carry):
            more, d_keys, sums = correct(k, lay.keys(in_ref, k)[0], xh_ref[k], xl_ref[k])
            store(k, gx_ref[k] + wide_ref[k] * more, din_ref[k] + d_keys, dout_ref[k])
            row_ref[k], col_ref[k] = r_ref[k], c_ref[k] + sums
            return carry

        grouped(chunks, one, 0)

    @pl.when(jnp.logical_not(first))
    def _():
        def one(k, carry):
            _, d_keys, sums = correct(k, lay.keys(in_ref, k)[1], gh_ref[k], gl_ref[k])
            store(k, gx_ref[k], din_ref[k], dout_ref[k] + d_keys)
            row_ref[k], col_ref[k] = r_ref[k] + sums, c_ref[k]
            return carry

        grouped(chunks, one, 0)

    spread = lay.spread()
    per_head = lambda row: jnp.sum(spread * row, axis=1, keepdims=True)
    cross = per_head(jnp.sum(sent_ref[...] * came_ref[...], axis=0, keepdims=True))
    later = jnp.broadcast_to(jnp.where(first, cross, 0.0), TILE)
    col = col_ref[...]
    since = one_hot(iota(SQUARE, 0) >= iota(SQUARE, 1))
    suffix = mm_exact((row_ref[...] - col).reshape(lay.flat), since).reshape(cube)
    sums = jnp.broadcast_to(suffix[:, :, :1], cube)
    carried = [None] * chunks
    for k in reversed(range(chunks)):
        carried[k] = later[None]
        later = later + sums[k]
    d_decay = suffix + jnp.concatenate(carried, axis=0)
    rate = -jnp.exp(par_ref[0])
    d_raw = slope_ref[...] * (col / step_ref[...] + rate[None] * d_decay)
    out_ref[:, lay.body :] = jnp.concatenate([d_raw, jnp.zeros(cube, f32)], axis=1).astype(bf16)

    result = jnp.zeros(TILE, f32)
    per = (
        jnp.sum(jnp.sum(d_decay * decay_ref[...], axis=0), axis=1, keepdims=True),
        per_head(jnp.sum(skip_ref[...], axis=0, keepdims=True)),
        jnp.sum(jnp.sum(d_raw, axis=0), axis=1, keepdims=True),
    )
    for i, v in enumerate(per):
        row = jnp.sum(jnp.where(iota(TILE, 0) == iota(TILE, 1), jnp.broadcast_to(v, TILE), 0.0), axis=0, keepdims=True)
        result = jnp.where(iota(TILE, 0) == i, jnp.broadcast_to(row, TILE), result)
    pout_ref[...] = result


def scan_finish(received, own, local, came, flag, lay):
    gh, gl, xh, xl, _, _, wide, step, slope, decay, total, par, skip, sent = own
    vmem = pl.BlockSpec(memory_space=pltpu.VMEM)
    shape = jax.ShapeDtypeStruct
    small = pltpu.VMEM(lay.cube, f32)
    return pl.pallas_call(
        lambda *refs: finish_kernel(lay, *refs),
        in_specs=[vmem] * 19 + [pl.BlockSpec(memory_space=pltpu.SMEM)],
        out_specs=[vmem] * 2,
        out_shape=[shape((lay.chunks, lay.body + 16, LANES), bf16), shape(TILE, f32)],
        scratch_shapes=[small, small, small],
        compiler_params=pltpu.CompilerParams(vmem_limit_bytes=FINISH_VMEM * MIB),
        name="scan_finish",
    )(received, gh, gl, xh, xl, wide, step, slope, decay, total, par, skip, sent, came, *local, flag)


def unpack_kernel(lay, in_ref, x_ref, s_ref, b_ref, c_ref):
    groups, width = in_ref.shape[0], lay.width
    narrow = width // HALVES
    some = lay.heads // HALVES
    for n in range(groups):
        for half in range(HALVES):
            for i in range(narrow // LANES):
                start = (half * groups + n) * narrow + i * LANES
                row = half * narrow + i * CHUNK
                x_ref[:, start : start + LANES] = in_ref[n, row : row + CHUNK]
    part = lambda n, j: in_ref[n, width + j * CHUNK : width + (j + 1) * CHUNK].astype(f32)
    every = range(groups)
    b_ref[...] = sum(part(n, 0) + part(n, 1) for n in every).astype(bf16)
    c_ref[...] = sum(part(n, 2) + part(n, 3) for n in every).astype(bf16)
    picks = [head_pick(16, s_ref.shape[0], n, some, groups) for n in every]
    s_ref[...] = sum(mm_tn(picks[n], in_ref[n, lay.body :]) for n in every).astype(bf16)


def unpack(received, lay):
    groups = received.shape[0]
    shapes = [(CHUNK, groups * lay.width), (groups * lay.heads, CHUNK), (CHUNK, NSTATE), (CHUNK, NSTATE)]
    vmem = pl.BlockSpec(memory_space=pltpu.VMEM)
    return pl.pallas_call(
        lambda *refs: unpack_kernel(lay, *refs),
        in_specs=[vmem],
        out_specs=[vmem] * 4,
        out_shape=[jax.ShapeDtypeStruct(s, bf16) for s in shapes],
        compiler_params=pltpu.CompilerParams(vmem_limit_bytes=24 * MIB),
        name="unpack",
    )(received)


def exchange(v):
    groups = v.shape[0]
    halves = [[half * groups + i for i in range(groups)] for half in range(HALVES)]
    return lax.all_to_all(v, "seq", split_axis=0, concat_axis=0, tiled=True, axis_index_groups=halves)


def from_partner(v):
    groups = lax.axis_size("seq") // HALVES
    return lax.ppermute(v, "seq", [(i, (i + groups) % (2 * groups)) for i in range(2 * groups)])


def near_sum(v):
    replicas, shards = lax.axis_size("dp"), lax.axis_size("seq")
    if replicas == 1:
        return v + from_partner(v)
    halves = lambda i: (i + shards // HALVES) % shards
    across = [(r * shards + i, (r ^ 1) * shards + halves(i)) for r in range(replicas) for i in range(shards)]
    pair = lax.ppermute(v, "dp", [(r, r ^ 1) for r in range(replicas)])
    return (v + from_partner(v)) + (pair + lax.ppermute(v, ("dp", "seq"), across))


def line_sum(v):
    half = lax.axis_size("dp") // 2
    if half <= 1:
        return v
    v = v + lax.ppermute(v, "dp", [(i, i ^ 2) for i in range(2 * half)])
    if half == 2:
        return v
    lines = [[2 * i + bit for i in range(odd, half, 2)] for odd in range(2) for bit in range(2)]
    return lax.psum(v, "dp", axis_index_groups=lines)


def shards(inputs, raw_step, write_keys, read_keys, grad_out, decay_log, skip_gain, step_bias):
    groups = lax.axis_size("seq") // HALVES
    some = decay_log.shape[0]
    lay = Layout(HALVES * some, groups)
    half = lax.axis_index("seq") // groups
    flag = half.astype(jnp.int32)[None]
    send = pack(inputs[0], grad_out[0], write_keys[0], read_keys[0], raw_step[0].T, groups)
    send, *mine = lax.optimization_barrier((send, decay_log, skip_gain, step_bias))
    mine = jnp.stack(mine)
    other = from_partner(mine)
    first = half == 0
    params = jnp.concatenate([jnp.where(first, mine, other), jnp.where(first, other, mine)], axis=1)
    params = jnp.pad(params, ((0, 0), (0, LANES - lay.heads)))

    received = exchange(send)
    own = scan_states(received, params, flag, lay)
    came = from_partner(own[-1])
    local = scan_local(received, own, lay)
    back, per_head = scan_finish(received, own, local, came, flag, lay)
    grad_x, grad_step, grad_write, grad_read = unpack(exchange(back), lay)
    totals = line_sum(near_sum(per_head))[:3] / lax.axis_size("dp")
    totals = jnp.where(first, totals[:, :some], totals[:, some : 2 * some])
    return grad_x[None], grad_step.T[None], grad_write[None], grad_read[None], totals


def solution(mesh):
    rows = P("dp", "seq", None)
    heads = P("seq")
    return jax.shard_map(
        shards,
        mesh=mesh,
        in_specs=(rows,) * 5 + (heads,) * 3,
        out_specs=(rows,) * 4 + (P(None, "seq"),),
        check_vma=False,
    )
```

```python
import jax
import jax.numpy as jnp
from jax import lax
from jax.experimental import pallas as pl
from jax.experimental.pallas import tpu as pltpu
from jax.sharding import PartitionSpec as P

CHUNK = 128
LANES = 128
HDIM = 64
NSTATE = 128
ROWS = 8
MIB = 1 << 20
PACK_STEPS = 2
HALVES = 2
PER_TILE = LANES // (2 * ROWS)
UNROLL = 8
STATES_VMEM = 24
LOCAL_VMEM = 24
FINISH_VMEM = 24

f32 = jnp.float32
bf16 = jnp.bfloat16


def mm(a, b):
    return jnp.dot(a, b, preferred_element_type=f32)


def mm_nt(a, b):
    return lax.dot_general(a, b, (((1,), (1,)), ((), ())), preferred_element_type=f32)


def mm_tn(a, b):
    return lax.dot_general(a, b, (((0,), (0,)), ((), ())), preferred_element_type=f32)


def split2(v):
    high = v.astype(bf16)
    return high, (v - high.astype(f32)).astype(bf16)


def split3(v):
    high = v.astype(bf16).astype(f32)
    rest = v - high
    mid = rest.astype(bf16).astype(f32)
    return high, mid, rest - mid


def iota(shape, axis):
    return lax.broadcasted_iota(jnp.int32, shape, axis)


def one_hot(cond):
    return jnp.where(cond, 1.0, 0.0)


def mm_exact(v, ones):
    parts = mm(jnp.concatenate(split3(v), axis=0).astype(bf16), ones.astype(bf16))
    n = v.shape[0]
    return parts[:n] + parts[n : 2 * n] + parts[2 * n :]


def pack_kernel(groups, xa_ref, xb_ref, ga_ref, gb_ref, b_ref, c_ref, s_ref, out_ref):
    some = s_ref.shape[0] // (HALVES * groups)
    narrow = some * HDIM
    width = HALVES * narrow
    tall = 2 * width + 2 * CHUNK
    for n in range(out_ref.shape[0]):
        row = 0
        for ref in (xa_ref, xb_ref, ga_ref, gb_ref):
            for i in range(narrow // LANES):
                start = n * narrow + i * LANES
                out_ref[n, row : row + CHUNK] = ref[:, start : start + LANES]
                row += CHUNK
        out_ref[n, 2 * width : 2 * width + CHUNK] = b_ref[...]
        out_ref[n, 2 * width + CHUNK : tall] = c_ref[...]
        group = pl.program_id(0) * out_ref.shape[0] + n
        out_ref[n, tall:] = mm(head_pick(16, s_ref.shape[0], group, some, groups), s_ref[...]).astype(bf16)


def head_pick(rows, heads, group, some, groups):
    shape = (rows, heads)
    row, head = iota(shape, 0), iota(shape, 1)
    owner = group + groups * (row // some)
    return one_hot((head == owner * some + row % some) & (row < HALVES * some)).astype(bf16)


def pack(x, g, b, c, s, groups):
    narrow = s.shape[0] // (HALVES * groups) * HDIM
    rows = 2 * HALVES * narrow + 2 * CHUNK + 16
    part = groups // PACK_STEPS
    whole = lambda a: pl.BlockSpec(a.shape, lambda j: (0, 0))
    first = pl.BlockSpec((CHUNK, part * narrow), lambda j: (0, j))
    second = pl.BlockSpec((CHUNK, part * narrow), lambda j: (0, PACK_STEPS + j))
    return pl.pallas_call(
        lambda *refs: pack_kernel(groups, *refs),
        grid=(PACK_STEPS,),
        in_specs=[first, second, first, second, whole(b), whole(c), whole(s)],
        out_specs=pl.BlockSpec((part, rows, LANES), lambda j: (j, 0, 0)),
        out_shape=jax.ShapeDtypeStruct((groups, rows, LANES), bf16),
        compiler_params=pltpu.CompilerParams(vmem_limit_bytes=56 * MIB),
        name="pack",
    )(x, x, g, g, b, c, s)


class Layout:
    def __init__(self, heads, chunks):
        self.heads, self.chunks, self.width = heads, chunks, heads * HDIM
        self.blocks = self.width // LANES
        self.at_b = 2 * self.width
        self.at_c = self.at_b + CHUNK
        self.at_s = self.at_c + CHUNK
        self.body = self.width + 4 * CHUNK
        self.flat = (chunks * ROWS, LANES)
        self.cube = (chunks, ROWS, LANES)
        self.wide = (chunks, CHUNK, self.width)

    def spread(self):
        shape = (ROWS, self.width)
        return one_hot(iota(shape, 1) // HDIM == iota(shape, 0))

    def to_lanes(self, tile):
        return jnp.sum(jnp.concatenate([tile] * self.blocks, axis=1) * self.spread(), axis=0, keepdims=True)

    def columns(self, ref, k, start):
        return jnp.concatenate(
            [ref[k, start + i * CHUNK : start + (i + 1) * CHUNK] for i in range(self.blocks)], axis=1
        )

    def keys(self, ref, k):
        return ref[k, self.at_b : self.at_b + CHUNK], ref[k, self.at_c : self.at_c + CHUNK]

    def by_head(self):
        shape = (16, self.width)
        return one_hot(iota(shape, 1) // HDIM == iota(shape, 0)).astype(bf16)


SQUARE = (LANES, LANES)
TILE = (ROWS, LANES)


def along(*parts):
    return jnp.concatenate(parts, axis=1)


def under(*parts):
    return jnp.concatenate(parts, axis=0)


def grouped(chunks, step, carry, reverse=False):
    def turn(i, carry):
        for n in range(UNROLL):
            k = i * UNROLL + n
            carry = step(chunks - 1 - k if reverse else k, carry)
        return carry

    return lax.fori_loop(0, chunks // UNROLL, turn, carry)


def states_kernel(lay, in_ref, given_ref, flag_ref,
                  gh_ref, gl_ref, xh_ref, xl_ref, hs_ref, dl_ref, wide_ref,
                  step_ref, slope_ref, decay_ref, total_ref, par_ref, skip_ref, send_ref,
                  alpha_ref, gamma_ref, pick_ref):
    chunks, width = lay.chunks, lay.width

    for i in range(3):
        row = jnp.broadcast_to(given_ref[i : i + 1], TILE)
        mine = jnp.where(iota(TILE, 1) == iota(TILE, 0), row, 0.0)
        par_ref[i] = jnp.broadcast_to(jnp.sum(mine, axis=1, keepdims=True), TILE)

    raw = in_ref[:, lay.at_s : lay.at_s + 16].astype(f32)[:, :ROWS]
    z = raw + par_ref[2][None]
    step = jnp.maximum(z, 0.0) + jnp.log1p(jnp.exp(-jnp.abs(z)))
    decay = -jnp.exp(par_ref[0])[None] * step
    step_ref[...], slope_ref[...], decay_ref[...] = step, jnp.exp(z - step), decay
    upto = one_hot(iota(SQUARE, 0) <= iota(SQUARE, 1))
    level = mm_exact(decay.reshape(lay.flat), upto)
    total_ref[...] = jnp.exp(jnp.broadcast_to(level[:, LANES - 1 :], lay.flat)).reshape(lay.cube)
    for ref, v in ((alpha_ref, jnp.exp(level)), (gamma_ref, jnp.exp(-level) * step.reshape(lay.flat))):
        high = v.astype(bf16).astype(f32)
        parts = jnp.concatenate([high.reshape(lay.cube), (v - high).reshape(lay.cube)], axis=1)
        parts = parts.reshape(chunks // PER_TILE, LANES, LANES)
        for i in range(chunks // PER_TILE):
            ref[i] = parts[i].T.astype(bf16)

    in_tile = (LANES, width)
    at_head = iota(in_tile, 1) // HDIM == iota(in_tile, 0) % ROWS
    eye = one_hot(iota(SQUARE, 0) == iota(SQUARE, 1)).astype(bf16)
    for i in range(PER_TILE):
        pick_ref[i] = one_hot(at_head & (iota(in_tile, 0) // (2 * ROWS) == i)).astype(bf16)

    def expand(ref, k):
        return mm(ref[k // PER_TILE], pick_ref[k % PER_TILE])

    def flip(v):
        return mm_nt(eye, v).astype(bf16)

    skip_ref[...] = jnp.zeros_like(skip_ref)

    def forward(k, carry):
        state, early, prefix = carry
        x = lay.columns(in_ref, k, 0).astype(f32)
        g = lay.columns(in_ref, k, width).astype(f32)
        gt_high, gt_low = split2(expand(alpha_ref, k) * g)
        wide = expand(gamma_ref, k)
        xt_high, xt_low = split2(wide * x)
        wide_ref[k] = wide
        gh_ref[k], gl_ref[k], xh_ref[k], xl_ref[k] = gt_high, gt_low, xt_high, xt_low
        skip_ref[...] += jnp.sum((x * g).reshape(CHUNK // ROWS, ROWS, width), axis=0)
        hs_ref[k] = state
        keys_in, keys_out = lay.keys(in_ref, k)
        keys_in, keys_out = flip(keys_in), flip(keys_out)
        back = mm(along(keys_out, keys_out), under(gt_high, gt_low))
        dl_ref[k] = back
        total = lay.to_lanes(total_ref[k])
        state = total * (state + mm(along(keys_in, keys_in), under(xt_high, xt_low)))
        return state, early + prefix * back, prefix * total

    nothing = jnp.zeros((NSTATE, width), f32)
    state, early, _ = grouped(chunks, forward, (nothing, nothing, jnp.ones((1, width), f32)))
    send_ref[...] = jnp.where(flag_ref[0] == 0, state, early)


def scan_states(received, params, flag, lay):
    vmem = pl.BlockSpec(memory_space=pltpu.VMEM)
    shape = jax.ShapeDtypeStruct
    wide, cube = lay.wide, lay.cube
    tiles = pltpu.VMEM((lay.chunks // PER_TILE, LANES, LANES), bf16)
    return pl.pallas_call(
        lambda *refs: states_kernel(lay, *refs),
        in_specs=[vmem, vmem, pl.BlockSpec(memory_space=pltpu.SMEM)],
        out_specs=[vmem] * 14,
        out_shape=[shape(wide, bf16)] * 4 + [shape(wide, f32)] * 3 + [shape(cube, f32)] * 4
        + [shape((3, ROWS, LANES), f32), shape((ROWS, lay.width), f32), shape((NSTATE, lay.width), f32)],
        scratch_shapes=[tiles, tiles, pltpu.VMEM((PER_TILE, LANES, lay.width), bf16)],
        compiler_params=pltpu.CompilerParams(vmem_limit_bytes=STATES_VMEM * MIB),
        name="scan_states",
    )(received, params, flag)


def local_kernel(lay, in_ref, gh_ref, gl_ref, xh_ref, xl_ref, hs_ref, dl_ref, wide_ref, total_ref, par_ref,
                 gx_ref, din_ref, dout_ref, r_ref, c_ref):
    width = lay.width
    gather = lay.by_head()
    skip_wide = lay.to_lanes(par_ref[1])
    causal = iota(SQUARE, 0) >= iota(SQUARE, 1)

    def backward(k, dstate):
        through = lay.to_lanes(total_ref[k]) * dstate
        dh, dl = split2(through)
        hh, hl = split2(hs_ref[k])
        gh, gl, xh, xl = gh_ref[k], gl_ref[k], xh_ref[k], xl_ref[k]
        keys_in, keys_out = lay.keys(in_ref, k)

        sh, sl = split2(jnp.where(causal, mm_nt(keys_out, keys_in), 0.0))
        th, tl = split2(jnp.where(causal.T, mm_nt(keys_in, keys_out), 0.0))
        out_h, in_h = along(sh, keys_out), along(th, keys_in)
        y = mm(out_h, under(xh, hh)) + mm(out_h, under(xl, hl)) + mm(sl, xh)
        dx = mm(in_h, under(gh, dh)) + mm(in_h, under(gl, dl)) + mm(tl, gh)

        ds = mm_nt(gh, xh) + mm_nt(gh, xl) + mm_nt(gl, xh)
        ds = jnp.where(causal, ds, 0.0)
        ph, plow = split2(ds)
        qh, qlow = split2(ds.T)
        dout_ref[k] = mm(along(ph, plow), under(keys_in, keys_in)) + mm_nt(gh, hh) + mm_nt(gh, hl) + mm_nt(gl, hh)
        din_ref[k] = mm(along(qh, qlow), under(keys_out, keys_out)) + mm_nt(xh, dh) + mm_nt(xh, dl) + mm_nt(xl, dh)

        gt = gh.astype(f32) + gl.astype(f32)
        xt = xh.astype(f32) + xl.astype(f32)
        high, low = split2(under(gt * y, xt * dx))
        sums = mm_nt(gather, high) + mm_nt(gather, low)
        r_ref[k], c_ref[k] = sums[:ROWS, :CHUNK], sums[:ROWS, CHUNK:]
        gx_ref[k] = wide_ref[k] * dx + skip_wide * lay.columns(in_ref, k, width).astype(f32)
        return dl_ref[k] + through

    grouped(lay.chunks, backward, jnp.zeros((NSTATE, width), f32), reverse=True)


def scan_local(received, own, lay):
    gh, gl, xh, xl, hs, dl, wide, _, _, _, total, par, _, _ = own
    vmem = pl.BlockSpec(memory_space=pltpu.VMEM)
    shape = jax.ShapeDtypeStruct
    keys = (lay.chunks, CHUNK, NSTATE)
    return pl.pallas_call(
        lambda *refs: local_kernel(lay, *refs),
        in_specs=[vmem] * 10,
        out_specs=[vmem] * 5,
        out_shape=[shape(lay.wide, f32), shape(keys, f32), shape(keys, f32), shape(lay.cube, f32), shape(lay.cube, f32)],
        compiler_params=pltpu.CompilerParams(vmem_limit_bytes=LOCAL_VMEM * MIB),
        name="scan_local",
    )(received, gh, gl, xh, xl, hs, dl, wide, total, par)


def finish_kernel(lay, in_ref, gh_ref, gl_ref, xh_ref, xl_ref,
                  step_ref, slope_ref, decay_ref, total_ref, par_ref, skip_ref, sent_ref, came_ref,
                  r_ref, c_ref, flag_ref, dstep_ref, pout_ref, uh_ref, ul_ref, more_ref,
                  reach_ref, col_ref, row_ref):
    chunks, width, cube = lay.chunks, lay.width, lay.cube
    gather = lay.by_head()
    first = flag_ref[0] == 0

    run = jnp.ones(TILE, f32)
    before = []
    for k in range(chunks):
        before.append(run)
        run = run * total_ref[k]
    run = jnp.ones(TILE, f32)
    for k in reversed(range(chunks)):
        run = run * total_ref[k]
        reach_ref[k] = jnp.where(first, run, before[k])

    def correct(keys_at, high_ref, low_ref, old_ref, new_ref):
        def one(k, carry):
            uh, ul = split2(lay.to_lanes(reach_ref[k]) * came_ref[...])
            uh_ref[k], ul_ref[k] = uh, ul
            keys = in_ref[k, keys_at : keys_at + CHUNK]
            more = mm(along(keys, keys), under(uh, ul))
            more_ref[k] = more
            ph, plow = split2((high_ref[k].astype(f32) + low_ref[k].astype(f32)) * more)
            new_ref[k] = old_ref[k] + (mm_nt(gather, ph) + mm_nt(gather, plow))[:ROWS]
            return carry

        grouped(chunks, one, 0)

    @pl.when(first)
    def _():
        row_ref[...] = r_ref[...]
        correct(lay.at_b, xh_ref, xl_ref, c_ref, col_ref)

    @pl.when(jnp.logical_not(first))
    def _():
        col_ref[...] = c_ref[...]
        correct(lay.at_c, gh_ref, gl_ref, r_ref, row_ref)

    spread = lay.spread()
    per_head = lambda row: jnp.sum(spread * row, axis=1, keepdims=True)
    cross = per_head(jnp.sum(sent_ref[...] * came_ref[...], axis=0, keepdims=True))
    later = jnp.broadcast_to(jnp.where(first, cross, 0.0), TILE)
    col = col_ref[...]
    since = one_hot(iota(SQUARE, 0) >= iota(SQUARE, 1))
    suffix = mm_exact((row_ref[...] - col).reshape(lay.flat), since).reshape(cube)
    sums = jnp.broadcast_to(suffix[:, :, :1], cube)
    carried = [None] * chunks
    for k in reversed(range(chunks)):
        carried[k] = later[None]
        later = later + sums[k]
    d_decay = suffix + jnp.concatenate(carried, axis=0)
    rate = -jnp.exp(par_ref[0])
    d_raw = slope_ref[...] * (col / step_ref[...] + rate[None] * d_decay)
    dstep_ref[...] = jnp.concatenate([d_raw, jnp.zeros(cube, f32)], axis=1).astype(bf16)

    result = jnp.zeros(TILE, f32)
    per = (
        jnp.sum(jnp.sum(d_decay * decay_ref[...], axis=0), axis=1, keepdims=True),
        per_head(jnp.sum(skip_ref[...], axis=0, keepdims=True)),
        jnp.sum(jnp.sum(d_raw, axis=0), axis=1, keepdims=True),
    )
    for i, v in enumerate(per):
        row = jnp.sum(jnp.where(iota(TILE, 0) == iota(TILE, 1), jnp.broadcast_to(v, TILE), 0.0), axis=0, keepdims=True)
        result = jnp.where(iota(TILE, 0) == i, jnp.broadcast_to(row, TILE), result)
    pout_ref[...] = result


def scan_finish(received, own, r, c, came, flag, lay):
    gh, gl, xh, xl, _, _, _, step, slope, decay, total, par, skip, sent = own
    vmem = pl.BlockSpec(memory_space=pltpu.VMEM)
    shape = jax.ShapeDtypeStruct
    small = pltpu.VMEM(lay.cube, f32)
    return pl.pallas_call(
        lambda *refs: finish_kernel(lay, *refs),
        in_specs=[vmem] * 15 + [pl.BlockSpec(memory_space=pltpu.SMEM)],
        out_specs=[vmem] * 5,
        out_shape=[shape((lay.chunks, 16, LANES), bf16), shape(TILE, f32), shape(lay.wide, bf16), shape(lay.wide, bf16),
                   shape(lay.wide, f32)],
        scratch_shapes=[small, small, small],
        compiler_params=pltpu.CompilerParams(vmem_limit_bytes=FINISH_VMEM * MIB),
        name="scan_finish",
    )(received, gh, gl, xh, xl, step, slope, decay, total, par, skip, sent, came, r, c, flag)


def message_kernel(lay, gh_ref, gl_ref, xh_ref, xl_ref, wide_ref, gx_ref, din_ref, dout_ref,
                   dstep_ref, uh_ref, ul_ref, more_ref, flag_ref, out_hbm, out_ref, sem):
    width = lay.width
    first = flag_ref[0] == 0
    put = lambda k: pltpu.make_async_copy(out_ref.at[k], out_hbm.at[k], sem.at[k])

    def d_keys(k, high_ref, low_ref):
        high, low = high_ref[k], low_ref[k]
        return mm_nt(high, uh_ref[k]) + mm_nt(high, ul_ref[k]) + mm_nt(low, uh_ref[k])

    def store(k, grad_x, d_in, d_out):
        grad_x = grad_x.astype(bf16)
        for j in range(lay.blocks):
            out_ref[k, j * CHUNK : (j + 1) * CHUNK] = grad_x[:, j * LANES : (j + 1) * LANES]
        for j, part in enumerate(split2(d_in) + split2(d_out)):
            out_ref[k, width + j * CHUNK : width + (j + 1) * CHUNK] = part
        out_ref[k, lay.body :] = dstep_ref[k]
        put(k).start()

    @pl.when(first)
    def _():
        def one(k, carry):
            store(k, gx_ref[k] + wide_ref[k] * more_ref[k], din_ref[k] + d_keys(k, xh_ref, xl_ref), dout_ref[k])
            return carry

        grouped(lay.chunks, one, 0)

    @pl.when(jnp.logical_not(first))
    def _():
        def one(k, carry):
            store(k, gx_ref[k], din_ref[k], dout_ref[k] + d_keys(k, gh_ref, gl_ref))
            return carry

        grouped(lay.chunks, one, 0)

    for k in range(lay.chunks):
        put(k).wait()


def message(own, local, finish, flag, lay):
    gh, gl, xh, xl, _, _, wide, *_ = own
    dstep, _, uh, ul, more = finish
    vmem = pl.BlockSpec(memory_space=pltpu.VMEM)
    return pl.pallas_call(
        lambda *refs: message_kernel(lay, *refs),
        in_specs=[vmem] * 12 + [pl.BlockSpec(memory_space=pltpu.SMEM)],
        out_specs=pl.BlockSpec(memory_space=pl.ANY),
        out_shape=jax.ShapeDtypeStruct((lay.chunks, lay.body + 16, LANES), bf16),
        scratch_shapes=[
            pltpu.VMEM((lay.chunks, lay.body + 16, LANES), bf16),
            pltpu.SemaphoreType.DMA((lay.chunks,)),
        ],
        compiler_params=pltpu.CompilerParams(vmem_limit_bytes=FINISH_VMEM * MIB),
        cost_estimate=pl.CostEstimate(flops=400_000_000, bytes_accessed=20_000_000, transcendentals=0),
        name="message",
    )(gh, gl, xh, xl, wide, *local[:3], dstep, uh, ul, more, flag)


def unpack_kernel(lay, replicas, in_ref, sums_ref, flag_ref, x_ref, s_ref, b_ref, c_ref, p_ref):
    groups, width = in_ref.shape[0], lay.width
    narrow = width // HALVES
    some = lay.heads // HALVES
    for n in range(groups):
        for half in range(HALVES):
            for i in range(narrow // LANES):
                start = (half * groups + n) * narrow + i * LANES
                row = half * narrow + i * CHUNK
                x_ref[:, start : start + LANES] = in_ref[n, row : row + CHUNK]
    part = lambda n, j: in_ref[n, width + j * CHUNK : width + (j + 1) * CHUNK].astype(f32)
    every = range(groups)
    b_ref[...] = sum(part(n, 0) + part(n, 1) for n in every).astype(bf16)
    c_ref[...] = sum(part(n, 2) + part(n, 3) for n in every).astype(bf16)
    picks = [head_pick(16, s_ref.shape[0], n, some, groups) for n in every]
    s_ref[...] = sum(mm_tn(picks[n], in_ref[n, lay.body :]) for n in every).astype(bf16)
    mean = sums_ref[:3] / replicas
    p_ref[...] = jnp.where(flag_ref[0] == 0, mean[:, :some], mean[:, some : 2 * some])


def unpack(received, sums, flag, replicas, lay):
    groups = received.shape[0]
    shapes = [(CHUNK, groups * lay.width), (groups * lay.heads, CHUNK), (CHUNK, NSTATE), (CHUNK, NSTATE)]
    vmem = pl.BlockSpec(memory_space=pltpu.VMEM)
    return pl.pallas_call(
        lambda *refs: unpack_kernel(lay, replicas, *refs),
        in_specs=[vmem, vmem, pl.BlockSpec(memory_space=pltpu.SMEM)],
        out_specs=[vmem] * 5,
        out_shape=[jax.ShapeDtypeStruct(s, bf16) for s in shapes]
        + [jax.ShapeDtypeStruct((3, lay.heads // HALVES), f32)],
        compiler_params=pltpu.CompilerParams(vmem_limit_bytes=24 * MIB),
        name="unpack",
    )(received, sums, flag)


def exchange(v):
    groups = v.shape[0]
    halves = [[half * groups + i for i in range(groups)] for half in range(HALVES)]
    return lax.all_to_all(v, "seq", split_axis=0, concat_axis=0, tiled=True, axis_index_groups=halves)


def from_partner(v):
    groups = lax.axis_size("seq") // HALVES
    return lax.ppermute(v, "seq", [(i, (i + groups) % (2 * groups)) for i in range(2 * groups)])


def near_sum(v):
    replicas, shards = lax.axis_size("dp"), lax.axis_size("seq")
    v = v + from_partner(v)
    if replicas == 1:
        return v
    halves = lambda i: (i + shards // HALVES) % shards
    across = [(r * shards + i, (r ^ 1) * shards + halves(i)) for r in range(replicas) for i in range(shards)]
    return v + lax.ppermute(v, ("dp", "seq"), across)


def line_sum(v):
    half = lax.axis_size("dp") // 2
    if half <= 1:
        return v
    v = v + lax.ppermute(v, "dp", [(i, i ^ 2) for i in range(2 * half)])
    if half == 2:
        return v
    lines = [[2 * i + bit for i in range(odd, half, 2)] for odd in range(2) for bit in range(2)]
    return lax.psum(v, "dp", axis_index_groups=lines)


def shards(inputs, raw_step, write_keys, read_keys, grad_out, decay_log, skip_gain, step_bias):
    groups = lax.axis_size("seq") // HALVES
    some = decay_log.shape[0]
    lay = Layout(HALVES * some, groups)
    half = lax.axis_index("seq") // groups
    flag = half.astype(jnp.int32)[None]
    send = pack(inputs[0], grad_out[0], write_keys[0], read_keys[0], raw_step[0].T, groups)
    send, *mine = lax.optimization_barrier((send, decay_log, skip_gain, step_bias))
    mine = jnp.stack(mine)
    other = from_partner(mine)
    first = half == 0
    params = jnp.concatenate([jnp.where(first, mine, other), jnp.where(first, other, mine)], axis=1)
    params = jnp.pad(params, ((0, 0), (0, LANES - lay.heads)))

    received = exchange(send)
    own = scan_states(received, params, flag, lay)
    came = from_partner(own[-1])
    local = scan_local(received, own, lay)
    finish = scan_finish(received, own, local[3], local[4], came, flag, lay)
    back = message(own, local, finish, flag, lay)
    back, per_head = lax.optimization_barrier((back, near_sum(finish[1])))
    sums = line_sum(per_head)
    grad_x, grad_step, grad_write, grad_read, totals = unpack(exchange(back), sums, flag, lax.axis_size("dp"), lay)
    return grad_x[None], grad_step.T[None], grad_write[None], grad_read[None], totals


def solution(mesh):
    rows = P("dp", "seq", None)
    heads = P("seq")
    return jax.shard_map(
        shards,
        mesh=mesh,
        in_specs=(rows,) * 5 + (heads,) * 3,
        out_specs=(rows,) * 4 + (P(None, "seq"),),
        check_vma=False,
    )
```

```python
import jax
import jax.numpy as jnp
from jax import lax
from jax.experimental import pallas as pl
from jax.experimental.pallas import tpu as pltpu
from jax.sharding import PartitionSpec as P

CHUNK = 128
LANES = 128
HDIM = 64
NSTATE = 128
ROWS = 8
MIB = 1 << 20
PACK_STEPS = 2
HALVES = 2
PER_TILE = LANES // (2 * ROWS)
UNROLL = 8
STATES_VMEM = 24
LOCAL_VMEM = 24
FINISH_VMEM = 24

f32 = jnp.float32
bf16 = jnp.bfloat16


def mm(a, b):
    return jnp.dot(a, b, preferred_element_type=f32)


def mm_nt(a, b):
    return lax.dot_general(a, b, (((1,), (1,)), ((), ())), preferred_element_type=f32)


def mm_tn(a, b):
    return lax.dot_general(a, b, (((0,), (0,)), ((), ())), preferred_element_type=f32)


def split2(v):
    high = v.astype(bf16)
    return high, (v - high.astype(f32)).astype(bf16)


def split3(v):
    high = v.astype(bf16).astype(f32)
    rest = v - high
    mid = rest.astype(bf16).astype(f32)
    return high, mid, rest - mid


def iota(shape, axis):
    return lax.broadcasted_iota(jnp.int32, shape, axis)


def one_hot(cond):
    return jnp.where(cond, 1.0, 0.0)


def mm_exact(v, ones):
    parts = mm(jnp.concatenate(split3(v), axis=0).astype(bf16), ones.astype(bf16))
    n = v.shape[0]
    return parts[:n] + parts[n : 2 * n] + parts[2 * n :]


def pack_kernel(groups, xa_ref, xb_ref, ga_ref, gb_ref, b_ref, c_ref, s_ref, out_ref):
    some = s_ref.shape[0] // (HALVES * groups)
    narrow = some * HDIM
    width = HALVES * narrow
    tall = 2 * width + 2 * CHUNK
    for n in range(out_ref.shape[0]):
        row = 0
        for ref in (xa_ref, xb_ref, ga_ref, gb_ref):
            for i in range(narrow // LANES):
                start = n * narrow + i * LANES
                out_ref[n, row : row + CHUNK] = ref[:, start : start + LANES]
                row += CHUNK
        out_ref[n, 2 * width : 2 * width + CHUNK] = b_ref[...]
        out_ref[n, 2 * width + CHUNK : tall] = c_ref[...]
        group = pl.program_id(0) * out_ref.shape[0] + n
        out_ref[n, tall:] = mm(head_pick(16, s_ref.shape[0], group, some, groups), s_ref[...]).astype(bf16)


def head_pick(rows, heads, group, some, groups):
    shape = (rows, heads)
    row, head = iota(shape, 0), iota(shape, 1)
    owner = group + groups * (row // some)
    return one_hot((head == owner * some + row % some) & (row < HALVES * some)).astype(bf16)


def pack(x, g, b, c, s, groups):
    narrow = s.shape[0] // (HALVES * groups) * HDIM
    rows = 2 * HALVES * narrow + 2 * CHUNK + 16
    part = groups // PACK_STEPS
    whole = lambda a: pl.BlockSpec(a.shape, lambda j: (0, 0))
    first = pl.BlockSpec((CHUNK, part * narrow), lambda j: (0, j))
    second = pl.BlockSpec((CHUNK, part * narrow), lambda j: (0, PACK_STEPS + j))
    return pl.pallas_call(
        lambda *refs: pack_kernel(groups, *refs),
        grid=(PACK_STEPS,),
        in_specs=[first, second, first, second, whole(b), whole(c), whole(s)],
        out_specs=pl.BlockSpec((part, rows, LANES), lambda j: (j, 0, 0)),
        out_shape=jax.ShapeDtypeStruct((groups, rows, LANES), bf16),
        compiler_params=pltpu.CompilerParams(vmem_limit_bytes=56 * MIB),
        name="pack",
    )(x, x, g, g, b, c, s)


class Layout:
    def __init__(self, heads, chunks):
        self.heads, self.chunks, self.width = heads, chunks, heads * HDIM
        self.blocks = self.width // LANES
        self.at_b = 2 * self.width
        self.at_c = self.at_b + CHUNK
        self.at_s = self.at_c + CHUNK
        self.body = self.width + 4 * CHUNK
        self.flat = (chunks * ROWS, LANES)
        self.cube = (chunks, ROWS, LANES)
        self.wide = (chunks, CHUNK, self.width)

    def spread(self):
        shape = (ROWS, self.width)
        return one_hot(iota(shape, 1) // HDIM == iota(shape, 0))

    def to_lanes(self, tile):
        return jnp.sum(jnp.concatenate([tile] * self.blocks, axis=1) * self.spread(), axis=0, keepdims=True)

    def columns(self, ref, k, start):
        return jnp.concatenate(
            [ref[k, start + i * CHUNK : start + (i + 1) * CHUNK] for i in range(self.blocks)], axis=1
        )

    def keys(self, ref, k):
        return ref[k, self.at_b : self.at_b + CHUNK], ref[k, self.at_c : self.at_c + CHUNK]

    def by_head(self):
        shape = (16, self.width)
        return one_hot(iota(shape, 1) // HDIM == iota(shape, 0)).astype(bf16)


SQUARE = (LANES, LANES)
TILE = (ROWS, LANES)


def along(*parts):
    return jnp.concatenate(parts, axis=1)


def under(*parts):
    return jnp.concatenate(parts, axis=0)


def grouped(chunks, step, carry, reverse=False):
    def turn(i, carry):
        for n in range(UNROLL):
            k = i * UNROLL + n
            carry = step(chunks - 1 - k if reverse else k, carry)
        return carry

    return lax.fori_loop(0, chunks // UNROLL, turn, carry)


def states_kernel(lay, in_ref, given_ref, flag_ref,
                  gh_ref, gl_ref, xh_ref, xl_ref, hs_ref, dl_ref, wide_ref,
                  step_ref, slope_ref, decay_ref, total_ref, par_ref, skip_ref, send_ref,
                  alpha_ref, gamma_ref, pick_ref):
    chunks, width = lay.chunks, lay.width

    for i in range(3):
        row = jnp.broadcast_to(given_ref[i : i + 1], TILE)
        mine = jnp.where(iota(TILE, 1) == iota(TILE, 0), row, 0.0)
        par_ref[i] = jnp.broadcast_to(jnp.sum(mine, axis=1, keepdims=True), TILE)

    raw = in_ref[:, lay.at_s : lay.at_s + 16].astype(f32)[:, :ROWS]
    z = raw + par_ref[2][None]
    step = jnp.maximum(z, 0.0) + jnp.log1p(jnp.exp(-jnp.abs(z)))
    decay = -jnp.exp(par_ref[0])[None] * step
    step_ref[...], slope_ref[...], decay_ref[...] = step, jnp.exp(z - step), decay
    upto = one_hot(iota(SQUARE, 0) <= iota(SQUARE, 1))
    level = mm_exact(decay.reshape(lay.flat), upto)
    total_ref[...] = jnp.exp(jnp.broadcast_to(level[:, LANES - 1 :], lay.flat)).reshape(lay.cube)
    for ref, v in ((alpha_ref, jnp.exp(level)), (gamma_ref, jnp.exp(-level) * step.reshape(lay.flat))):
        high = v.astype(bf16).astype(f32)
        parts = jnp.concatenate([high.reshape(lay.cube), (v - high).reshape(lay.cube)], axis=1)
        parts = parts.reshape(chunks // PER_TILE, LANES, LANES)
        for i in range(chunks // PER_TILE):
            ref[i] = parts[i].T.astype(bf16)

    in_tile = (LANES, width)
    at_head = iota(in_tile, 1) // HDIM == iota(in_tile, 0) % ROWS
    eye = one_hot(iota(SQUARE, 0) == iota(SQUARE, 1)).astype(bf16)
    for i in range(PER_TILE):
        pick_ref[i] = one_hot(at_head & (iota(in_tile, 0) // (2 * ROWS) == i)).astype(bf16)

    def expand(ref, k):
        return mm(ref[k // PER_TILE], pick_ref[k % PER_TILE])

    def flip(v):
        return mm_nt(eye, v).astype(bf16)

    skip_ref[...] = jnp.zeros_like(skip_ref)

    def forward(k, carry):
        state, early, prefix = carry
        x = lay.columns(in_ref, k, 0).astype(f32)
        g = lay.columns(in_ref, k, width).astype(f32)
        gt_high, gt_low = split2(expand(alpha_ref, k) * g)
        wide = expand(gamma_ref, k)
        xt_high, xt_low = split2(wide * x)
        wide_ref[k] = wide
        gh_ref[k], gl_ref[k], xh_ref[k], xl_ref[k] = gt_high, gt_low, xt_high, xt_low
        skip_ref[...] += jnp.sum((x * g).reshape(CHUNK // ROWS, ROWS, width), axis=0)
        hs_ref[k] = state
        keys_in, keys_out = lay.keys(in_ref, k)
        keys_in, keys_out = flip(keys_in), flip(keys_out)
        back = mm(along(keys_out, keys_out), under(gt_high, gt_low))
        dl_ref[k] = back
        total = lay.to_lanes(total_ref[k])
        state = total * (state + mm(along(keys_in, keys_in), under(xt_high, xt_low)))
        return state, early + prefix * back, prefix * total

    nothing = jnp.zeros((NSTATE, width), f32)
    state, early, _ = grouped(chunks, forward, (nothing, nothing, jnp.ones((1, width), f32)))
    send_ref[...] = jnp.where(flag_ref[0] == 0, state, early)


def scan_states(received, params, flag, lay):
    vmem = pl.BlockSpec(memory_space=pltpu.VMEM)
    shape = jax.ShapeDtypeStruct
    wide, cube = lay.wide, lay.cube
    tiles = pltpu.VMEM((lay.chunks // PER_TILE, LANES, LANES), bf16)
    return pl.pallas_call(
        lambda *refs: states_kernel(lay, *refs),
        in_specs=[vmem, vmem, pl.BlockSpec(memory_space=pltpu.SMEM)],
        out_specs=[vmem] * 14,
        out_shape=[shape(wide, bf16)] * 4 + [shape(wide, f32)] * 3 + [shape(cube, f32)] * 4
        + [shape((3, ROWS, LANES), f32), shape((ROWS, lay.width), f32), shape((NSTATE, lay.width), f32)],
        scratch_shapes=[tiles, tiles, pltpu.VMEM((PER_TILE, LANES, lay.width), bf16)],
        compiler_params=pltpu.CompilerParams(vmem_limit_bytes=STATES_VMEM * MIB),
        name="scan_states",
    )(received, params, flag)


def local_kernel(lay, in_ref, gh_ref, gl_ref, xh_ref, xl_ref, hs_ref, dl_ref, wide_ref, total_ref, par_ref,
                 gx_ref, din_ref, dout_ref, r_ref, c_ref):
    width = lay.width
    gather = lay.by_head()
    skip_wide = lay.to_lanes(par_ref[1])
    causal = iota(SQUARE, 0) >= iota(SQUARE, 1)

    def backward(k, dstate):
        through = lay.to_lanes(total_ref[k]) * dstate
        dh, dl = split2(through)
        hh, hl = split2(hs_ref[k])
        gh, gl, xh, xl = gh_ref[k], gl_ref[k], xh_ref[k], xl_ref[k]
        keys_in, keys_out = lay.keys(in_ref, k)

        sh, sl = split2(jnp.where(causal, mm_nt(keys_out, keys_in), 0.0))
        th, tl = split2(jnp.where(causal.T, mm_nt(keys_in, keys_out), 0.0))
        out_h, in_h = along(sh, keys_out), along(th, keys_in)
        y = mm(out_h, under(xh, hh)) + mm(out_h, under(xl, hl)) + mm(sl, xh)
        dx = mm(in_h, under(gh, dh)) + mm(in_h, under(gl, dl)) + mm(tl, gh)

        ds = mm_nt(gh, xh) + mm_nt(gh, xl) + mm_nt(gl, xh)
        ds = jnp.where(causal, ds, 0.0)
        ph, plow = split2(ds)
        qh, qlow = split2(ds.T)
        dout_ref[k] = mm(along(ph, plow), under(keys_in, keys_in)) + mm_nt(gh, hh) + mm_nt(gh, hl) + mm_nt(gl, hh)
        din_ref[k] = mm(along(qh, qlow), under(keys_out, keys_out)) + mm_nt(xh, dh) + mm_nt(xh, dl) + mm_nt(xl, dh)

        gt = gh.astype(f32) + gl.astype(f32)
        xt = xh.astype(f32) + xl.astype(f32)
        high, low = split2(under(gt * y, xt * dx))
        sums = mm_nt(gather, high) + mm_nt(gather, low)
        r_ref[k], c_ref[k] = sums[:ROWS, :CHUNK], sums[:ROWS, CHUNK:]
        gx_ref[k] = wide_ref[k] * dx + skip_wide * lay.columns(in_ref, k, width).astype(f32)
        return dl_ref[k] + through

    grouped(lay.chunks, backward, jnp.zeros((NSTATE, width), f32), reverse=True)


def scan_local(received, own, lay):
    gh, gl, xh, xl, hs, dl, wide, _, _, _, total, par, _, _ = own
    vmem = pl.BlockSpec(memory_space=pltpu.VMEM)
    shape = jax.ShapeDtypeStruct
    keys = (lay.chunks, CHUNK, NSTATE)
    return pl.pallas_call(
        lambda *refs: local_kernel(lay, *refs),
        in_specs=[vmem] * 10,
        out_specs=[vmem] * 5,
        out_shape=[shape(lay.wide, f32), shape(keys, f32), shape(keys, f32), shape(lay.cube, f32), shape(lay.cube, f32)],
        compiler_params=pltpu.CompilerParams(vmem_limit_bytes=LOCAL_VMEM * MIB),
        name="scan_local",
    )(received, gh, gl, xh, xl, hs, dl, wide, total, par)


def finish_kernel(lay, in_ref, gh_ref, gl_ref, xh_ref, xl_ref,
                  step_ref, slope_ref, decay_ref, total_ref, par_ref, skip_ref, sent_ref, came_ref,
                  r_ref, c_ref, flag_ref, dstep_ref, pout_ref, uh_ref, ul_ref, more_ref,
                  reach_ref, col_ref, row_ref):
    chunks, width, cube = lay.chunks, lay.width, lay.cube
    gather = lay.by_head()
    first = flag_ref[0] == 0

    run = jnp.ones(TILE, f32)
    before = []
    for k in range(chunks):
        before.append(run)
        run = run * total_ref[k]
    run = jnp.ones(TILE, f32)
    for k in reversed(range(chunks)):
        run = run * total_ref[k]
        reach_ref[k] = jnp.where(first, run, before[k])

    def correct(keys_at, high_ref, low_ref, old_ref, new_ref):
        def one(k, carry):
            uh, ul = split2(lay.to_lanes(reach_ref[k]) * came_ref[...])
            uh_ref[k], ul_ref[k] = uh, ul
            keys = in_ref[k, keys_at : keys_at + CHUNK]
            more = mm(along(keys, keys), under(uh, ul))
            more_ref[k] = more
            ph, plow = split2((high_ref[k].astype(f32) + low_ref[k].astype(f32)) * more)
            new_ref[k] = old_ref[k] + (mm_nt(gather, ph) + mm_nt(gather, plow))[:ROWS]
            return carry

        grouped(chunks, one, 0)

    @pl.when(first)
    def _():
        row_ref[...] = r_ref[...]
        correct(lay.at_b, xh_ref, xl_ref, c_ref, col_ref)

    @pl.when(jnp.logical_not(first))
    def _():
        col_ref[...] = c_ref[...]
        correct(lay.at_c, gh_ref, gl_ref, r_ref, row_ref)

    spread = lay.spread()
    per_head = lambda row: jnp.sum(spread * row, axis=1, keepdims=True)
    cross = per_head(jnp.sum(sent_ref[...] * came_ref[...], axis=0, keepdims=True))
    later = jnp.broadcast_to(jnp.where(first, cross, 0.0), TILE)
    col = col_ref[...]
    since = one_hot(iota(SQUARE, 0) >= iota(SQUARE, 1))
    suffix = mm_exact((row_ref[...] - col).reshape(lay.flat), since).reshape(cube)
    sums = jnp.broadcast_to(suffix[:, :, :1], cube)
    carried = [None] * chunks
    for k in reversed(range(chunks)):
        carried[k] = later[None]
        later = later + sums[k]
    d_decay = suffix + jnp.concatenate(carried, axis=0)
    rate = -jnp.exp(par_ref[0])
    d_raw = slope_ref[...] * (col / step_ref[...] + rate[None] * d_decay)
    dstep_ref[...] = jnp.concatenate([d_raw, jnp.zeros(cube, f32)], axis=1).astype(bf16)

    result = jnp.zeros(TILE, f32)
    per = (
        jnp.sum(jnp.sum(d_decay * decay_ref[...], axis=0), axis=1, keepdims=True),
        per_head(jnp.sum(skip_ref[...], axis=0, keepdims=True)),
        jnp.sum(jnp.sum(d_raw, axis=0), axis=1, keepdims=True),
    )
    for i, v in enumerate(per):
        row = jnp.sum(jnp.where(iota(TILE, 0) == iota(TILE, 1), jnp.broadcast_to(v, TILE), 0.0), axis=0, keepdims=True)
        result = jnp.where(iota(TILE, 0) == i, jnp.broadcast_to(row, TILE), result)
    pout_ref[...] = result


def scan_finish(received, own, r, c, came, flag, lay):
    gh, gl, xh, xl, _, _, _, step, slope, decay, total, par, skip, sent = own
    vmem = pl.BlockSpec(memory_space=pltpu.VMEM)
    shape = jax.ShapeDtypeStruct
    small = pltpu.VMEM(lay.cube, f32)
    return pl.pallas_call(
        lambda *refs: finish_kernel(lay, *refs),
        in_specs=[vmem] * 15 + [pl.BlockSpec(memory_space=pltpu.SMEM)],
        out_specs=[vmem] * 5,
        out_shape=[shape((lay.chunks, 16, LANES), bf16), shape(TILE, f32), shape(lay.wide, bf16), shape(lay.wide, bf16),
                   shape(lay.wide, f32)],
        scratch_shapes=[small, small, small],
        compiler_params=pltpu.CompilerParams(vmem_limit_bytes=FINISH_VMEM * MIB),
        name="scan_finish",
    )(received, gh, gl, xh, xl, step, slope, decay, total, par, skip, sent, came, r, c, flag)


def message_kernel(lay, gh_ref, gl_ref, xh_ref, xl_ref, wide_ref, gx_ref, din_ref, dout_ref,
                   dstep_ref, uh_ref, ul_ref, more_ref, flag_ref, out_hbm, out_ref, sem):
    width = lay.width
    first = flag_ref[0] == 0
    put = lambda k: pltpu.make_async_copy(out_ref.at[k], out_hbm.at[k], sem.at[k])

    def d_keys(k, high_ref, low_ref):
        high, low = high_ref[k], low_ref[k]
        return mm_nt(high, uh_ref[k]) + mm_nt(high, ul_ref[k]) + mm_nt(low, uh_ref[k])

    def store(k, grad_x, d_in, d_out):
        grad_x = grad_x.astype(bf16)
        for j in range(lay.blocks):
            out_ref[k, j * CHUNK : (j + 1) * CHUNK] = grad_x[:, j * LANES : (j + 1) * LANES]
        for j, part in enumerate(split2(d_in) + split2(d_out)):
            out_ref[k, width + j * CHUNK : width + (j + 1) * CHUNK] = part
        out_ref[k, lay.body :] = dstep_ref[k]
        put(k).start()

    @pl.when(first)
    def _():
        def one(k, carry):
            store(k, gx_ref[k] + wide_ref[k] * more_ref[k], din_ref[k] + d_keys(k, xh_ref, xl_ref), dout_ref[k])
            return carry

        grouped(lay.chunks, one, 0)

    @pl.when(jnp.logical_not(first))
    def _():
        def one(k, carry):
            store(k, gx_ref[k], din_ref[k], dout_ref[k] + d_keys(k, gh_ref, gl_ref))
            return carry

        grouped(lay.chunks, one, 0)

    for k in range(lay.chunks):
        put(k).wait()


def message(own, local, finish, flag, lay):
    gh, gl, xh, xl, _, _, wide, *_ = own
    dstep, _, uh, ul, more = finish
    vmem = pl.BlockSpec(memory_space=pltpu.VMEM)
    return pl.pallas_call(
        lambda *refs: message_kernel(lay, *refs),
        in_specs=[vmem] * 12 + [pl.BlockSpec(memory_space=pltpu.SMEM)],
        out_specs=pl.BlockSpec(memory_space=pl.ANY),
        out_shape=jax.ShapeDtypeStruct((lay.chunks, lay.body + 16, LANES), bf16),
        scratch_shapes=[
            pltpu.VMEM((lay.chunks, lay.body + 16, LANES), bf16),
            pltpu.SemaphoreType.DMA((lay.chunks,)),
        ],
        compiler_params=pltpu.CompilerParams(vmem_limit_bytes=FINISH_VMEM * MIB),
        cost_estimate=pl.CostEstimate(flops=400_000_000, bytes_accessed=20_000_000, transcendentals=0),
        name="message",
    )(gh, gl, xh, xl, wide, *local[:3], dstep, uh, ul, more, flag)


def unpack_kernel(lay, replicas, in_ref, sums_ref, flag_ref, x_ref, s_ref, b_ref, c_ref, p_ref):
    groups, width = in_ref.shape[0], lay.width
    narrow = width // HALVES
    some = lay.heads // HALVES
    for n in range(groups):
        for half in range(HALVES):
            for i in range(narrow // LANES):
                start = (half * groups + n) * narrow + i * LANES
                row = half * narrow + i * CHUNK
                x_ref[:, start : start + LANES] = in_ref[n, row : row + CHUNK]
    part = lambda n, j: in_ref[n, width + j * CHUNK : width + (j + 1) * CHUNK].astype(f32)
    every = range(groups)
    b_ref[...] = sum(part(n, 0) + part(n, 1) for n in every).astype(bf16)
    c_ref[...] = sum(part(n, 2) + part(n, 3) for n in every).astype(bf16)
    picks = [head_pick(16, s_ref.shape[0], n, some, groups) for n in every]
    s_ref[...] = sum(mm_tn(picks[n], in_ref[n, lay.body :]) for n in every).astype(bf16)
    mean = sums_ref[:3] / replicas
    p_ref[...] = jnp.where(flag_ref[0] == 0, mean[:, :some], mean[:, some : 2 * some])


def unpack(received, sums, flag, replicas, lay):
    groups = received.shape[0]
    shapes = [(CHUNK, groups * lay.width), (groups * lay.heads, CHUNK), (CHUNK, NSTATE), (CHUNK, NSTATE)]
    vmem = pl.BlockSpec(memory_space=pltpu.VMEM)
    return pl.pallas_call(
        lambda *refs: unpack_kernel(lay, replicas, *refs),
        in_specs=[vmem, vmem, pl.BlockSpec(memory_space=pltpu.SMEM)],
        out_specs=[vmem] * 5,
        out_shape=[jax.ShapeDtypeStruct(s, bf16) for s in shapes]
        + [jax.ShapeDtypeStruct((3, lay.heads // HALVES), f32)],
        compiler_params=pltpu.CompilerParams(vmem_limit_bytes=24 * MIB),
        name="unpack",
    )(received, sums, flag)


def exchange(v):
    groups = v.shape[0]
    halves = [[half * groups + i for i in range(groups)] for half in range(HALVES)]
    return lax.all_to_all(v, "seq", split_axis=0, concat_axis=0, tiled=True, axis_index_groups=halves)


def from_partner(v):
    groups = lax.axis_size("seq") // HALVES
    return lax.ppermute(v, "seq", [(i, (i + groups) % (2 * groups)) for i in range(2 * groups)])


def across_sum(v):
    replicas, shards = lax.axis_size("dp"), lax.axis_size("seq")
    if replicas == 1:
        return v
    halves = lambda i: (i + shards // HALVES) % shards
    across = [(r * shards + i, (r ^ 1) * shards + halves(i)) for r in range(replicas) for i in range(shards)]
    return v + lax.ppermute(v, ("dp", "seq"), across)


def line_sum(v):
    half = lax.axis_size("dp") // 2
    if half <= 1:
        return v
    v = v + lax.ppermute(v, "dp", [(i, i ^ 2) for i in range(2 * half)])
    if half == 2:
        return v
    lines = [[2 * i + bit for i in range(odd, half, 2)] for odd in range(2) for bit in range(2)]
    return lax.psum(v, "dp", axis_index_groups=lines)


def shards(inputs, raw_step, write_keys, read_keys, grad_out, decay_log, skip_gain, step_bias):
    groups = lax.axis_size("seq") // HALVES
    some = decay_log.shape[0]
    lay = Layout(HALVES * some, groups)
    half = lax.axis_index("seq") // groups
    flag = half.astype(jnp.int32)[None]
    send = pack(inputs[0], grad_out[0], write_keys[0], read_keys[0], raw_step[0].T, groups)
    send, *mine = lax.optimization_barrier((send, decay_log, skip_gain, step_bias))
    mine = jnp.stack(mine)
    other = from_partner(mine)
    first = half == 0
    params = jnp.concatenate([jnp.where(first, mine, other), jnp.where(first, other, mine)], axis=1)
    params = jnp.pad(params, ((0, 0), (0, LANES - lay.heads)))

    received = exchange(send)
    own = scan_states(received, params, flag, lay)
    came = from_partner(own[-1])
    local = scan_local(received, own, lay)
    finish = scan_finish(received, own, local[3], local[4], came, flag, lay)
    back = message(own, local, finish, flag, lay)
    per_head = finish[1] + from_partner(finish[1])
    back, per_head = lax.optimization_barrier((back, per_head))
    sums = line_sum(across_sum(per_head))
    grad_x, grad_step, grad_write, grad_read, totals = unpack(exchange(back), sums, flag, lax.axis_size("dp"), lay)
    return grad_x[None], grad_step.T[None], grad_write[None], grad_read[None], totals


def solution(mesh):
    rows = P("dp", "seq", None)
    heads = P("seq")
    return jax.shard_map(
        shards,
        mesh=mesh,
        in_specs=(rows,) * 5 + (heads,) * 3,
        out_specs=(rows,) * 4 + (P(None, "seq"),),
        check_vma=False,
    )
```

```python
import jax
import jax.numpy as jnp
from jax import lax
from jax.experimental import pallas as pl
from jax.experimental.pallas import tpu as pltpu
from jax.sharding import PartitionSpec as P

CHUNK = 128
LANES = 128
HDIM = 64
NSTATE = 128
ROWS = 8
MIB = 1 << 20
PACK_STEPS = 2
HALVES = 2
PER_TILE = LANES // (2 * ROWS)
UNROLL = 8
STATES_VMEM = 24
LOCAL_VMEM = 24
FINISH_VMEM = 24

f32 = jnp.float32
bf16 = jnp.bfloat16


def mm(a, b):
    return jnp.dot(a, b, preferred_element_type=f32)


def mm_nt(a, b):
    return lax.dot_general(a, b, (((1,), (1,)), ((), ())), preferred_element_type=f32)


def mm_tn(a, b):
    return lax.dot_general(a, b, (((0,), (0,)), ((), ())), preferred_element_type=f32)


def split2(v):
    high = v.astype(bf16)
    return high, (v - high.astype(f32)).astype(bf16)


def split3(v):
    high = v.astype(bf16).astype(f32)
    rest = v - high
    mid = rest.astype(bf16).astype(f32)
    return high, mid, rest - mid


def iota(shape, axis):
    return lax.broadcasted_iota(jnp.int32, shape, axis)


def one_hot(cond):
    return jnp.where(cond, 1.0, 0.0)


def mm_exact(v, ones):
    parts = mm(jnp.concatenate(split3(v), axis=0).astype(bf16), ones.astype(bf16))
    n = v.shape[0]
    return parts[:n] + parts[n : 2 * n] + parts[2 * n :]


def pack_kernel(groups, xa_ref, xb_ref, ga_ref, gb_ref, b_ref, c_ref, s_ref, out_ref):
    some = s_ref.shape[0] // (HALVES * groups)
    narrow = some * HDIM
    width = HALVES * narrow
    tall = 2 * width + 2 * CHUNK
    for n in range(out_ref.shape[0]):
        row = 0
        for ref in (xa_ref, xb_ref, ga_ref, gb_ref):
            for i in range(narrow // LANES):
                start = n * narrow + i * LANES
                out_ref[n, row : row + CHUNK] = ref[:, start : start + LANES]
                row += CHUNK
        out_ref[n, 2 * width : 2 * width + CHUNK] = b_ref[...]
        out_ref[n, 2 * width + CHUNK : tall] = c_ref[...]
        group = pl.program_id(0) * out_ref.shape[0] + n
        out_ref[n, tall:] = mm(head_pick(16, s_ref.shape[0], group, some, groups), s_ref[...]).astype(bf16)


def head_pick(rows, heads, group, some, groups):
    shape = (rows, heads)
    row, head = iota(shape, 0), iota(shape, 1)
    owner = group + groups * (row // some)
    return one_hot((head == owner * some + row % some) & (row < HALVES * some)).astype(bf16)


def pack(x, g, b, c, s, groups):
    narrow = s.shape[0] // (HALVES * groups) * HDIM
    rows = 2 * HALVES * narrow + 2 * CHUNK + 16
    part = groups // PACK_STEPS
    whole = lambda a: pl.BlockSpec(a.shape, lambda j: (0, 0))
    first = pl.BlockSpec((CHUNK, part * narrow), lambda j: (0, j))
    second = pl.BlockSpec((CHUNK, part * narrow), lambda j: (0, PACK_STEPS + j))
    return pl.pallas_call(
        lambda *refs: pack_kernel(groups, *refs),
        grid=(PACK_STEPS,),
        in_specs=[first, second, first, second, whole(b), whole(c), whole(s)],
        out_specs=pl.BlockSpec((part, rows, LANES), lambda j: (j, 0, 0)),
        out_shape=jax.ShapeDtypeStruct((groups, rows, LANES), bf16),
        compiler_params=pltpu.CompilerParams(vmem_limit_bytes=56 * MIB),
        name="pack",
    )(x, x, g, g, b, c, s)


class Layout:
    def __init__(self, heads, chunks):
        self.heads, self.chunks, self.width = heads, chunks, heads * HDIM
        self.blocks = self.width // LANES
        self.at_b = 2 * self.width
        self.at_c = self.at_b + CHUNK
        self.at_s = self.at_c + CHUNK
        self.body = self.width + 4 * CHUNK
        self.flat = (chunks * ROWS, LANES)
        self.cube = (chunks, ROWS, LANES)
        self.wide = (chunks, CHUNK, self.width)

    def spread(self):
        shape = (ROWS, self.width)
        return one_hot(iota(shape, 1) // HDIM == iota(shape, 0))

    def to_lanes(self, tile):
        return jnp.sum(jnp.concatenate([tile] * self.blocks, axis=1) * self.spread(), axis=0, keepdims=True)

    def columns(self, ref, k, start):
        return jnp.concatenate(
            [ref[k, start + i * CHUNK : start + (i + 1) * CHUNK] for i in range(self.blocks)], axis=1
        )

    def keys(self, ref, k):
        return ref[k, self.at_b : self.at_b + CHUNK], ref[k, self.at_c : self.at_c + CHUNK]

    def by_head(self):
        shape = (16, self.width)
        return one_hot(iota(shape, 1) // HDIM == iota(shape, 0)).astype(bf16)


SQUARE = (LANES, LANES)
TILE = (ROWS, LANES)


def along(*parts):
    return jnp.concatenate(parts, axis=1)


def under(*parts):
    return jnp.concatenate(parts, axis=0)


def grouped(chunks, step, carry, reverse=False):
    def turn(i, carry):
        for n in range(UNROLL):
            k = i * UNROLL + n
            carry = step(chunks - 1 - k if reverse else k, carry)
        return carry

    return lax.fori_loop(0, chunks // UNROLL, turn, carry)


def states_kernel(lay, in_ref, given_ref, flag_ref,
                  gh_ref, gl_ref, xh_ref, xl_ref, hs_ref, dl_ref, wide_ref,
                  step_ref, slope_ref, decay_ref, total_ref, par_ref, skip_ref, send_ref,
                  alpha_ref, gamma_ref, pick_ref):
    chunks, width = lay.chunks, lay.width

    for i in range(3):
        row = jnp.broadcast_to(given_ref[i : i + 1], TILE)
        mine = jnp.where(iota(TILE, 1) == iota(TILE, 0), row, 0.0)
        par_ref[i] = jnp.broadcast_to(jnp.sum(mine, axis=1, keepdims=True), TILE)

    raw = in_ref[:, lay.at_s : lay.at_s + 16].astype(f32)[:, :ROWS]
    z = raw + par_ref[2][None]
    step = jnp.maximum(z, 0.0) + jnp.log1p(jnp.exp(-jnp.abs(z)))
    decay = -jnp.exp(par_ref[0])[None] * step
    step_ref[...], slope_ref[...], decay_ref[...] = step, jnp.exp(z - step), decay
    upto = one_hot(iota(SQUARE, 0) <= iota(SQUARE, 1))
    level = mm_exact(decay.reshape(lay.flat), upto)
    total_ref[...] = jnp.exp(jnp.broadcast_to(level[:, LANES - 1 :], lay.flat)).reshape(lay.cube)
    for ref, v in ((alpha_ref, jnp.exp(level)), (gamma_ref, jnp.exp(-level) * step.reshape(lay.flat))):
        high = v.astype(bf16).astype(f32)
        parts = jnp.concatenate([high.reshape(lay.cube), (v - high).reshape(lay.cube)], axis=1)
        parts = parts.reshape(chunks // PER_TILE, LANES, LANES)
        for i in range(chunks // PER_TILE):
            ref[i] = parts[i].T.astype(bf16)

    in_tile = (LANES, width)
    at_head = iota(in_tile, 1) // HDIM == iota(in_tile, 0) % ROWS
    eye = one_hot(iota(SQUARE, 0) == iota(SQUARE, 1)).astype(bf16)
    for i in range(PER_TILE):
        pick_ref[i] = one_hot(at_head & (iota(in_tile, 0) // (2 * ROWS) == i)).astype(bf16)

    def expand(ref, k):
        return mm(ref[k // PER_TILE], pick_ref[k % PER_TILE])

    def flip(v):
        return mm_nt(eye, v).astype(bf16)

    skip_ref[...] = jnp.zeros_like(skip_ref)

    def forward(k, carry):
        state, early, prefix = carry
        x = lay.columns(in_ref, k, 0).astype(f32)
        g = lay.columns(in_ref, k, width).astype(f32)
        gt_high, gt_low = split2(expand(alpha_ref, k) * g)
        wide = expand(gamma_ref, k)
        xt_high, xt_low = split2(wide * x)
        wide_ref[k] = wide
        gh_ref[k], gl_ref[k], xh_ref[k], xl_ref[k] = gt_high, gt_low, xt_high, xt_low
        skip_ref[...] += jnp.sum((x * g).reshape(CHUNK // ROWS, ROWS, width), axis=0)
        hs_ref[k] = state
        keys_in, keys_out = lay.keys(in_ref, k)
        keys_in, keys_out = flip(keys_in), flip(keys_out)
        back = mm(along(keys_out, keys_out), under(gt_high, gt_low))
        dl_ref[k] = back
        total = lay.to_lanes(total_ref[k])
        state = total * (state + mm(along(keys_in, keys_in), under(xt_high, xt_low)))
        return state, early + prefix * back, prefix * total

    nothing = jnp.zeros((NSTATE, width), f32)
    state, early, _ = grouped(chunks, forward, (nothing, nothing, jnp.ones((1, width), f32)))
    send_ref[...] = jnp.where(flag_ref[0] == 0, state, early)


def scan_states(received, params, flag, lay):
    vmem = pl.BlockSpec(memory_space=pltpu.VMEM)
    shape = jax.ShapeDtypeStruct
    wide, cube = lay.wide, lay.cube
    tiles = pltpu.VMEM((lay.chunks // PER_TILE, LANES, LANES), bf16)
    return pl.pallas_call(
        lambda *refs: states_kernel(lay, *refs),
        in_specs=[vmem, vmem, pl.BlockSpec(memory_space=pltpu.SMEM)],
        out_specs=[vmem] * 14,
        out_shape=[shape(wide, bf16)] * 4 + [shape(wide, f32)] * 3 + [shape(cube, f32)] * 4
        + [shape((3, ROWS, LANES), f32), shape((ROWS, lay.width), f32), shape((NSTATE, lay.width), f32)],
        scratch_shapes=[tiles, tiles, pltpu.VMEM((PER_TILE, LANES, lay.width), bf16)],
        compiler_params=pltpu.CompilerParams(vmem_limit_bytes=STATES_VMEM * MIB),
        name="scan_states",
    )(received, params, flag)


def local_kernel(lay, in_ref, gh_ref, gl_ref, xh_ref, xl_ref, hs_ref, dl_ref, wide_ref, total_ref, par_ref,
                 gx_ref, din_ref, dout_ref, r_ref, c_ref):
    width = lay.width
    gather = lay.by_head()
    skip_wide = lay.to_lanes(par_ref[1])
    causal = iota(SQUARE, 0) >= iota(SQUARE, 1)

    def backward(k, dstate):
        through = lay.to_lanes(total_ref[k]) * dstate
        dh, dl = split2(through)
        hh, hl = split2(hs_ref[k])
        gh, gl, xh, xl = gh_ref[k], gl_ref[k], xh_ref[k], xl_ref[k]
        keys_in, keys_out = lay.keys(in_ref, k)

        sh, sl = split2(jnp.where(causal, mm_nt(keys_out, keys_in), 0.0))
        th, tl = split2(jnp.where(causal.T, mm_nt(keys_in, keys_out), 0.0))
        out_h, in_h = along(sh, keys_out), along(th, keys_in)
        y = mm(out_h, under(xh, hh)) + mm(out_h, under(xl, hl)) + mm(sl, xh)
        dx = mm(in_h, under(gh, dh)) + mm(in_h, under(gl, dl)) + mm(tl, gh)

        ds = mm_nt(gh, xh) + mm_nt(gh, xl) + mm_nt(gl, xh)
        ds = jnp.where(causal, ds, 0.0)
        ph, plow = split2(ds)
        qh, qlow = split2(ds.T)
        dout_ref[k] = mm(along(ph, plow), under(keys_in, keys_in)) + mm_nt(gh, hh) + mm_nt(gh, hl) + mm_nt(gl, hh)
        din_ref[k] = mm(along(qh, qlow), under(keys_out, keys_out)) + mm_nt(xh, dh) + mm_nt(xh, dl) + mm_nt(xl, dh)

        gt = gh.astype(f32) + gl.astype(f32)
        xt = xh.astype(f32) + xl.astype(f32)
        high, low = split2(under(gt * y, xt * dx))
        sums = mm_nt(gather, high) + mm_nt(gather, low)
        r_ref[k], c_ref[k] = sums[:ROWS, :CHUNK], sums[:ROWS, CHUNK:]
        gx_ref[k] = wide_ref[k] * dx + skip_wide * lay.columns(in_ref, k, width).astype(f32)
        return dl_ref[k] + through

    grouped(lay.chunks, backward, jnp.zeros((NSTATE, width), f32), reverse=True)


def scan_local(received, own, lay):
    gh, gl, xh, xl, hs, dl, wide, _, _, _, total, par, _, _ = own
    vmem = pl.BlockSpec(memory_space=pltpu.VMEM)
    shape = jax.ShapeDtypeStruct
    keys = (lay.chunks, CHUNK, NSTATE)
    return pl.pallas_call(
        lambda *refs: local_kernel(lay, *refs),
        in_specs=[vmem] * 10,
        out_specs=[vmem] * 5,
        out_shape=[shape(lay.wide, f32), shape(keys, f32), shape(keys, f32), shape(lay.cube, f32), shape(lay.cube, f32)],
        compiler_params=pltpu.CompilerParams(vmem_limit_bytes=LOCAL_VMEM * MIB),
        name="scan_local",
    )(received, gh, gl, xh, xl, hs, dl, wide, total, par)


def finish_kernel(lay, in_ref, gh_ref, gl_ref, xh_ref, xl_ref,
                  step_ref, slope_ref, decay_ref, total_ref, par_ref, skip_ref, sent_ref, came_ref,
                  r_ref, c_ref, flag_ref, dstep_ref, pout_ref, uh_ref, ul_ref, more_ref,
                  reach_ref, col_ref, row_ref):
    chunks, width, cube = lay.chunks, lay.width, lay.cube
    gather = lay.by_head()
    first = flag_ref[0] == 0

    run = jnp.ones(TILE, f32)
    before = []
    for k in range(chunks):
        before.append(run)
        run = run * total_ref[k]
    run = jnp.ones(TILE, f32)
    for k in reversed(range(chunks)):
        run = run * total_ref[k]
        reach_ref[k] = jnp.where(first, run, before[k])

    def correct(keys_at, high_ref, low_ref, old_ref, new_ref):
        def one(k, carry):
            uh, ul = split2(lay.to_lanes(reach_ref[k]) * came_ref[...])
            uh_ref[k], ul_ref[k] = uh, ul
            keys = in_ref[k, keys_at : keys_at + CHUNK]
            more = mm(along(keys, keys), under(uh, ul))
            more_ref[k] = more
            ph, plow = split2((high_ref[k].astype(f32) + low_ref[k].astype(f32)) * more)
            new_ref[k] = old_ref[k] + (mm_nt(gather, ph) + mm_nt(gather, plow))[:ROWS]
            return carry

        grouped(chunks, one, 0)

    @pl.when(first)
    def _():
        row_ref[...] = r_ref[...]
        correct(lay.at_b, xh_ref, xl_ref, c_ref, col_ref)

    @pl.when(jnp.logical_not(first))
    def _():
        col_ref[...] = c_ref[...]
        correct(lay.at_c, gh_ref, gl_ref, r_ref, row_ref)

    spread = lay.spread()
    per_head = lambda row: jnp.sum(spread * row, axis=1, keepdims=True)
    cross = per_head(jnp.sum(sent_ref[...] * came_ref[...], axis=0, keepdims=True))
    later = jnp.broadcast_to(jnp.where(first, cross, 0.0), TILE)
    col = col_ref[...]
    since = one_hot(iota(SQUARE, 0) >= iota(SQUARE, 1))
    suffix = mm_exact((row_ref[...] - col).reshape(lay.flat), since).reshape(cube)
    sums = jnp.broadcast_to(suffix[:, :, :1], cube)
    carried = [None] * chunks
    for k in reversed(range(chunks)):
        carried[k] = later[None]
        later = later + sums[k]
    d_decay = suffix + jnp.concatenate(carried, axis=0)
    rate = -jnp.exp(par_ref[0])
    d_raw = slope_ref[...] * (col / step_ref[...] + rate[None] * d_decay)
    dstep_ref[...] = jnp.concatenate([d_raw, jnp.zeros(cube, f32)], axis=1).astype(bf16)

    result = jnp.zeros(TILE, f32)
    per = (
        jnp.sum(jnp.sum(d_decay * decay_ref[...], axis=0), axis=1, keepdims=True),
        per_head(jnp.sum(skip_ref[...], axis=0, keepdims=True)),
        jnp.sum(jnp.sum(d_raw, axis=0), axis=1, keepdims=True),
    )
    for i, v in enumerate(per):
        row = jnp.sum(jnp.where(iota(TILE, 0) == iota(TILE, 1), jnp.broadcast_to(v, TILE), 0.0), axis=0, keepdims=True)
        result = jnp.where(iota(TILE, 0) == i, jnp.broadcast_to(row, TILE), result)
    pout_ref[...] = result


def scan_finish(received, own, r, c, came, flag, lay):
    gh, gl, xh, xl, _, _, _, step, slope, decay, total, par, skip, sent = own
    vmem = pl.BlockSpec(memory_space=pltpu.VMEM)
    shape = jax.ShapeDtypeStruct
    small = pltpu.VMEM(lay.cube, f32)
    return pl.pallas_call(
        lambda *refs: finish_kernel(lay, *refs),
        in_specs=[vmem] * 15 + [pl.BlockSpec(memory_space=pltpu.SMEM)],
        out_specs=[vmem] * 5,
        out_shape=[shape((lay.chunks, 16, LANES), bf16), shape(TILE, f32), shape(lay.wide, bf16), shape(lay.wide, bf16),
                   shape(lay.wide, f32)],
        scratch_shapes=[small, small, small],
        compiler_params=pltpu.CompilerParams(vmem_limit_bytes=FINISH_VMEM * MIB),
        name="scan_finish",
    )(received, gh, gl, xh, xl, step, slope, decay, total, par, skip, sent, came, r, c, flag)


def message_kernel(lay, gh_ref, gl_ref, xh_ref, xl_ref, wide_ref, gx_ref, din_ref, dout_ref,
                   dstep_ref, uh_ref, ul_ref, more_ref, flag_ref, out_hbm, out_ref, sem):
    width = lay.width
    first = flag_ref[0] == 0
    put = lambda k: pltpu.make_async_copy(out_ref.at[k], out_hbm.at[k], sem.at[k])

    def d_keys(k, high_ref, low_ref):
        high, low = high_ref[k], low_ref[k]
        return mm_nt(high, uh_ref[k]) + mm_nt(high, ul_ref[k]) + mm_nt(low, uh_ref[k])

    def store(k, grad_x, d_in, d_out):
        grad_x = grad_x.astype(bf16)
        for j in range(lay.blocks):
            out_ref[k, j * CHUNK : (j + 1) * CHUNK] = grad_x[:, j * LANES : (j + 1) * LANES]
        for j, part in enumerate(split2(d_in) + split2(d_out)):
            out_ref[k, width + j * CHUNK : width + (j + 1) * CHUNK] = part
        out_ref[k, lay.body :] = dstep_ref[k]
        put(k).start()

    @pl.when(first)
    def _():
        def one(k, carry):
            store(k, gx_ref[k] + wide_ref[k] * more_ref[k], din_ref[k] + d_keys(k, xh_ref, xl_ref), dout_ref[k])
            return carry

        grouped(lay.chunks, one, 0)

    @pl.when(jnp.logical_not(first))
    def _():
        def one(k, carry):
            store(k, gx_ref[k], din_ref[k], dout_ref[k] + d_keys(k, gh_ref, gl_ref))
            return carry

        grouped(lay.chunks, one, 0)

    for k in range(lay.chunks):
        put(k).wait()


def message(own, local, finish, flag, lay):
    gh, gl, xh, xl, _, _, wide, *_ = own
    dstep, _, uh, ul, more = finish
    vmem = pl.BlockSpec(memory_space=pltpu.VMEM)
    return pl.pallas_call(
        lambda *refs: message_kernel(lay, *refs),
        in_specs=[vmem] * 12 + [pl.BlockSpec(memory_space=pltpu.SMEM)],
        out_specs=pl.BlockSpec(memory_space=pl.ANY),
        out_shape=jax.ShapeDtypeStruct((lay.chunks, lay.body + 16, LANES), bf16),
        scratch_shapes=[
            pltpu.VMEM((lay.chunks, lay.body + 16, LANES), bf16),
            pltpu.SemaphoreType.DMA((lay.chunks,)),
        ],
        compiler_params=pltpu.CompilerParams(vmem_limit_bytes=FINISH_VMEM * MIB),
        cost_estimate=pl.CostEstimate(flops=400_000_000, bytes_accessed=20_000_000, transcendentals=0),
        name="message",
    )(gh, gl, xh, xl, wide, *local[:3], dstep, uh, ul, more, flag)


def unpack_kernel(lay, replicas, in_ref, sums_ref, flag_ref, x_ref, s_ref, b_ref, c_ref, p_ref):
    groups, width = in_ref.shape[0], lay.width
    narrow = width // HALVES
    some = lay.heads // HALVES
    for n in range(groups):
        for half in range(HALVES):
            for i in range(narrow // LANES):
                start = (half * groups + n) * narrow + i * LANES
                row = half * narrow + i * CHUNK
                x_ref[:, start : start + LANES] = in_ref[n, row : row + CHUNK]
    part = lambda n, j: in_ref[n, width + j * CHUNK : width + (j + 1) * CHUNK].astype(f32)
    every = range(groups)
    b_ref[...] = sum(part(n, 0) + part(n, 1) for n in every).astype(bf16)
    c_ref[...] = sum(part(n, 2) + part(n, 3) for n in every).astype(bf16)
    picks = [head_pick(16, s_ref.shape[0], n, some, groups) for n in every]
    s_ref[...] = sum(mm_tn(picks[n], in_ref[n, lay.body :]) for n in every).astype(bf16)
    mean = sums_ref[:3] / replicas
    p_ref[...] = jnp.where(flag_ref[0] == 0, mean[:, :some], mean[:, some : 2 * some])


def unpack(received, sums, flag, replicas, lay):
    groups = received.shape[0]
    shapes = [(CHUNK, groups * lay.width), (groups * lay.heads, CHUNK), (CHUNK, NSTATE), (CHUNK, NSTATE)]
    vmem = pl.BlockSpec(memory_space=pltpu.VMEM)
    return pl.pallas_call(
        lambda *refs: unpack_kernel(lay, replicas, *refs),
        in_specs=[vmem, vmem, pl.BlockSpec(memory_space=pltpu.SMEM)],
        out_specs=[vmem] * 5,
        out_shape=[jax.ShapeDtypeStruct(s, bf16) for s in shapes]
        + [jax.ShapeDtypeStruct((3, lay.heads // HALVES), f32)],
        compiler_params=pltpu.CompilerParams(vmem_limit_bytes=24 * MIB),
        name="unpack",
    )(received, sums, flag)


def exchange(v):
    groups = v.shape[0]
    halves = [[half * groups + i for i in range(groups)] for half in range(HALVES)]
    return lax.all_to_all(v, "seq", split_axis=0, concat_axis=0, tiled=True, axis_index_groups=halves)


def from_partner(v):
    groups = lax.axis_size("seq") // HALVES
    return lax.ppermute(v, "seq", [(i, (i + groups) % (2 * groups)) for i in range(2 * groups)])


def near_sum(v):
    replicas, shards = lax.axis_size("dp"), lax.axis_size("seq")
    if replicas == 1:
        return v
    halves = lambda i: (i + shards // HALVES) % shards

    def across(bits):
        pairs = [(r * shards + i, (r ^ bits) * shards + halves(i)) for r in range(replicas) for i in range(shards)]
        return lax.ppermute(v, ("dp", "seq"), pairs)

    if replicas == 2:
        return v + across(1)
    return (v + across(1)) + (lax.ppermute(v, "dp", [(r, r ^ 2) for r in range(replicas)]) + across(3))


def line_sum(v):
    half = lax.axis_size("dp") // 2
    if half <= 2:
        return v
    lines = [[2 * i + bit for i in range(odd, half, 2)] for odd in range(2) for bit in range(2)]
    return lax.psum(v, "dp", axis_index_groups=lines)


def shards(inputs, raw_step, write_keys, read_keys, grad_out, decay_log, skip_gain, step_bias):
    groups = lax.axis_size("seq") // HALVES
    some = decay_log.shape[0]
    lay = Layout(HALVES * some, groups)
    half = lax.axis_index("seq") // groups
    flag = half.astype(jnp.int32)[None]
    send = pack(inputs[0], grad_out[0], write_keys[0], read_keys[0], raw_step[0].T, groups)
    send, *mine = lax.optimization_barrier((send, decay_log, skip_gain, step_bias))
    mine = jnp.stack(mine)
    other = from_partner(mine)
    first = half == 0
    params = jnp.concatenate([jnp.where(first, mine, other), jnp.where(first, other, mine)], axis=1)
    params = jnp.pad(params, ((0, 0), (0, LANES - lay.heads)))

    received = exchange(send)
    own = scan_states(received, params, flag, lay)
    came = from_partner(own[-1])
    local = scan_local(received, own, lay)
    finish = scan_finish(received, own, local[3], local[4], came, flag, lay)
    back = message(own, local, finish, flag, lay)
    per_head = finish[1] + from_partner(finish[1])
    back, per_head = lax.optimization_barrier((back, per_head))
    sums = line_sum(near_sum(per_head))
    grad_x, grad_step, grad_write, grad_read, totals = unpack(exchange(back), sums, flag, lax.axis_size("dp"), lay)
    return grad_x[None], grad_step.T[None], grad_write[None], grad_read[None], totals


def solution(mesh):
    rows = P("dp", "seq", None)
    heads = P("seq")
    return jax.shard_map(
        shards,
        mesh=mesh,
        in_specs=(rows,) * 5 + (heads,) * 3,
        out_specs=(rows,) * 4 + (P(None, "seq"),),
        check_vma=False,
    )
```

```python
import jax
import jax.numpy as jnp
from jax import lax
from jax.experimental import pallas as pl
from jax.experimental.pallas import tpu as pltpu
from jax.sharding import PartitionSpec as P

CHUNK = 128
LANES = 128
HDIM = 64
NSTATE = 128
ROWS = 8
MIB = 1 << 20
PACK_STEPS = 2
HALVES = 2
PER_TILE = LANES // (2 * ROWS)
UNROLL = 8
STATES_VMEM = 24
LOCAL_VMEM = 24
FINISH_VMEM = 24

f32 = jnp.float32
bf16 = jnp.bfloat16


def mm(a, b):
    return jnp.dot(a, b, preferred_element_type=f32)


def mm_nt(a, b):
    return lax.dot_general(a, b, (((1,), (1,)), ((), ())), preferred_element_type=f32)


def mm_tn(a, b):
    return lax.dot_general(a, b, (((0,), (0,)), ((), ())), preferred_element_type=f32)


def split2(v):
    high = v.astype(bf16)
    return high, (v - high.astype(f32)).astype(bf16)


def split3(v):
    high = v.astype(bf16).astype(f32)
    rest = v - high
    mid = rest.astype(bf16).astype(f32)
    return high, mid, rest - mid


def iota(shape, axis):
    return lax.broadcasted_iota(jnp.int32, shape, axis)


def one_hot(cond):
    return jnp.where(cond, 1.0, 0.0)


def mm_exact(v, ones):
    parts = mm(jnp.concatenate(split3(v), axis=0).astype(bf16), ones.astype(bf16))
    n = v.shape[0]
    return parts[:n] + parts[n : 2 * n] + parts[2 * n :]


def pack_kernel(groups, xa_ref, xb_ref, ga_ref, gb_ref, b_ref, c_ref, s_ref, out_ref):
    some = s_ref.shape[0] // (HALVES * groups)
    narrow = some * HDIM
    width = HALVES * narrow
    tall = 2 * width + 2 * CHUNK
    for n in range(out_ref.shape[0]):
        row = 0
        for ref in (xa_ref, xb_ref, ga_ref, gb_ref):
            for i in range(narrow // LANES):
                start = n * narrow + i * LANES
                out_ref[n, row : row + CHUNK] = ref[:, start : start + LANES]
                row += CHUNK
        out_ref[n, 2 * width : 2 * width + CHUNK] = b_ref[...]
        out_ref[n, 2 * width + CHUNK : tall] = c_ref[...]
        group = pl.program_id(0) * out_ref.shape[0] + n
        out_ref[n, tall:] = mm(head_pick(16, s_ref.shape[0], group, some, groups), s_ref[...]).astype(bf16)


def head_pick(rows, heads, group, some, groups):
    shape = (rows, heads)
    row, head = iota(shape, 0), iota(shape, 1)
    owner = group + groups * (row // some)
    return one_hot((head == owner * some + row % some) & (row < HALVES * some)).astype(bf16)


def pack(x, g, b, c, s, groups):
    narrow = s.shape[0] // (HALVES * groups) * HDIM
    rows = 2 * HALVES * narrow + 2 * CHUNK + 16
    part = groups // PACK_STEPS
    whole = lambda a: pl.BlockSpec(a.shape, lambda j: (0, 0))
    first = pl.BlockSpec((CHUNK, part * narrow), lambda j: (0, j))
    second = pl.BlockSpec((CHUNK, part * narrow), lambda j: (0, PACK_STEPS + j))
    return pl.pallas_call(
        lambda *refs: pack_kernel(groups, *refs),
        grid=(PACK_STEPS,),
        in_specs=[first, second, first, second, whole(b), whole(c), whole(s)],
        out_specs=pl.BlockSpec((part, rows, LANES), lambda j: (j, 0, 0)),
        out_shape=jax.ShapeDtypeStruct((groups, rows, LANES), bf16),
        compiler_params=pltpu.CompilerParams(vmem_limit_bytes=56 * MIB),
        name="pack",
    )(x, x, g, g, b, c, s)


class Layout:
    def __init__(self, heads, chunks):
        self.heads, self.chunks, self.width = heads, chunks, heads * HDIM
        self.blocks = self.width // LANES
        self.at_b = 2 * self.width
        self.at_c = self.at_b + CHUNK
        self.at_s = self.at_c + CHUNK
        self.body = self.width + 4 * CHUNK
        self.flat = (chunks * ROWS, LANES)
        self.cube = (chunks, ROWS, LANES)
        self.wide = (chunks, CHUNK, self.width)

    def spread(self):
        shape = (ROWS, self.width)
        return one_hot(iota(shape, 1) // HDIM == iota(shape, 0))

    def to_lanes(self, tile):
        return jnp.sum(jnp.concatenate([tile] * self.blocks, axis=1) * self.spread(), axis=0, keepdims=True)

    def columns(self, ref, k, start):
        return jnp.concatenate(
            [ref[k, start + i * CHUNK : start + (i + 1) * CHUNK] for i in range(self.blocks)], axis=1
        )

    def keys(self, ref, k):
        return ref[k, self.at_b : self.at_b + CHUNK], ref[k, self.at_c : self.at_c + CHUNK]

    def by_head(self):
        shape = (16, self.width)
        return one_hot(iota(shape, 1) // HDIM == iota(shape, 0)).astype(bf16)


SQUARE = (LANES, LANES)
TILE = (ROWS, LANES)


def along(*parts):
    return jnp.concatenate(parts, axis=1)


def under(*parts):
    return jnp.concatenate(parts, axis=0)


def grouped(chunks, step, carry, reverse=False):
    def turn(i, carry):
        for n in range(UNROLL):
            k = i * UNROLL + n
            carry = step(chunks - 1 - k if reverse else k, carry)
        return carry

    return lax.fori_loop(0, chunks // UNROLL, turn, carry)


def states_kernel(lay, in_ref, given_ref, flag_ref,
                  gh_ref, gl_ref, xh_ref, xl_ref, hs_ref, dl_ref, wide_ref,
                  step_ref, slope_ref, decay_ref, total_ref, par_ref, skip_ref, send_ref,
                  alpha_ref, gamma_ref, pick_ref):
    chunks, width = lay.chunks, lay.width

    for i in range(3):
        row = jnp.broadcast_to(given_ref[i : i + 1], TILE)
        mine = jnp.where(iota(TILE, 1) == iota(TILE, 0), row, 0.0)
        par_ref[i] = jnp.broadcast_to(jnp.sum(mine, axis=1, keepdims=True), TILE)

    raw = in_ref[:, lay.at_s : lay.at_s + 16].astype(f32)[:, :ROWS]
    z = raw + par_ref[2][None]
    step = jnp.maximum(z, 0.0) + jnp.log1p(jnp.exp(-jnp.abs(z)))
    decay = -jnp.exp(par_ref[0])[None] * step
    step_ref[...], slope_ref[...], decay_ref[...] = step, jnp.exp(z - step), decay
    upto = one_hot(iota(SQUARE, 0) <= iota(SQUARE, 1))
    level = mm_exact(decay.reshape(lay.flat), upto)
    total_ref[...] = jnp.exp(jnp.broadcast_to(level[:, LANES - 1 :], lay.flat)).reshape(lay.cube)
    for ref, v in ((alpha_ref, jnp.exp(level)), (gamma_ref, jnp.exp(-level) * step.reshape(lay.flat))):
        high = v.astype(bf16).astype(f32)
        parts = jnp.concatenate([high.reshape(lay.cube), (v - high).reshape(lay.cube)], axis=1)
        parts = parts.reshape(chunks // PER_TILE, LANES, LANES)
        for i in range(chunks // PER_TILE):
            ref[i] = parts[i].T.astype(bf16)

    in_tile = (LANES, width)
    at_head = iota(in_tile, 1) // HDIM == iota(in_tile, 0) % ROWS
    eye = one_hot(iota(SQUARE, 0) == iota(SQUARE, 1)).astype(bf16)
    for i in range(PER_TILE):
        pick_ref[i] = one_hot(at_head & (iota(in_tile, 0) // (2 * ROWS) == i)).astype(bf16)

    def expand(ref, k):
        return mm(ref[k // PER_TILE], pick_ref[k % PER_TILE])

    def flip(v):
        return mm_nt(eye, v).astype(bf16)

    skip_ref[...] = jnp.zeros_like(skip_ref)

    def forward(k, carry):
        state, early, prefix = carry
        x = lay.columns(in_ref, k, 0).astype(f32)
        g = lay.columns(in_ref, k, width).astype(f32)
        gt_high, gt_low = split2(expand(alpha_ref, k) * g)
        wide = expand(gamma_ref, k)
        xt_high, xt_low = split2(wide * x)
        wide_ref[k] = wide
        gh_ref[k], gl_ref[k], xh_ref[k], xl_ref[k] = gt_high, gt_low, xt_high, xt_low
        skip_ref[...] += jnp.sum((x * g).reshape(CHUNK // ROWS, ROWS, width), axis=0)
        hs_ref[k] = state
        keys_in, keys_out = lay.keys(in_ref, k)
        keys_in, keys_out = flip(keys_in), flip(keys_out)
        back = mm(along(keys_out, keys_out), under(gt_high, gt_low))
        dl_ref[k] = back
        total = lay.to_lanes(total_ref[k])
        state = total * (state + mm(along(keys_in, keys_in), under(xt_high, xt_low)))
        return state, early + prefix * back, prefix * total

    nothing = jnp.zeros((NSTATE, width), f32)
    state, early, _ = grouped(chunks, forward, (nothing, nothing, jnp.ones((1, width), f32)))
    send_ref[...] = jnp.where(flag_ref[0] == 0, state, early)


def scan_states(received, params, flag, lay):
    vmem = pl.BlockSpec(memory_space=pltpu.VMEM)
    shape = jax.ShapeDtypeStruct
    wide, cube = lay.wide, lay.cube
    tiles = pltpu.VMEM((lay.chunks // PER_TILE, LANES, LANES), bf16)
    return pl.pallas_call(
        lambda *refs: states_kernel(lay, *refs),
        in_specs=[vmem, vmem, pl.BlockSpec(memory_space=pltpu.SMEM)],
        out_specs=[vmem] * 14,
        out_shape=[shape(wide, bf16)] * 4 + [shape(wide, f32)] * 3 + [shape(cube, f32)] * 4
        + [shape((3, ROWS, LANES), f32), shape((ROWS, lay.width), f32), shape((NSTATE, lay.width), f32)],
        scratch_shapes=[tiles, tiles, pltpu.VMEM((PER_TILE, LANES, lay.width), bf16)],
        compiler_params=pltpu.CompilerParams(vmem_limit_bytes=STATES_VMEM * MIB),
        name="scan_states",
    )(received, params, flag)


def local_kernel(lay, in_ref, gh_ref, gl_ref, xh_ref, xl_ref, hs_ref, dl_ref, wide_ref, total_ref, par_ref,
                 gx_ref, din_ref, dout_ref, r_ref, c_ref):
    width = lay.width
    gather = lay.by_head()
    skip_wide = lay.to_lanes(par_ref[1])
    causal = iota(SQUARE, 0) >= iota(SQUARE, 1)

    def backward(k, dstate):
        through = lay.to_lanes(total_ref[k]) * dstate
        dh, dl = split2(through)
        hh, hl = split2(hs_ref[k])
        gh, gl, xh, xl = gh_ref[k], gl_ref[k], xh_ref[k], xl_ref[k]
        keys_in, keys_out = lay.keys(in_ref, k)

        sh, sl = split2(jnp.where(causal, mm_nt(keys_out, keys_in), 0.0))
        th, tl = split2(jnp.where(causal.T, mm_nt(keys_in, keys_out), 0.0))
        out_h, in_h = along(sh, keys_out), along(th, keys_in)
        y = mm(out_h, under(xh, hh)) + mm(out_h, under(xl, hl)) + mm(sl, xh)
        dx = mm(in_h, under(gh, dh)) + mm(in_h, under(gl, dl)) + mm(tl, gh)

        ds = mm_nt(gh, xh) + mm_nt(gh, xl) + mm_nt(gl, xh)
        ds = jnp.where(causal, ds, 0.0)
        ph, plow = split2(ds)
        qh, qlow = split2(ds.T)
        dout_ref[k] = mm(along(ph, plow), under(keys_in, keys_in)) + mm_nt(gh, hh) + mm_nt(gh, hl) + mm_nt(gl, hh)
        din_ref[k] = mm(along(qh, qlow), under(keys_out, keys_out)) + mm_nt(xh, dh) + mm_nt(xh, dl) + mm_nt(xl, dh)

        gt = gh.astype(f32) + gl.astype(f32)
        xt = xh.astype(f32) + xl.astype(f32)
        high, low = split2(under(gt * y, xt * dx))
        sums = mm_nt(gather, high) + mm_nt(gather, low)
        r_ref[k], c_ref[k] = sums[:ROWS, :CHUNK], sums[:ROWS, CHUNK:]
        gx_ref[k] = wide_ref[k] * dx + skip_wide * lay.columns(in_ref, k, width).astype(f32)
        return dl_ref[k] + through

    grouped(lay.chunks, backward, jnp.zeros((NSTATE, width), f32), reverse=True)


def scan_local(received, own, lay):
    gh, gl, xh, xl, hs, dl, wide, _, _, _, total, par, _, _ = own
    vmem = pl.BlockSpec(memory_space=pltpu.VMEM)
    shape = jax.ShapeDtypeStruct
    keys = (lay.chunks, CHUNK, NSTATE)
    return pl.pallas_call(
        lambda *refs: local_kernel(lay, *refs),
        in_specs=[vmem] * 10,
        out_specs=[vmem] * 5,
        out_shape=[shape(lay.wide, f32), shape(keys, f32), shape(keys, f32), shape(lay.cube, f32), shape(lay.cube, f32)],
        compiler_params=pltpu.CompilerParams(vmem_limit_bytes=LOCAL_VMEM * MIB),
        name="scan_local",
    )(received, gh, gl, xh, xl, hs, dl, wide, total, par)


def finish_kernel(lay, in_ref, gh_ref, gl_ref, xh_ref, xl_ref,
                  step_ref, slope_ref, decay_ref, total_ref, par_ref, skip_ref, sent_ref, came_ref,
                  r_ref, c_ref, flag_ref, dstep_ref, pout_ref, uh_ref, ul_ref, more_ref,
                  reach_ref, col_ref, row_ref):
    chunks, width, cube = lay.chunks, lay.width, lay.cube
    gather = lay.by_head()
    first = flag_ref[0] == 0

    run = jnp.ones(TILE, f32)
    before = []
    for k in range(chunks):
        before.append(run)
        run = run * total_ref[k]
    run = jnp.ones(TILE, f32)
    for k in reversed(range(chunks)):
        run = run * total_ref[k]
        reach_ref[k] = jnp.where(first, run, before[k])

    def correct(keys_at, high_ref, low_ref, old_ref, new_ref):
        def one(k, carry):
            uh, ul = split2(lay.to_lanes(reach_ref[k]) * came_ref[...])
            uh_ref[k], ul_ref[k] = uh, ul
            keys = in_ref[k, keys_at : keys_at + CHUNK]
            more = mm(along(keys, keys), under(uh, ul))
            more_ref[k] = more
            ph, plow = split2((high_ref[k].astype(f32) + low_ref[k].astype(f32)) * more)
            new_ref[k] = old_ref[k] + (mm_nt(gather, ph) + mm_nt(gather, plow))[:ROWS]
            return carry

        grouped(chunks, one, 0)

    @pl.when(first)
    def _():
        row_ref[...] = r_ref[...]
        correct(lay.at_b, xh_ref, xl_ref, c_ref, col_ref)

    @pl.when(jnp.logical_not(first))
    def _():
        col_ref[...] = c_ref[...]
        correct(lay.at_c, gh_ref, gl_ref, r_ref, row_ref)

    spread = lay.spread()
    per_head = lambda row: jnp.sum(spread * row, axis=1, keepdims=True)
    cross = per_head(jnp.sum(sent_ref[...] * came_ref[...], axis=0, keepdims=True))
    later = jnp.broadcast_to(jnp.where(first, cross, 0.0), TILE)
    col = col_ref[...]
    since = one_hot(iota(SQUARE, 0) >= iota(SQUARE, 1))
    suffix = mm_exact((row_ref[...] - col).reshape(lay.flat), since).reshape(cube)
    sums = jnp.broadcast_to(suffix[:, :, :1], cube)
    carried = [None] * chunks
    for k in reversed(range(chunks)):
        carried[k] = later[None]
        later = later + sums[k]
    d_decay = suffix + jnp.concatenate(carried, axis=0)
    rate = -jnp.exp(par_ref[0])
    d_raw = slope_ref[...] * (col / step_ref[...] + rate[None] * d_decay)
    dstep_ref[...] = jnp.concatenate([d_raw, jnp.zeros(cube, f32)], axis=1).astype(bf16)

    result = jnp.zeros(TILE, f32)
    per = (
        jnp.sum(jnp.sum(d_decay * decay_ref[...], axis=0), axis=1, keepdims=True),
        per_head(jnp.sum(skip_ref[...], axis=0, keepdims=True)),
        jnp.sum(jnp.sum(d_raw, axis=0), axis=1, keepdims=True),
    )
    for i, v in enumerate(per):
        row = jnp.sum(jnp.where(iota(TILE, 0) == iota(TILE, 1), jnp.broadcast_to(v, TILE), 0.0), axis=0, keepdims=True)
        result = jnp.where(iota(TILE, 0) == i, jnp.broadcast_to(row, TILE), result)
    pout_ref[...] = result


def scan_finish(received, own, r, c, came, flag, lay):
    gh, gl, xh, xl, _, _, _, step, slope, decay, total, par, skip, sent = own
    vmem = pl.BlockSpec(memory_space=pltpu.VMEM)
    shape = jax.ShapeDtypeStruct
    small = pltpu.VMEM(lay.cube, f32)
    return pl.pallas_call(
        lambda *refs: finish_kernel(lay, *refs),
        in_specs=[vmem] * 15 + [pl.BlockSpec(memory_space=pltpu.SMEM)],
        out_specs=[vmem] * 5,
        out_shape=[shape((lay.chunks, 16, LANES), bf16), shape(TILE, f32), shape(lay.wide, bf16), shape(lay.wide, bf16),
                   shape(lay.wide, f32)],
        scratch_shapes=[small, small, small],
        compiler_params=pltpu.CompilerParams(vmem_limit_bytes=FINISH_VMEM * MIB),
        name="scan_finish",
    )(received, gh, gl, xh, xl, step, slope, decay, total, par, skip, sent, came, r, c, flag)


def message_kernel(lay, gh_ref, gl_ref, xh_ref, xl_ref, wide_ref, gx_ref, din_ref, dout_ref,
                   dstep_ref, uh_ref, ul_ref, more_ref, flag_ref, out_hbm, out_ref, sem):
    width = lay.width
    first = flag_ref[0] == 0
    put = lambda k: pltpu.make_async_copy(out_ref.at[k], out_hbm.at[k], sem.at[k])

    def d_keys(k, high_ref, low_ref):
        high, low = high_ref[k], low_ref[k]
        return mm_nt(high, uh_ref[k]) + mm_nt(high, ul_ref[k]) + mm_nt(low, uh_ref[k])

    def store(k, grad_x, d_in, d_out):
        grad_x = grad_x.astype(bf16)
        for j in range(lay.blocks):
            out_ref[k, j * CHUNK : (j + 1) * CHUNK] = grad_x[:, j * LANES : (j + 1) * LANES]
        for j, part in enumerate(split2(d_in) + split2(d_out)):
            out_ref[k, width + j * CHUNK : width + (j + 1) * CHUNK] = part
        out_ref[k, lay.body :] = dstep_ref[k]
        put(k).start()

    @pl.when(first)
    def _():
        def one(k, carry):
            store(k, gx_ref[k] + wide_ref[k] * more_ref[k], din_ref[k] + d_keys(k, xh_ref, xl_ref), dout_ref[k])
            return carry

        grouped(lay.chunks, one, 0)

    @pl.when(jnp.logical_not(first))
    def _():
        def one(k, carry):
            store(k, gx_ref[k], din_ref[k], dout_ref[k] + d_keys(k, gh_ref, gl_ref))
            return carry

        grouped(lay.chunks, one, 0)

    for k in range(lay.chunks):
        put(k).wait()


def message(own, local, finish, flag, lay):
    gh, gl, xh, xl, _, _, wide, *_ = own
    dstep, _, uh, ul, more = finish
    vmem = pl.BlockSpec(memory_space=pltpu.VMEM)
    return pl.pallas_call(
        lambda *refs: message_kernel(lay, *refs),
        in_specs=[vmem] * 12 + [pl.BlockSpec(memory_space=pltpu.SMEM)],
        out_specs=pl.BlockSpec(memory_space=pl.ANY),
        out_shape=jax.ShapeDtypeStruct((lay.chunks, lay.body + 16, LANES), bf16),
        scratch_shapes=[
            pltpu.VMEM((lay.chunks, lay.body + 16, LANES), bf16),
            pltpu.SemaphoreType.DMA((lay.chunks,)),
        ],
        compiler_params=pltpu.CompilerParams(vmem_limit_bytes=FINISH_VMEM * MIB),
        cost_estimate=pl.CostEstimate(flops=400_000_000, bytes_accessed=20_000_000, transcendentals=0),
        name="message",
    )(gh, gl, xh, xl, wide, *local[:3], dstep, uh, ul, more, flag)


def unpack_kernel(lay, replicas, in_ref, sums_ref, flag_ref, x_ref, s_ref, b_ref, c_ref, p_ref):
    groups, width = in_ref.shape[0], lay.width
    narrow = width // HALVES
    some = lay.heads // HALVES
    for n in range(groups):
        for half in range(HALVES):
            for i in range(narrow // LANES):
                start = (half * groups + n) * narrow + i * LANES
                row = half * narrow + i * CHUNK
                x_ref[:, start : start + LANES] = in_ref[n, row : row + CHUNK]
    part = lambda n, j: in_ref[n, width + j * CHUNK : width + (j + 1) * CHUNK].astype(f32)
    every = range(groups)
    b_ref[...] = sum(part(n, 0) + part(n, 1) for n in every).astype(bf16)
    c_ref[...] = sum(part(n, 2) + part(n, 3) for n in every).astype(bf16)
    picks = [head_pick(16, s_ref.shape[0], n, some, groups) for n in every]
    s_ref[...] = sum(mm_tn(picks[n], in_ref[n, lay.body :]) for n in every).astype(bf16)
    mean = sums_ref[:3] / replicas
    p_ref[...] = jnp.where(flag_ref[0] == 0, mean[:, :some], mean[:, some : 2 * some])


def unpack(received, sums, flag, replicas, lay):
    groups = received.shape[0]
    shapes = [(CHUNK, groups * lay.width), (groups * lay.heads, CHUNK), (CHUNK, NSTATE), (CHUNK, NSTATE)]
    vmem = pl.BlockSpec(memory_space=pltpu.VMEM)
    return pl.pallas_call(
        lambda *refs: unpack_kernel(lay, replicas, *refs),
        in_specs=[vmem, vmem, pl.BlockSpec(memory_space=pltpu.SMEM)],
        out_specs=[vmem] * 5,
        out_shape=[jax.ShapeDtypeStruct(s, bf16) for s in shapes]
        + [jax.ShapeDtypeStruct((3, lay.heads // HALVES), f32)],
        compiler_params=pltpu.CompilerParams(vmem_limit_bytes=24 * MIB),
        name="unpack",
    )(received, sums, flag)


def exchange(v):
    groups = v.shape[0]
    halves = [[half * groups + i for i in range(groups)] for half in range(HALVES)]
    return lax.all_to_all(v, "seq", split_axis=0, concat_axis=0, tiled=True, axis_index_groups=halves)


def from_partner(v):
    groups = lax.axis_size("seq") // HALVES
    return lax.ppermute(v, "seq", [(i, (i + groups) % (2 * groups)) for i in range(2 * groups)])


def across_sum(v):
    replicas, shards = lax.axis_size("dp"), lax.axis_size("seq")
    if replicas == 1:
        return v
    halves = lambda i: (i + shards // HALVES) % shards
    across = [(r * shards + i, (r ^ 1) * shards + halves(i)) for r in range(replicas) for i in range(shards)]
    return v + lax.ppermute(v, ("dp", "seq"), across)


def line_sum(v):
    half = lax.axis_size("dp") // 2
    if half <= 1:
        return v
    v = v + lax.ppermute(v, "dp", [(i, i ^ 2) for i in range(2 * half)])
    if half == 2:
        return v
    lines = [[2 * i + bit for i in range(odd, half, 2)] for odd in range(2) for bit in range(2)]
    return lax.psum(v, "dp", axis_index_groups=lines)


def shards(inputs, raw_step, write_keys, read_keys, grad_out, decay_log, skip_gain, step_bias):
    groups = lax.axis_size("seq") // HALVES
    some = decay_log.shape[0]
    lay = Layout(HALVES * some, groups)
    half = lax.axis_index("seq") // groups
    flag = half.astype(jnp.int32)[None]
    send = pack(inputs[0], grad_out[0], write_keys[0], read_keys[0], raw_step[0].T, groups)
    send, *mine = lax.optimization_barrier((send, decay_log, skip_gain, step_bias))
    mine = jnp.stack(mine)
    other = from_partner(mine)
    first = half == 0
    params = jnp.concatenate([jnp.where(first, mine, other), jnp.where(first, other, mine)], axis=1)
    params = jnp.pad(params, ((0, 0), (0, LANES - lay.heads)))

    received = exchange(send)
    own = scan_states(received, params, flag, lay)
    came = from_partner(own[-1])
    local = scan_local(received, own, lay)
    finish = scan_finish(received, own, local[3], local[4], came, flag, lay)
    back = message(own, local, finish, flag, lay)
    per_head = finish[1] + from_partner(finish[1])
    back, per_head = lax.optimization_barrier((back, per_head))
    back, per_head = lax.optimization_barrier((back, across_sum(per_head)))
    sums = line_sum(per_head)
    grad_x, grad_step, grad_write, grad_read, totals = unpack(exchange(back), sums, flag, lax.axis_size("dp"), lay)
    return grad_x[None], grad_step.T[None], grad_write[None], grad_read[None], totals


def solution(mesh):
    rows = P("dp", "seq", None)
    heads = P("seq")
    return jax.shard_map(
        shards,
        mesh=mesh,
        in_specs=(rows,) * 5 + (heads,) * 3,
        out_specs=(rows,) * 4 + (P(None, "seq"),),
        check_vma=False,
    )
```
